32 devices in a mesh: dp: 4 (over x, core), seq: 8 (over z, y).
Axes of the slice: x: 2, y: 2, z: 4, core: 2. Of those that a mesh axis runs over, the one named last changes fastest.
Arguments:
- layer_input: bfloat16 [4, 1024, 4096], P('dp', 'seq'), may hold values from -6 to 6
- proj_weight: bfloat16 [4096, 256], replicated, may hold values from -0.0078125 to 0.0078125
- inputs: bfloat16 [4, 1024, 2048], P('dp', 'seq'), may hold values from -6 to 6
- step_size: float32 [4, 32, 1024], P('dp', None, 'seq'), may hold values from 0.02 to 0.2
- log_decay: float32 [4, 32, 1024], P('dp', None, 'seq'), may hold values from -0.8 to 0, as said below
- skip_gain: float32 [32], replicated, may hold values from 0.1 to 1.9
- grad_out: bfloat16 [4, 1024, 2048], P('dp', 'seq'), may hold values from -6 to 6
Outputs:
- grad_inputs: bfloat16 [4, 1024, 2048], P('dp', 'seq')
- grad_weight: float32 [4096, 256], P(('dp', 'seq'))
The draws below stay inside these ranges and needn't reach their ends.
Inputs may be any that keep to these rules, and one draw needn't show every extreme that they name: `log_decay`: every entry is negative.
All inputs are finite; a program needn't handle non-finite values.
Results may differ from the reference program's by a relative error of at most 0.0069.
Values sent between devices are 32-bit elements; how exact they have to be, the bound alone decides.
No kernel may reach another device: no remote copies, remote signals or barrier semaphores. Data moves between devices by JAX's collectives and lax.ppermute only.
A program may use at most 192 MiB of HBM per device.

```python
import math
import jax
import jax.numpy as jnp
from jax import lax

D = 4096
SHARD_CHANNELS = 32
HEAD_DIM = 64
STATE = 128
SPAN = 128
L_DEV = 128
SAMPLE_COUNT = 4
TIME_EXTENT = 1024
INNER = 2048


def draw_log_decay(key, part):
    stochastic_seed_splits = jax.random.split(key, 7)
    fast_share = 0.5
    slow_low = 1.0 / 16.0
    slow_high = 1.0 / 4.0
    head_picks = jax.random.uniform(stochastic_seed_splits[0], (1, SHARD_CHANNELS, 1))
    fast_rate = jnp.exp(jax.random.uniform(stochastic_seed_splits[1], (1, SHARD_CHANNELS, 1), minval=jnp.log(1.0 / 50.0), maxval=jnp.log(1.0 / 30.0)))
    slow_rate = jnp.exp(jax.random.uniform(stochastic_seed_splits[2], (1, SHARD_CHANNELS, 1), minval=jnp.log(slow_low), maxval=jnp.log(slow_high))) / L_DEV
    nominal_forgetting_speed = jnp.where(head_picks < fast_share, fast_rate, slow_rate)
    segment_factor = jnp.exp(jax.random.uniform(stochastic_seed_splits[3], (SAMPLE_COUNT, SHARD_CHANNELS, TIME_EXTENT // L_DEV), minval=jnp.log(0.5), maxval=jnp.log(2.0)))
    segment_factor = jnp.repeat(segment_factor, L_DEV, axis=2)
    forgetting_perturbation = jax.random.uniform(stochastic_seed_splits[4], (SAMPLE_COUNT, SHARD_CHANNELS, TIME_EXTENT), minval=0.5, maxval=1.5)
    episode_onset = jax.random.randint(stochastic_seed_splits[5], (2,), 0, TIME_EXTENT)
    element_displacements = jnp.arange(TIME_EXTENT)
    within_episode_flags = jnp.any(element_displacements[None, :] == episode_onset[:, None], axis=0)
    episode_duration = jnp.log(jax.random.uniform(stochastic_seed_splits[6], (SAMPLE_COUNT, SHARD_CHANNELS, 1), minval=0.5, maxval=0.8))
    payload_vectors = -nominal_forgetting_speed * segment_factor * forgetting_perturbation + jnp.where(within_episode_flags[None, None, :], episode_duration, 0.0)
    return payload_vectors.astype(jnp.float32)


def with_spikes(drawn, rng, source, target, blocks, factor):
    def block_of(dim):
        return (jnp.arange(drawn.shape[dim]) // (drawn.shape[dim] // blocks)).reshape((-1,) + (1,) * (drawn.ndim - 1 - dim))

    first = jax.random.permutation(rng, blocks)[block_of(target)]
    far = (block_of(target) + blocks // 2) % blocks
    return jnp.where((block_of(source) == first) | (block_of(source) == far), factor * drawn, drawn)


def block_levels(own_key, extent, cuts, least, high):
    loudness = 1.0
    for position, shards_of in cuts:
        heights = jax.random.uniform(jax.random.fold_in(jax.random.fold_in(own_key, 6), position), (shards_of,), jnp.float32, least / len(cuts), high / len(cuts))
        loudness = loudness * jnp.repeat(jnp.exp(heights), extent[position] // shards_of).reshape((-1,) + (1,) * (len(extent) - 1 - position))
    return loudness


def gaussian(key, extent, deviation, limit, cuts=(), held_as=jnp.bfloat16):
    drawn = deviation * jax.random.normal(key, extent, jnp.float32)
    if cuts:
        drawn = drawn * block_levels(key, extent, cuts, -0.22, 0.18)
    return jnp.clip(drawn, -limit, limit).astype(held_as)


def noise_with(rng, shape, spread, reach, shards, heavy, held_as=jnp.bfloat16):
    drawn = spread * jax.random.normal(rng, shape, jnp.float32)
    if shards:
        drawn = drawn * block_levels(rng, shape, shards, -0.22, 0.18)
    return jnp.clip(with_spikes(drawn, jax.random.fold_in(rng, 3), *heavy), -reach, reach).astype(held_as)


def setup_inputs(seed: int = 0) -> dict:
    key_of = jax.random.split(jax.random.key(seed), 8)
    return {
        "layer_input": noise_with(key_of[0], (SAMPLE_COUNT, TIME_EXTENT, D), 1.0, 6.0, ((0, 4), (1, 8)), (1, 2, 8, 2.0)),
        "proj_weight": gaussian(key_of[1], (D, 2 * STATE), (D * STATE) ** -0.5, 0.0078125),
        "inputs": gaussian(key_of[2], (SAMPLE_COUNT, TIME_EXTENT, INNER), 1.0, 6.0, ((0, 4), (1, 8))),
        "step_size": jnp.clip(jnp.exp(math.log(0.2) - 2.3025851 * jax.random.uniform(key_of[3], (SAMPLE_COUNT, SHARD_CHANNELS, TIME_EXTENT), jnp.float32) ** block_levels(key_of[3], (SAMPLE_COUNT, SHARD_CHANNELS, TIME_EXTENT), ((0, 4), (2, 8)), -0.2, 0.2)), 0.02, 0.2),
        "log_decay": draw_log_decay(jax.random.fold_in(key_of[7], 71), 0),
        "skip_gain": jnp.clip(1.0 + 0.18 * jax.random.normal(key_of[5], (SHARD_CHANNELS,), jnp.float32), 0.1, 1.9),
        "grad_out": gaussian(key_of[6], (SAMPLE_COUNT, TIME_EXTENT, INNER), 1.0, 6.0, ((0, 4), (1, 8))),
    }


def span_inputs(proj, inputs, grad_out, step_size, log_decay):
    length = inputs.shape[0]
    spans = length // SPAN
    b_cols = proj[:, :STATE].reshape(spans, SPAN, STATE)
    c_cols = proj[:, STATE:].reshape(spans, SPAN, STATE)
    inputs_c = inputs.reshape(spans, SPAN, SHARD_CHANNELS, HEAD_DIM)
    grad_rows = grad_out.reshape(spans, SPAN, SHARD_CHANNELS, HEAD_DIM)
    step_rows = step_size.reshape(SHARD_CHANNELS, spans, SPAN).transpose(1, 0, 2)
    decay_sum = jnp.cumsum(log_decay.reshape(SHARD_CHANNELS, spans, SPAN).transpose(1, 0, 2), axis=2)
    span_total = decay_sum[:, :, -1]
    to_end = jnp.exp(span_total[:, :, None] - decay_sum)
    weighted = (inputs_c.astype(jnp.float32) * jnp.transpose(step_rows * to_end, (0, 2, 1))[..., None]).astype(jnp.bfloat16)
    scaled = (grad_rows.astype(jnp.float32) * jnp.transpose(jnp.exp(decay_sum), (0, 2, 1))[..., None]).astype(jnp.bfloat16)
    own_state = jnp.einsum('cqhp,cqn->chpn', weighted.astype(jnp.float32), b_cols.astype(jnp.float32))
    own_grad = jnp.einsum('cqhp,cqn->chpn', scaled.astype(jnp.float32), c_cols.astype(jnp.float32))
    return b_cols, c_cols, inputs_c, grad_rows, step_rows, decay_sum, span_total, weighted, scaled, own_state, own_grad


def span_grads(b_cols, c_cols, inputs_c, grad_rows, step_rows, decay_sum, span_total, weighted, scaled, start, after, skip_gain):
    start_bf = start.astype(jnp.bfloat16)
    after_bf = after.astype(jnp.bfloat16)
    row_ids = lax.broadcasted_iota(jnp.int32, (SPAN, SPAN), 0)
    col_ids = lax.broadcasted_iota(jnp.int32, (SPAN, SPAN), 1)
    causal = row_ids >= col_ids
    log_gap = decay_sum[:, :, None] - decay_sum[:, None, :]
    decay_mat = jnp.exp(jnp.where(causal[None], log_gap, -jnp.inf))
    kernel = jnp.dot(c_cols, b_cols.T, preferred_element_type=jnp.float32)
    weights = (decay_mat * kernel[None]).astype(jnp.bfloat16)
    within = jnp.einsum('hsj,shp->jhp', weights.astype(jnp.float32), grad_rows.astype(jnp.float32))
    carried = jnp.einsum('hpn,jn->jhp', after_bf.astype(jnp.float32), b_cols.astype(jnp.float32))
    to_end = jnp.exp(span_total[:, None] - decay_sum)
    grad_x = step_rows.T[:, :, None] * (within + to_end.T[:, :, None] * carried) + skip_gain[None, :, None] * grad_rows.astype(jnp.float32)
    intersection = jnp.einsum('shp,jhp->hsj', grad_rows.astype(jnp.float32), inputs_c.astype(jnp.float32))
    mixing = jnp.sum(decay_mat * step_rows[:, None, :] * intersection, axis=0).astype(jnp.bfloat16)
    grad_c = jnp.dot(mixing, b_cols, preferred_element_type=jnp.float32) + jnp.dot(scaled.reshape(SPAN, -1), start_bf.reshape(-1, STATE), preferred_element_type=jnp.float32)
    grad_b = jnp.dot(mixing.T, c_cols, preferred_element_type=jnp.float32) + jnp.dot(weighted.reshape(SPAN, -1), after_bf.reshape(-1, STATE), preferred_element_type=jnp.float32)
    grad_proj = jnp.concatenate([grad_b, grad_c], axis=1).astype(jnp.bfloat16)
    return grad_x.astype(jnp.bfloat16).reshape(SPAN, -1), grad_proj


def one_sequence(layer_input, inputs, grad_out, step_size, log_decay, proj_weight, skip_gain):
    proj = jnp.dot(layer_input, proj_weight, preferred_element_type=jnp.float32).astype(jnp.bfloat16)
    pieces = span_inputs(proj, inputs, grad_out, step_size, log_decay)
    own_state, own_grad, span_total = pieces[9], pieces[10], pieces[6]
    empty_state = jnp.zeros((SHARD_CHANNELS, HEAD_DIM, STATE), jnp.float32)

    def advance(state_carry, piece):
        return jnp.exp(piece[1])[:, None, None] * state_carry + piece[0], state_carry

    _, starts = lax.scan(advance, empty_state, (own_state, span_total))
    _, afters = lax.scan(advance, empty_state, (own_grad, span_total), reverse=True)

    def finish(parts):
        return span_grads(*parts, skip_gain)

    grad_x, grad_proj = lax.map(finish, pieces[:9] + (starts, afters))
    grad_proj = grad_proj.reshape(-1, 2 * STATE)
    contrib = jnp.dot(layer_input.T, grad_proj, preferred_element_type=jnp.float32)
    return grad_x.reshape(-1, INNER), contrib


def reference(layer_input, proj_weight, inputs, step_size, log_decay, skip_gain, grad_out):
    def per_sequence(parts):
        return one_sequence(parts[0], parts[1], parts[2], parts[3], parts[4], proj_weight, skip_gain)

    grad_inputs, contribs = lax.map(per_sequence, (layer_input, inputs, grad_out, step_size, log_decay))
    grad_weight = jnp.sum(contribs, axis=0) / TIME_EXTENT
    return grad_inputs, grad_weight
```

```python
import functools

import jax
import jax.numpy as jnp
from jax import lax
from jax.experimental import pallas as pl
from jax.experimental.pallas import tpu as pltpu
from jax.sharding import PartitionSpec as P

HEADS = 32
HEAD_DIM = 64
STATE = 128
SPAN = 128
CHUNKS = 2
F32 = jnp.float32
BF16 = jnp.bfloat16
VMEM_LIMIT = 40 * 1024 * 1024


def group_size(n_seq):
    q = 1
    while n_seq % (2 * q) == 0 and 4 * q * q <= n_seq:
        q *= 2
    return q


def nn(a, b):
    return lax.dot_general(a, b, (((1,), (0,)), ((), ())), preferred_element_type=F32)


def nt(a, b):
    return lax.dot_general(a, b, (((1,), (1,)), ((), ())), preferred_element_type=F32)


def tn(a, b):
    return lax.dot_general(a, b, (((0,), (0,)), ((), ())), preferred_element_type=F32)


def exact(a, b, dims):
    return lax.dot_general(
        a, b, (dims, ((), ())), preferred_element_type=F32, precision=lax.Precision.HIGHEST
    )


def call(body, outs, n_in, scratch=(), name=None, cost=None):
    specs = [pl.BlockSpec(memory_space=pltpu.SMEM)]
    specs += [pl.BlockSpec(memory_space=pltpu.VMEM)] * n_in
    return pl.pallas_call(
        body,
        out_shape=outs,
        in_specs=specs,
        out_specs=jax.tree.map(lambda _: pl.BlockSpec(memory_space=pltpu.VMEM), outs),
        scratch_shapes=scratch,
        compiler_params=pltpu.CompilerParams(vmem_limit_bytes=VMEM_LIMIT),
        cost_estimate=cost,
        name=name,
    )


def out(shape, dtype=F32):
    return jax.ShapeDtypeStruct(shape, dtype)


def iotas():
    rows = lax.broadcasted_iota(jnp.int32, (SPAN, SPAN), 0)
    cols = lax.broadcasted_iota(jnp.int32, (SPAN, SPAN), 1)
    return rows, cols


def columns(ref, start, width):
    return ref[:, pl.ds(pl.multiple_of(start, 128), width)]


def states_body(q, hc, chunk, *refs):
    n = q - 1
    it = iter(refs)
    ids, x_ref, g_ref = next(it), next(it), next(it)
    xg_in = [next(it) for _ in range(n)]
    bc_own = next(it)
    bc_in = [next(it) for _ in range(n)]
    ls_own = next(it)
    ls_in = [next(it) for _ in range(n)]
    xs, gs, ws, ss, f1s, ds, own_s, own_g, total_s, total_g, plane, bcs, cums, avs = it
    width = hc * HEAD_DIM
    y = ids[0]
    first = (y * CHUNKS + chunk) * width
    xs[y] = columns(x_ref, first, width)
    gs[y] = columns(g_ref, first, width)
    bcs[y] = bc_own[...].astype(BF16)
    cums[y] = ls_own[0]
    avs[y] = ls_own[1]
    for r in range(1, q):
        at = lax.rem(y - r + q, q)
        xs[at] = xg_in[r - 1][0].astype(BF16)
        gs[at] = xg_in[r - 1][1].astype(BF16)
        bcs[at] = bc_in[r - 1][...].astype(BF16)
        cums[at] = ls_in[r - 1][0]
        avs[at] = ls_in[r - 1][1]
    rows, cols = iotas()
    tri = (rows >= cols).astype(F32)
    eye = (rows == cols).astype(F32)
    head_of = lax.broadcasted_iota(jnp.int32, (hc, width), 1) // HEAD_DIM
    spread = (head_of == lax.broadcasted_iota(jnp.int32, (hc, width), 0)).astype(F32)
    last = ((1,), (1,))
    for b in range(q):
        decay = cums[b]
        cum_c = exact(tri, decay, last)
        a_c = cum_c - exact(eye, jnp.log(avs[b]), last)
        cums[b] = exact(decay, tri, last)
        cum_x = exact(cum_c, spread, ((1,), (0,)))
        a_x = exact(a_c, spread, ((1,), (0,)))
        avs[b] = exact(a_c, eye, ((0,), (0,)))
        total = cum_x[SPAN - 1 : SPAN, :]
        f1 = jnp.exp(total - a_x)
        f1s[b] = f1
        ds[b] = jnp.exp(total)
        weighted = (xs[b].astype(F32) * f1).astype(BF16)
        scaled = (gs[b].astype(F32) * jnp.exp(cum_x)).astype(BF16)
        ws[b] = weighted
        ss[b] = scaled
        own_s[b] = tn(bcs[b][:, :STATE], weighted)
        own_g[b] = tn(bcs[b][:, STATE:], scaled)
    forward, backward, through = own_s[0], own_g[q - 1], ds[0]
    for b in range(1, q):
        forward = ds[b] * forward + own_s[b]
        backward = ds[q - 1 - b] * backward + own_g[q - 1 - b]
        through = through * ds[b]
    total_s[...] = forward
    total_g[...] = backward
    plane[...] = through


def local_body(q, hc, ids, xs, gs, bcs, cums, avs, skip, gx, gp):
    rows, cols = iotas()
    causal = rows <= cols
    low = lax.broadcasted_iota(jnp.int32, (SPAN, 128), 1) < HEAD_DIM
    eye = (rows == cols).astype(F32)
    for b in range(q):
        b_cols, c_cols = bcs[b][:, :STATE], bcs[b][:, STATE:]
        kernel = nt(b_cols, c_cols)
        a_c = exact(eye, avs[b], ((1,), (1,)))
        mixing = jnp.zeros((SPAN, SPAN), F32)
        for pair in range(hc // 2):
            at = slice(pair * 128, pair * 128 + 128)
            x, g = xs[b][:, at], gs[b][:, at]
            parts = []
            for half in range(2):
                h = 2 * pair + half
                gap = cums[b][h : h + 1, :] - a_c[:, h : h + 1]
                decay = jnp.exp(jnp.where(causal, gap, -jnp.inf))
                picked = jnp.where(low if half == 0 else ~low, x, jnp.zeros_like(x))
                mixing += decay * nt(picked, g)
                parts.append(nn((decay * kernel).astype(BF16), g))
            gx[b, :, at] = jnp.where(low, parts[0], parts[1]) + skip[:, at] * g.astype(F32)
        mixed = mixing.astype(BF16)
        gp[b, :, :STATE] = nn(mixed, c_cols)
        gp[b, :, STATE:] = tn(mixed, b_cols)


def final_body(q, more, *refs):
    it = iter(refs)
    ids, start, after, own_s, own_g, ds, ws, ss, f1s, bcs, gx, gp = [next(it) for _ in range(12)]
    before = [next(it) for _ in range(q)] if more else None
    gx_out = [next(it) for _ in range(q)]
    gp_out = [next(it) for _ in range(q)]
    gx_all, gp_all = it
    y = ids[0]
    state = start[...]
    for b in range(q):
        gp_all[b, :, STATE:] = gp[b, :, STATE:] + nt(ss[b], state.astype(BF16))
        if b < q - 1:
            state = ds[b] * state + own_s[b]
    state = after[...]
    for b in range(q - 1, -1, -1):
        rounded = state.astype(BF16)
        gx_all[b] = gx[b] + f1s[b] * nn(bcs[b][:, :STATE], rounded)
        gp_all[b, :, :STATE] = gp[b, :, :STATE] + nt(ws[b], rounded)
        if b > 0:
            state = ds[b] * state + own_g[b]
    for r in range(q):
        at = lax.rem(y + r, q)
        gx_out[r][...] = gx_all[at]
        gp_out[r][...] = gp_all[at] if before is None else gp_all[at] + before[r][...]


def assemble_body(q, width, *refs):
    ids, result = refs[0], refs[-1]
    parts = refs[1:-1]
    y = ids[0]
    for r in range(q):
        group = lax.rem(y - r + q, q)
        for c in range(CHUNKS):
            at = pl.multiple_of((group * CHUNKS + c) * width, 128)
            result[:, pl.ds(at, width)] = parts[r * CHUNKS + c][...].astype(BF16)


def weight_body(n_dp, n_seq, rows, scale, *refs):
    it = iter(refs)
    ids, tokens = next(it), next(it)
    tokens_in = [next(it) for _ in range(n_dp - 1)]
    gp_own = next(it)
    gp_in = [next(it) for _ in range(n_dp - 1)]
    outs = [next(it) for _ in range(n_seq)]
    held, products = it
    width = n_seq * rows
    dp, seq = ids[2], ids[1]
    grads = [r[...].astype(BF16) for r in [gp_own] + gp_in]
    held[0] = columns(tokens, dp * width, width)
    for r in range(1, n_dp):
        held[r] = tokens_in[r - 1][...].astype(BF16)
    total = tn(held[0], grads[0])
    for r in range(1, n_dp):
        total += tn(held[r], grads[r])
    products[...] = (total * scale).reshape(n_seq, rows, 2 * STATE)
    for r in range(n_seq):
        outs[r][...] = products[lax.rem(seq + r, n_seq)]


def on_device(layer_input, proj_weight, inputs, step_size, log_decay, skip_gain, grad_out):
    n_seq, n_dp = lax.axis_size("seq"), lax.axis_size("dp")
    q = group_size(n_seq)
    planes = n_seq // q
    group_heads = HEADS // q
    hc = group_heads // CHUNKS
    width = hc * HEAD_DIM
    tokens, x, g = layer_input[0], inputs[0], grad_out[0]
    length, features = tokens.shape
    decay_step = jnp.stack([log_decay[0], step_size[0]])
    seq, dp = lax.axis_index("seq"), lax.axis_index("dp")
    y = lax.rem(seq, q)
    ids = jnp.stack([y, seq, dp]).astype(jnp.int32)

    def in_group(r):
        return [(z * q + i, z * q + (i + r) % q) for z in range(planes) for i in range(q)]

    def swap(value, r):
        return lax.ppermute(value, "seq", in_group(r))

    def heads_of(group, c):
        return lax.dynamic_slice_in_dim(decay_step, (group * CHUNKS + c) * hc, hc, axis=1)

    xg_in, ls_in = {}, {}
    for c in range(CHUNKS):
        for r in range(1, q):
            to = lax.rem(y + r, q)
            at = (to * CHUNKS + c) * width
            cut = [lax.dynamic_slice_in_dim(v, at, width, axis=1) for v in (x, g)]
            xg_in[c, r] = swap(jnp.stack(cut).astype(F32), r)
            ls_in[c, r] = swap(heads_of(to, c), r)
    proj = jnp.dot(tokens, proj_weight, preferred_element_type=F32)
    proj = lax.reduce_precision(proj, exponent_bits=8, mantissa_bits=7)
    bc_in = [swap(proj, r) for r in range(1, q)]
    columns_each = features // n_dp
    tokens_in = []
    for r in range(1, n_dp):
        to = lax.rem(dp + r, n_dp)
        piece = lax.dynamic_slice_in_dim(tokens, to * columns_each, columns_each, axis=1)
        pairs = [(i, (i + r) % n_dp) for i in range(n_dp)]
        tokens_in.append(lax.ppermute(piece.astype(F32), "dp", pairs))

    row_b, row_f = (q, SPAN, width), (q, SPAN, width)
    held = []
    for c in range(CHUNKS):
        outs = (
            out(row_b, BF16), out(row_b, BF16), out(row_b, BF16), out(row_b, BF16),
            out(row_f), out((q, 1, width)), out(row_f), out(row_f),
            out((STATE, width)), out((STATE, width)), out((1, width)),
            out((q, SPAN, 2 * STATE), BF16), out((q, hc, SPAN)), out((q, hc, SPAN)),
        )
        args = [x, g] + [xg_in[c, r] for r in range(1, q)] + [proj] + bc_in
        args += [heads_of(y, c)] + [ls_in[c, r] for r in range(1, q)]
        held.append(
            call(functools.partial(states_body, q, hc, c), outs, len(args), name="states")(ids, *args)
        )

    entries = []
    plane = seq // q
    for c in range(CHUNKS):
        total_s, total_g, through = held[c][8:11]
        sent, back = total_s, total_g
        start, after = jnp.zeros_like(total_s), jnp.zeros_like(total_g)
        for t in range(planes - 1):
            up = [(t * q + i, (t + 1) * q + i) for i in range(q)]
            top = planes - 1 - t
            down = [(top * q + i, (top - 1) * q + i) for i in range(q)]
            start += lax.ppermute(sent, "seq", up)
            after += lax.ppermute(back, "seq", down)
            if t < planes - 2:
                sent = total_s + through * start
                back = total_g + through * after
        entries.append((start, after))

    skip = jnp.repeat(skip_gain, HEAD_DIM)[None]
    before, gx_parts = [], {}
    for c in range(CHUNKS):
        xs, gs, ws, ss, f1s, ds, own_s, own_g, _, _, _, bcs, cums, avs = held[c]
        skip_c = lax.dynamic_slice_in_dim(skip, (y * CHUNKS + c) * width, width, axis=1)
        gx, gp = call(
            functools.partial(local_body, q, hc),
            (out(row_f), out((q, SPAN, 2 * STATE))), 6, name="local",
        )(ids, xs, gs, bcs, cums, avs, skip_c)
        start, after = entries[c]
        outs = (out((SPAN, width)),) * q + (out((SPAN, 2 * STATE)),) * q
        args = [start, after, own_s, own_g, ds, ws, ss, f1s, bcs, gx, gp] + before
        scratch = (pltpu.VMEM(row_f, F32), pltpu.VMEM((q, SPAN, 2 * STATE), F32))
        done = call(
            functools.partial(final_body, q, bool(before)), outs, len(args), scratch, name="final"
        )(ids, *args)
        for r in range(q):
            gx_parts[r, c] = done[r]
        before = list(done[q:])

    gp_own = before[0]
    for r in range(1, q):
        gp_own = gp_own + swap(before[r], r)
    gp_in = [
        lax.ppermute(gp_own, "dp", [(i, (i + r) % n_dp) for i in range(n_dp)]) for r in range(1, n_dp)
    ]
    rows = columns_each // n_seq
    scale = 1.0 / (length * n_seq)
    outs = (out((rows, 2 * STATE)),) * n_seq
    args = [tokens] + tokens_in + [gp_own] + gp_in
    scratch = (
        pltpu.VMEM((n_dp, length, columns_each), BF16),
        pltpu.VMEM((n_seq, rows, 2 * STATE), F32),
    )
    pieces = call(
        functools.partial(weight_body, n_dp, n_seq, rows, scale), outs, len(args), scratch, name="weight"
    )(ids, *args)
    grad_weight = pieces[0]
    for r in range(1, n_seq):
        pairs = [(i, (i + r) % n_seq) for i in range(n_seq)]
        grad_weight = grad_weight + lax.ppermute(pieces[r], "seq", pairs)

    parts = [gx_parts[0, c] for c in range(CHUNKS)]
    for r in range(1, q):
        parts += [swap(gx_parts[r, c], r) for c in range(CHUNKS)]
    grad_x = call(
        functools.partial(assemble_body, q, width),
        out((length, q * CHUNKS * width), BF16), len(parts), name="assemble",
    )(ids, *parts)
    return grad_x[None], grad_weight


def solution(mesh):
    return jax.shard_map(
        on_device,
        mesh=mesh,
        in_specs=(
            P("dp", "seq", None),
            P(),
            P("dp", "seq", None),
            P("dp", None, "seq"),
            P("dp", None, "seq"),
            P(),
            P("dp", "seq", None),
        ),
        out_specs=(P("dp", "seq", None), P(("dp", "seq"), None)),
        check_vma=False,
    )
```

```python
import functools

import jax
import jax.numpy as jnp
from jax import lax
from jax.experimental import pallas as pl
from jax.experimental.pallas import tpu as pltpu
from jax.sharding import PartitionSpec as P

HEADS = 32
HEAD_DIM = 64
STATE = 128
SPAN = 128
CHUNKS = 2
F32 = jnp.float32
BF16 = jnp.bfloat16
VMEM_LIMIT = 16 * 1024 * 1024


def group_size(n_seq):
    q = 1
    while n_seq % (2 * q) == 0 and 4 * q * q <= n_seq:
        q *= 2
    return q


def nn(a, b):
    return lax.dot_general(a, b, (((1,), (0,)), ((), ())), preferred_element_type=F32)


def nt(a, b):
    return lax.dot_general(a, b, (((1,), (1,)), ((), ())), preferred_element_type=F32)


def tn(a, b):
    return lax.dot_general(a, b, (((0,), (0,)), ((), ())), preferred_element_type=F32)


def exact(a, b, dims):
    return lax.dot_general(
        a, b, (dims, ((), ())), preferred_element_type=F32, precision=lax.Precision.HIGHEST
    )


def call(body, outs, n_in, scratch=(), name=None, cost=None, smem=1):
    specs = [pl.BlockSpec(memory_space=pltpu.SMEM)] * smem
    specs += [pl.BlockSpec(memory_space=pltpu.VMEM)] * n_in
    return pl.pallas_call(
        body,
        out_shape=outs,
        in_specs=specs,
        out_specs=jax.tree.map(lambda _: pl.BlockSpec(memory_space=pltpu.VMEM), outs),
        scratch_shapes=scratch,
        compiler_params=pltpu.CompilerParams(vmem_limit_bytes=VMEM_LIMIT),
        cost_estimate=cost,
        name=name,
    )


def out(shape, dtype=F32):
    return jax.ShapeDtypeStruct(shape, dtype)


def iotas():
    rows = lax.broadcasted_iota(jnp.int32, (SPAN, SPAN), 0)
    cols = lax.broadcasted_iota(jnp.int32, (SPAN, SPAN), 1)
    return rows, cols


def columns(ref, start, width):
    return ref[:, pl.ds(pl.multiple_of(start, 128), width)]


def pack_body(q, ids, *refs):
    x, g, packed = refs
    packed[0] = x[...].astype(F32)
    packed[1] = g[...].astype(F32)


def pack(ids, x, g, q, r, chunk, width):
    def place(i, ids):
        return 0, lax.rem(ids[0] + r, q) * CHUNKS + chunk

    block = pl.BlockSpec((SPAN, width), place)
    return pl.pallas_call(
        functools.partial(pack_body, q),
        out_shape=out((2, SPAN, width)),
        grid_spec=pltpu.PrefetchScalarGridSpec(
            num_scalar_prefetch=1,
            grid=(1,),
            in_specs=[block, block],
            out_specs=pl.BlockSpec((2, SPAN, width), lambda i, ids: (0, 0, 0)),
        ),
        compiler_params=pltpu.CompilerParams(vmem_limit_bytes=VMEM_LIMIT),
        name="pack",
    )(ids, x, g)


def project_body(q, ids, tokens, weight, decay, step, *bundles):
    proj = nn(tokens[...], weight[...]).astype(BF16).astype(F32)
    heads = HEADS // q
    for r in range(q):
        at = pl.multiple_of(lax.rem(ids[0] + r, q) * heads, heads)
        bundles[r][:SPAN, :] = proj
        bundles[r][SPAN:, :SPAN] = decay[pl.ds(at, heads), :]
        bundles[r][SPAN:, SPAN:] = step[pl.ds(at, heads), :]


def states_body(q, hc, chunk, *refs):
    n = q - 1
    it = iter(refs)
    ids, x_ref, g_ref = next(it), next(it), next(it)
    xg_in = [next(it) for _ in range(n)]
    bundles = [next(it) for _ in range(q)]
    xs, gs, ws, ss, f1s, ds, own_s, own_g, total_s, total_g, plane, bcs, cums, avs = it
    width = hc * HEAD_DIM
    y = ids[0]
    first = (y * CHUNKS + chunk) * width
    xs[y] = columns(x_ref, first, width)
    gs[y] = columns(g_ref, first, width)
    low = SPAN + chunk * hc
    for r in range(q):
        at = lax.rem(y - r + q, q)
        if r > 0:
            xs[at] = xg_in[r - 1][0].astype(BF16)
            gs[at] = xg_in[r - 1][1].astype(BF16)
        bcs[at] = bundles[r][:SPAN, :].astype(BF16)
        cums[at] = bundles[r][low : low + hc, :SPAN]
        avs[at] = bundles[r][low : low + hc, SPAN:]
    rows, cols = iotas()
    tri = (rows >= cols).astype(F32)
    eye = (rows == cols).astype(F32)
    head_of = lax.broadcasted_iota(jnp.int32, (hc, width), 1) // HEAD_DIM
    spread = (head_of == lax.broadcasted_iota(jnp.int32, (hc, width), 0)).astype(F32)
    last = ((1,), (1,))
    for b in range(q):
        decay = cums[b]
        cum_c = exact(tri, decay, last)
        a_c = cum_c - exact(eye, jnp.log(avs[b]), last)
        cums[b] = exact(decay, tri, last)
        cum_x = exact(cum_c, spread, ((1,), (0,)))
        a_x = exact(a_c, spread, ((1,), (0,)))
        avs[b] = exact(a_c, eye, ((0,), (0,)))
        total = cum_x[SPAN - 1 : SPAN, :]
        f1 = jnp.exp(total - a_x)
        f1s[b] = f1
        ds[b] = jnp.exp(total)
        weighted = (xs[b].astype(F32) * f1).astype(BF16)
        scaled = (gs[b].astype(F32) * jnp.exp(cum_x)).astype(BF16)
        ws[b] = weighted
        ss[b] = scaled
        own_s[b] = tn(bcs[b][:, :STATE], weighted)
        own_g[b] = tn(bcs[b][:, STATE:], scaled)
    forward, backward, through = own_s[0], own_g[q - 1], ds[0]
    for b in range(1, q):
        forward = ds[b] * forward + own_s[b]
        backward = ds[q - 1 - b] * backward + own_g[q - 1 - b]
        through = through * ds[b]
    total_s[...] = forward
    total_g[...] = backward
    plane[...] = through


def local_body(q, hc, chunk, ids, skip, xs, gs, bcs, cums, avs, gx, gp):
    rows, cols = iotas()
    causal = rows <= cols
    low = lax.broadcasted_iota(jnp.int32, (SPAN, 128), 1) < HEAD_DIM
    eye = (rows == cols).astype(F32)
    first = (ids[0] * CHUNKS + chunk) * hc
    for b in range(q):
        b_cols, c_cols = bcs[b][:, :STATE], bcs[b][:, STATE:]
        kernel = nt(b_cols, c_cols)
        a_c = exact(eye, avs[b], ((1,), (1,)))
        mixing = jnp.zeros((SPAN, SPAN), F32)
        for pair in range(hc // 2):
            at = slice(pair * 128, pair * 128 + 128)
            x, g = xs[b][:, at], gs[b][:, at]
            parts = []
            for half in range(2):
                h = 2 * pair + half
                gap = cums[b][h : h + 1, :] - a_c[:, h : h + 1]
                decay = jnp.exp(jnp.where(causal, gap, -jnp.inf))
                picked = jnp.where(low if half == 0 else ~low, x, jnp.zeros_like(x))
                mixing += decay * nt(picked, g)
                parts.append(nn((decay * kernel).astype(BF16), g))
            gains = jnp.where(low, skip[first + 2 * pair], skip[first + 2 * pair + 1])
            gx[b, :, at] = jnp.where(low, parts[0], parts[1]) + gains * g.astype(F32)
        mixed = mixing.astype(BF16)
        gp[b, :, :STATE] = nn(mixed, c_cols)
        gp[b, :, STATE:] = tn(mixed, b_cols)


def final_body(q, more, *refs):
    it = iter(refs)
    ids, start, after, own_s, own_g, ds, ws, ss, f1s, bcs, gx, gp = [next(it) for _ in range(12)]
    before = next(it) if more else None
    gx_out = [next(it) for _ in range(q)]
    gp_out, gx_all = it
    y = ids[0]
    state = start[...]
    for b in range(q):
        part = gp[b, :, STATE:] + nt(ss[b], state.astype(BF16))
        gp_out[b, :, STATE:] = part if before is None else part + before[b, :, STATE:]
        if b < q - 1:
            state = ds[b] * state + own_s[b]
    state = after[...]
    for b in range(q - 1, -1, -1):
        rounded = state.astype(BF16)
        gx_all[b] = gx[b] + f1s[b] * nn(bcs[b][:, :STATE], rounded)
        part = gp[b, :, :STATE] + nt(ws[b], rounded)
        gp_out[b, :, :STATE] = part if before is None else part + before[b, :, :STATE]
        if b > 0:
            state = ds[b] * state + own_g[b]
    for r in range(q):
        gx_out[r][...] = gx_all[lax.rem(y + r, q)]


def assemble_body(q, width, *refs):
    ids, result = refs[0], refs[-1]
    parts = refs[1:-1]
    y = ids[0]
    for r in range(q):
        group = lax.rem(y - r + q, q)
        for c in range(CHUNKS):
            at = pl.multiple_of((group * CHUNKS + c) * width, 128)
            result[:, pl.ds(at, width)] = parts[r * CHUNKS + c][...].astype(BF16)


def weight_body(n_dp, q, planes, rows, scale, *refs):
    it = iter(refs)
    ids = next(it)
    tokens = [next(it) for _ in range(n_dp)]
    swapped = [next(it) for _ in range(q - 1)]
    grads = [next(it) for _ in range(n_dp)]
    outs = [next(it) for _ in range(planes)]
    held, factors, products = it
    width = planes * rows
    y, z = ids[0], ids[1] // q
    for r in range(n_dp):
        held[y, r] = columns(tokens[r], y * width, width).astype(BF16)
        for b in range(q):
            factors[b, r] = grads[r][b].astype(BF16)
    for k in range(1, q):
        at = lax.rem(y - k + q, q)
        for r in range(n_dp):
            held[at, r] = swapped[k - 1][r].astype(BF16)
    total = tn(
        held[...].reshape(q * n_dp * SPAN, width), factors[...].reshape(q * n_dp * SPAN, 2 * STATE)
    )
    products[...] = (total * scale).reshape(planes, rows, 2 * STATE)
    for r in range(planes):
        outs[r][...] = products[lax.rem(z + r, planes)]


def behind(value, *others):
    return lax.optimization_barrier((value,) + others)[0]


def on_device(layer_input, proj_weight, inputs, step_size, log_decay, skip_gain, grad_out):
    n_seq, n_dp = lax.axis_size("seq"), lax.axis_size("dp")
    q = group_size(n_seq)
    planes = n_seq // q
    group_heads = HEADS // q
    hc = group_heads // CHUNKS
    width = hc * HEAD_DIM
    tokens, x, g = layer_input[0], inputs[0], grad_out[0]
    length, features = tokens.shape
    seq, dp = lax.axis_index("seq"), lax.axis_index("dp")
    y = lax.rem(seq, q)
    ids = jnp.stack([y, seq, dp]).astype(jnp.int32)

    def swap(value, r):
        pairs = [(z * q + i, z * q + (i + r) % q) for z in range(planes) for i in range(q)]
        return lax.ppermute(value, "seq", pairs)

    def across(value, r):
        return lax.ppermute(value, "dp", [(i, i ^ r) for i in range(n_dp)])

    xg_in = {}
    for r in range(1, q):
        xg_in[0, r] = swap(pack(ids, x, g, q, r, 0, width), r)
    bundle_out = (out((SPAN + group_heads, 2 * STATE)),) * q
    bundles = call(functools.partial(project_body, q), bundle_out, 4, name="project")(
        ids, tokens, proj_weight, log_decay[0], step_size[0]
    )
    bundles = [bundles[0]] + [swap(bundles[r], r) for r in range(1, q)]
    columns_each = features // n_dp
    rows = columns_each // n_seq
    part = planes * rows

    def quarter(owner):
        cut = lax.dynamic_slice_in_dim(tokens, owner * columns_each, columns_each, axis=1)
        order = [(z * q + i) * rows for i in range(q) for z in range(planes)]
        return jnp.concatenate([cut[:, at : at + rows] for at in order], axis=1)

    token_parts = [quarter(dp)]
    for r in range(1, n_dp):
        token_parts.append(across(quarter(dp ^ r).astype(F32), r))
    for c in range(1, CHUNKS):
        for r in range(1, q):
            packed = behind(pack(ids, x, g, q, r, c, width), xg_in[c - 1, r])
            xg_in[c, r] = swap(packed, r)
    swapped = []
    for r in range(1, q):
        at = lax.rem(y + r, q) * part
        cut = [lax.dynamic_slice_in_dim(v, at, part, axis=1).astype(F32) for v in token_parts]
        swapped.append(swap(behind(jnp.stack(cut), xg_in[CHUNKS - 1, r]), r))

    rows_of = (q, SPAN, width)
    held = []
    for c in range(CHUNKS):
        outs = (
            out(rows_of, BF16), out(rows_of, BF16), out(rows_of, BF16), out(rows_of, BF16),
            out(rows_of), out((q, 1, width)), out(rows_of), out(rows_of),
            out((STATE, width)), out((STATE, width)), out((1, width)),
            out((q, SPAN, 2 * STATE), BF16), out((q, hc, SPAN)), out((q, hc, SPAN)),
        )
        args = [x, g] + [xg_in[c, r] for r in range(1, q)] + bundles
        held.append(
            call(functools.partial(states_body, q, hc, c), outs, len(args), name="states")(ids, *args)
        )

    local = []
    for c in range(CHUNKS):
        xs, gs, _, _, _, _, _, _, _, _, _, bcs, cums, avs = held[c]
        local.append(
            call(
                functools.partial(local_body, q, hc, c),
                (out(rows_of), out((q, SPAN, 2 * STATE))), 5, smem=2, name="local",
            )(ids, skip_gain, xs, gs, bcs, cums, avs)
        )

    entries = []
    for c in range(CHUNKS):
        total_s, total_g, through = held[c][8:11]
        sent, back = total_s, total_g
        start, after = jnp.zeros_like(total_s), jnp.zeros_like(total_g)
        for t in range(planes - 1):
            up = [(t * q + i, (t + 1) * q + i) for i in range(q)]
            top = planes - 1 - t
            down = [(top * q + i, (top - 1) * q + i) for i in range(q)]
            got_s, got_g = lax.ppermute(sent, "seq", up), lax.ppermute(back, "seq", down)
            if t == planes - 2:
                got_s, got_g = behind(got_s, local[c]), behind(got_g, local[c])
            start += got_s
            after += got_g
            if t < planes - 2:
                sent = total_s + through * start
                back = total_g + through * after
        entries.append((start, after))

    before, gx_parts = [], {}
    for c in range(CHUNKS):
        _, _, ws, ss, f1s, ds, own_s, own_g, _, _, _, bcs, _, _ = held[c]
        gx, gp = local[c]
        start, after = entries[c]
        outs = (out((SPAN, width)),) * q + (out((q, SPAN, 2 * STATE)),)
        args = [start, after, own_s, own_g, ds, ws, ss, f1s, bcs, gx, gp] + before
        scratch = (pltpu.VMEM(rows_of, F32),)
        done = call(
            functools.partial(final_body, q, bool(before)), outs, len(args), scratch, name="final"
        )(ids, *args)
        for r in range(q):
            gx_parts[r, c] = done[r]
        before = [done[q]]

    gp = before[0]
    for r in range(1, q):
        gp = gp + swap(before[0], r)
    grads = {0: gp}
    bit = n_dp // 2
    while bit:
        for r in list(grads):
            grads[r ^ bit] = across(grads[r], bit)
        bit //= 2
    scale = 1.0 / (length * n_seq)
    outs = (out((rows, 2 * STATE)),) * planes
    args = token_parts + swapped + [grads[r] for r in range(n_dp)]
    scratch = (
        pltpu.VMEM((q, n_dp, SPAN, part), BF16),
        pltpu.VMEM((q, n_dp, SPAN, 2 * STATE), BF16),
        pltpu.VMEM((planes, rows, 2 * STATE), F32),
    )
    pieces = call(
        functools.partial(weight_body, n_dp, q, planes, rows, scale), outs, len(args), scratch, name="weight"
    )(ids, *args)
    grad_weight = pieces[0]
    for r in range(1, planes):
        pairs = [(z * q + i, (z + r) % planes * q + i) for z in range(planes) for i in range(q)]
        grad_weight = grad_weight + lax.ppermute(pieces[r], "seq", pairs)

    parts = [gx_parts[0, c] for c in range(CHUNKS)]
    for r in range(1, q):
        parts += [swap(gx_parts[r, c], r) for c in range(CHUNKS)]
    grad_x = call(
        functools.partial(assemble_body, q, width),
        out((length, q * CHUNKS * width), BF16), len(parts), name="assemble",
    )(ids, *parts)
    return grad_x[None], grad_weight


def solution(mesh):
    return jax.shard_map(
        on_device,
        mesh=mesh,
        in_specs=(
            P("dp", "seq", None),
            P(),
            P("dp", "seq", None),
            P("dp", None, "seq"),
            P("dp", None, "seq"),
            P(),
            P("dp", "seq", None),
        ),
        out_specs=(P("dp", "seq", None), P(("dp", "seq"), None)),
        check_vma=False,
    )
```

```python
import functools

import jax
import jax.numpy as jnp
from jax import lax
from jax.experimental import pallas as pl
from jax.experimental.pallas import tpu as pltpu
from jax.sharding import PartitionSpec as P

HEADS = 32
HEAD_DIM = 64
STATE = 128
SPAN = 128
PARTS = 3
F32 = jnp.float32
BF16 = jnp.bfloat16
VMEM_LIMIT = 16 * 1024 * 1024


def group_size(n_seq):
    q = 1
    while n_seq % (2 * q) == 0 and 4 * q * q <= n_seq:
        q *= 2
    return q


def nn(a, b):
    return lax.dot_general(a, b, (((1,), (0,)), ((), ())), preferred_element_type=F32)


def nt(a, b):
    return lax.dot_general(a, b, (((1,), (1,)), ((), ())), preferred_element_type=F32)


def tn(a, b):
    return lax.dot_general(a, b, (((0,), (0,)), ((), ())), preferred_element_type=F32)


def terms(a):
    high = a.astype(BF16)
    rest = a - high.astype(F32)
    mid = rest.astype(BF16)
    return high, mid, (rest - mid.astype(F32)).astype(BF16)


def head_chunks(heads):
    pairs, found, first = heads // 2, [], 0
    for c in range(PARTS):
        count = 2 * ((pairs + PARTS - 1 - c) // PARTS)
        found.append((first, count))
        first += count
    return found


def call(body, outs, n_in, scratch=(), name=None, smem=0, hbm=0):
    specs = [pl.BlockSpec(memory_space=pltpu.SMEM)] * smem
    specs += [pl.BlockSpec(memory_space=pltpu.HBM)] * hbm
    specs += [pl.BlockSpec(memory_space=pltpu.VMEM)] * n_in
    return pl.pallas_call(
        body,
        out_shape=outs,
        in_specs=specs,
        out_specs=jax.tree.map(lambda _: pl.BlockSpec(memory_space=pltpu.VMEM), outs),
        scratch_shapes=scratch,
        compiler_params=pltpu.CompilerParams(vmem_limit_bytes=VMEM_LIMIT),
        name=name,
    )


def in_group(q):
    return lax.rem(lax.axis_index("seq"), q)


def out(shape, dtype=F32):
    return jax.ShapeDtypeStruct(shape, dtype)


def iotas():
    rows = lax.broadcasted_iota(jnp.int32, (SPAN, SPAN), 0)
    cols = lax.broadcasted_iota(jnp.int32, (SPAN, SPAN), 1)
    return rows, cols


def columns(ref, start, width):
    return ref[:, pl.ds(pl.multiple_of(start, 128), width)]


def pack_body(q, group, first, width, x, g, own, *refs):
    packed, (stage, sems) = refs[: q - 1], refs[q - 1 :]
    y = in_group(q)
    copies = {}
    for r in list(range(1, q)) + [0]:
        at = pl.multiple_of(lax.rem(y + r, q) * group + first, 128)
        for k, source in enumerate((x, g)):
            target = stage.at[r - 1, k] if r else own.at[k]
            copy = pltpu.make_async_copy(source.at[:, pl.ds(at, width)], target, sems.at[r, k])
            copy.start()
            copies[r, k] = copy
    for r in range(1, q):
        for k in range(2):
            copies[r, k].wait()
            packed[r - 1][k] = stage[r - 1, k].astype(F32)
    for k in range(2):
        copies[0, k].wait()


def project_body(q, tokens, weight, decay, step, *bundles):
    proj = nn(tokens[...], weight[...]).astype(BF16).astype(F32)
    heads = HEADS // q
    y = in_group(q)
    for r in range(q):
        at = pl.multiple_of(lax.rem(y + r, q) * heads, heads)
        bundles[r][:SPAN, :] = proj
        bundles[r][SPAN:, :SPAN] = decay[pl.ds(at, heads), :]
        bundles[r][SPAN:, SPAN:] = step[pl.ds(at, heads), :]


def decays_body(q, heads, *refs):
    bundles = refs[:q]
    bcs, cums, a_cols, f1s, f2s, ds, steps = refs[q:]
    width = heads * HEAD_DIM
    y = in_group(q)
    for r in range(q):
        at = lax.rem(y - r + q, q)
        bcs[at] = bundles[r][:SPAN, :].astype(BF16)
        cums[at] = bundles[r][SPAN:, :SPAN]
        steps[at] = bundles[r][SPAN:, SPAN:]
    rows, cols = iotas()
    tri = jnp.where(rows <= cols, 1.0, 0.0).astype(BF16)
    head_of = lax.broadcasted_iota(jnp.int32, (heads, width), 1) // HEAD_DIM
    spread = head_of == lax.broadcasted_iota(jnp.int32, (heads, width), 0)
    spread = jnp.where(spread, 1.0, 0.0).astype(BF16)
    for b in range(q):
        cum = sum(nn(term, tri) for term in terms(cums[b]))
        a = cum - jnp.log(steps[b])
        cums[b] = cum
        cum_c, a_c = cum.T, a.T
        a_cols[b] = a_c
        cum_x = sum(nn(term, spread) for term in terms(cum_c))
        a_x = sum(nn(term, spread) for term in terms(a_c))
        total = cum_x[SPAN - 1 : SPAN, :]
        f1s[b] = jnp.exp(total - a_x)
        f2s[b] = jnp.exp(cum_x)
        ds[b] = jnp.exp(total)


def states_body(q, at, *refs):
    it = iter(refs)
    own = next(it)
    xg_in = [next(it) for _ in range(q - 1)]
    bcs, f1s, f2s, ds, xs, gs, ws, ss, own_s, own_g, total_s, total_g, plane = it
    y = in_group(q)
    xs[y] = own[0]
    gs[y] = own[1]
    for r in range(1, q):
        block = lax.rem(y - r + q, q)
        xs[block] = xg_in[r - 1][0].astype(BF16)
        gs[block] = xg_in[r - 1][1].astype(BF16)
    for b in range(q):
        ws[b] = (xs[b].astype(F32) * f1s[b, :, at]).astype(BF16)
        ss[b] = (gs[b].astype(F32) * f2s[b, :, at]).astype(BF16)
        own_s[b] = tn(bcs[b, :, :STATE], ws[b])
        own_g[b] = tn(bcs[b, :, STATE:], ss[b])
    forward, backward, through = own_s[0], own_g[q - 1], ds[0, :, at]
    for b in range(1, q):
        forward = ds[b, :, at] * forward + own_s[b]
        backward = ds[q - 1 - b, :, at] * backward + own_g[q - 1 - b]
        through = through * ds[b, :, at]
    total_s[...] = forward
    total_g[...] = backward
    plane[...] = through


def local_body(q, first, hc, skip, xs, gs, bcs, cums, a_cols, gx, gp):
    rows, cols = iotas()
    causal = rows <= cols
    low = lax.broadcasted_iota(jnp.int32, (SPAN, 128), 1) < HEAD_DIM
    skip_at = in_group(q) * (HEADS // q) + first
    for b in range(q):
        b_cols, c_cols = bcs[b, :, :STATE], bcs[b, :, STATE:]
        kernel = nt(b_cols, c_cols)
        mixing = jnp.zeros((SPAN, SPAN), F32)
        for pair in range(hc // 2):
            at = slice(pair * 128, pair * 128 + 128)
            x, g = xs[b, :, at], gs[b, :, at]
            parts = []
            for half in range(2):
                h = first + 2 * pair + half
                gap = cums[b, h : h + 1, :] - a_cols[b, :, h : h + 1]
                decay = jnp.exp(jnp.where(causal, gap, -jnp.inf))
                picked = jnp.where(low if half == 0 else ~low, x, jnp.zeros_like(x))
                mixing += decay * nt(picked, g)
                parts.append(nn((decay * kernel).astype(BF16), g))
            gains = jnp.where(low, skip[skip_at + 2 * pair], skip[skip_at + 2 * pair + 1])
            gx[b, :, at] = jnp.where(low, parts[0], parts[1]) + gains * g.astype(F32)
        mixed = mixing.astype(BF16)
        gp[b, :, :STATE] = nn(mixed, c_cols)
        gp[b, :, STATE:] = tn(mixed, b_cols)


def final_body(q, at, more, *refs):
    it = iter(refs)
    start, after, own_s, own_g, ds, ws, ss, f1s, bcs, gx, gp = [next(it) for _ in range(11)]
    before = next(it) if more else None
    gx_out = [next(it) for _ in range(q)]
    gp_out, gx_all = it
    y = in_group(q)
    state = start[...]
    for b in range(q):
        part = gp[b, :, STATE:] + nt(ss[b], state.astype(BF16))
        gp_out[b, :, STATE:] = part if before is None else part + before[b, :, STATE:]
        if b < q - 1:
            state = ds[b, :, at] * state + own_s[b]
    state = after[...]
    for b in range(q - 1, -1, -1):
        rounded = state.astype(BF16)
        gx_all[b] = gx[b] + f1s[b, :, at] * nn(bcs[b, :, :STATE], rounded)
        part = gp[b, :, :STATE] + nt(ws[b], rounded)
        gp_out[b, :, :STATE] = part if before is None else part + before[b, :, :STATE]
        if b > 0:
            state = ds[b, :, at] * state + own_g[b]
    for r in range(q):
        gx_out[r][...] = gx_all[lax.rem(y + r, q)]


def assemble_body(q, group, spans, *refs):
    parts, result = refs[:-1], refs[-1]
    y = in_group(q)
    for r in range(q):
        base = lax.rem(y - r + q, q) * group
        for c, (first, width) in enumerate(spans):
            at = pl.multiple_of(base + first, 128)
            result[:, pl.ds(at, width)] = parts[r * len(spans) + c][...].astype(BF16)


def weight_body(n_dp, q, planes, rows, scale, *refs):
    it = iter(refs)
    tokens = [next(it) for _ in range(n_dp)]
    swapped = [next(it) for _ in range(q - 1)]
    grads = [next(it) for _ in range(n_dp)]
    outs = [next(it) for _ in range(planes)]
    held, factors, products = it
    width = planes * rows
    seq = lax.axis_index("seq")
    y, z = lax.rem(seq, q), lax.div(seq, q)
    for r in range(n_dp):
        held[y, r] = columns(tokens[r], y * width, width).astype(BF16)
        for b in range(q):
            factors[b, r] = grads[r][b].astype(BF16)
    for k in range(1, q):
        at = lax.rem(y - k + q, q)
        for r in range(n_dp):
            held[at, r] = swapped[k - 1][r].astype(BF16)
    total = tn(
        held[...].reshape(q * n_dp * SPAN, width), factors[...].reshape(q * n_dp * SPAN, 2 * STATE)
    )
    products[...] = (total * scale).reshape(planes, rows, 2 * STATE)
    for r in range(planes):
        outs[r][...] = products[lax.rem(z + r, planes)]


def behind(value, *others):
    return lax.optimization_barrier((value,) + others)[0]


def on_device(layer_input, proj_weight, inputs, step_size, log_decay, skip_gain, grad_out):
    n_seq, n_dp = lax.axis_size("seq"), lax.axis_size("dp")
    q = group_size(n_seq)
    planes = n_seq // q
    heads = HEADS // q
    group = heads * HEAD_DIM
    chunks = head_chunks(heads)
    spans = [(first * HEAD_DIM, count * HEAD_DIM) for first, count in chunks]
    tokens, x, g = layer_input[0], inputs[0], grad_out[0]
    length, features = tokens.shape
    y, dp = in_group(q), lax.axis_index("dp")

    def swap(value, r):
        pairs = [(z * q + i, z * q + (i + r) % q) for z in range(planes) for i in range(q)]
        return lax.ppermute(value, "seq", pairs)

    def across(value, r):
        return lax.ppermute(value, "dp", [(i, i ^ r) for i in range(n_dp)])

    def pack(first, width):
        scratch = (pltpu.VMEM((q - 1, 2, SPAN, width), BF16), pltpu.SemaphoreType.DMA((q, 2)))
        outs = (out((2, SPAN, width), BF16),) + (out((2, SPAN, width)),) * (q - 1)
        body = functools.partial(pack_body, q, group, first, width)
        return call(body, outs, 0, scratch, name="pack", hbm=2)(x, g)

    packed = pack(*spans[0])
    own, xg_in = [packed[0]], [[swap(packed[r], r) for r in range(1, q)]]
    bundle_out = (out((SPAN + heads, 2 * STATE)),) * q
    bundles = call(functools.partial(project_body, q), bundle_out, 4, name="project")(
        tokens, proj_weight, log_decay[0], step_size[0]
    )
    bundles = [bundles[0]] + [swap(bundles[r], r) for r in range(1, q)]
    columns_each = features // n_dp
    rows = columns_each // n_seq
    part = planes * rows

    def quarter(owner):
        cut = lax.dynamic_slice_in_dim(tokens, owner * columns_each, columns_each, axis=1)
        order = [(z * q + i) * rows for i in range(q) for z in range(planes)]
        return jnp.concatenate([cut[:, at : at + rows] for at in order], axis=1)

    token_parts = [quarter(dp)] + [None] * (n_dp - 1)
    for r in range(n_dp - 1, 0, -1):
        token_parts[r] = across(quarter(dp ^ r).astype(F32), r)
    for c in range(1, PARTS):
        packed = pack(*spans[c])
        own.append(packed[0])
        got = [behind(packed[r], *xg_in[c - 1]) for r in range(1, q)]
        xg_in.append([swap(got[r - 1], r) for r in range(1, q)])

    rows_of = (q, SPAN, group)
    bcs, cums, a_cols, f1s, f2s, ds = call(
        functools.partial(decays_body, q, heads),
        (
            out((q, SPAN, 2 * STATE), BF16), out((q, heads, SPAN)), out((q, SPAN, heads)),
            out(rows_of), out(rows_of), out((q, 1, group)),
        ),
        q, (pltpu.VMEM((q, heads, SPAN), F32),), name="decays",
    )(*bundles)
    held = []
    for c, (first, width) in enumerate(spans):
        at = slice(first, first + width)
        wide, state = (q, SPAN, width), out((STATE, width))
        outs = (out(wide, BF16),) * 4 + (out(wide),) * 2 + (state, state, out((1, width)))
        args = [own[c]] + xg_in[c] + [bcs, f1s, f2s, ds]
        held.append(call(functools.partial(states_body, q, at), outs, len(args), name="states")(*args))

    swapped = []
    for r in range(1, q):
        at = lax.rem(y + r, q) * part
        ready = behind(tuple(token_parts), held[-1][6])
        cut = [lax.dynamic_slice_in_dim(v, at, part, axis=1).astype(F32) for v in ready]
        swapped.append(swap(jnp.stack(cut), r))

    local = []
    for c, (first, count) in enumerate(chunks):
        wide = (q, SPAN, count * HEAD_DIM)
        local.append(
            call(
                functools.partial(local_body, q, first, count),
                (out(wide), out((q, SPAN, 2 * STATE))), 5, smem=1, name="local",
            )(skip_gain, held[c][0], held[c][1], bcs, cums, a_cols)
        )

    sent = [(h[6], h[7]) for h in held]
    entries = [(jnp.zeros_like(h[6]), jnp.zeros_like(h[7])) for h in held]
    for t in range(planes - 1):
        up = [(t * q + i, (t + 1) * q + i) for i in range(q)]
        top = planes - 1 - t
        down = [(top * q + i, (top - 1) * q + i) for i in range(q)]
        for c in range(PARTS):
            got_s = lax.ppermute(sent[c][0], "seq", up)
            got_g = lax.ppermute(sent[c][1], "seq", down)
            if t == planes - 2:
                got_s, got_g = behind((got_s, got_g), local[c])
            start, after = entries[c][0] + got_s, entries[c][1] + got_g
            entries[c] = start, after
            total_s, total_g, through = held[c][6:9]
            sent[c] = total_s + through * start, total_g + through * after

    before, gx_parts = [], {}
    for c, (first, width) in enumerate(spans):
        _, _, ws, ss, own_s, own_g, _, _, _ = held[c]
        gx, gp = local[c]
        start, after = entries[c]
        at = slice(first, first + width)
        outs = (out((SPAN, width)),) * q + (out((q, SPAN, 2 * STATE)),)
        args = [start, after, own_s, own_g, ds, ws, ss, f1s, bcs, gx, gp] + before
        scratch = (pltpu.VMEM((q, SPAN, width), F32),)
        body = functools.partial(final_body, q, at, bool(before))
        done = call(body, outs, len(args), scratch, name="final")(*args)
        for r in range(q):
            gx_parts[r, c] = done[r]
        before = [done[q]]

    gp = before[0]
    for r in range(1, q):
        gp = gp + swap(before[0], r)
    grads = {0: gp}
    bit = n_dp // 2
    while bit:
        for r in list(grads):
            grads[r ^ bit] = across(grads[r], bit)
        bit //= 2
    scale = 1.0 / (length * n_seq)
    outs = (out((rows, 2 * STATE)),) * planes
    args = token_parts + swapped + [grads[r] for r in range(n_dp)]
    scratch = (
        pltpu.VMEM((q, n_dp, SPAN, part), BF16),
        pltpu.VMEM((q, n_dp, SPAN, 2 * STATE), BF16),
        pltpu.VMEM((planes, rows, 2 * STATE), F32),
    )
    body = functools.partial(weight_body, n_dp, q, planes, rows, scale)
    pieces = call(body, outs, len(args), scratch, name="weight")(*args)
    grad_weight = pieces[0]
    for r in range(1, planes):
        pairs = [(z * q + i, (z + r) % planes * q + i) for z in range(planes) for i in range(q)]
        grad_weight = grad_weight + lax.ppermute(pieces[r], "seq", pairs)

    parts = [gx_parts[0, c] for c in range(PARTS)]
    for r in range(1, q):
        parts += [swap(gx_parts[r, c], r) for c in range(PARTS)]
    grad_x = call(
        functools.partial(assemble_body, q, group, spans),
        out((length, q * group), BF16), len(parts), name="assemble",
    )(*parts)
    return grad_x[None], grad_weight


def solution(mesh):
    return jax.shard_map(
        on_device,
        mesh=mesh,
        in_specs=(
            P("dp", "seq", None),
            P(),
            P("dp", "seq", None),
            P("dp", None, "seq"),
            P("dp", None, "seq"),
            P(),
            P("dp", "seq", None),
        ),
        out_specs=(P("dp", "seq", None), P(("dp", "seq"), None)),
        check_vma=False,
    )
```

```python
import functools

import jax
import jax.numpy as jnp
from jax import lax
from jax.experimental import pallas as pl
from jax.experimental.pallas import tpu as pltpu
from jax.sharding import PartitionSpec as P

HEADS = 32
HEAD_DIM = 64
STATE = 128
SPAN = 128
PARTS = 3
F32 = jnp.float32
BF16 = jnp.bfloat16
VMEM_LIMIT = 16 * 1024 * 1024


def group_size(n_seq):
    q = 1
    while n_seq % (2 * q) == 0 and 4 * q * q <= n_seq:
        q *= 2
    return q


def nn(a, b):
    return lax.dot_general(a, b, (((1,), (0,)), ((), ())), preferred_element_type=F32)


def nt(a, b):
    return lax.dot_general(a, b, (((1,), (1,)), ((), ())), preferred_element_type=F32)


def tn(a, b):
    return lax.dot_general(a, b, (((0,), (0,)), ((), ())), preferred_element_type=F32)


def terms(a):
    high = a.astype(BF16)
    rest = a - high.astype(F32)
    mid = rest.astype(BF16)
    return high, mid, (rest - mid.astype(F32)).astype(BF16)


def head_chunks(heads):
    pairs, found, first = heads // 2, [], 0
    for c in range(PARTS):
        count = 2 * ((pairs + PARTS - 1 - c) // PARTS)
        found.append((first, count))
        first += count
    return found


def whole(shape):
    return pl.BlockSpec(shape, lambda i, rank=len(shape): (0,) * rank)


def call(body, outs, scratch=(), name=None, smem=0, hbm=0):
    def run(*args):
        args = list(args)
        for k in range(smem, len(args)):
            if isinstance(args[k], list):
                args[k] = args[k][0]
            else:
                args[k] = pltpu.with_memory_space_constraint(args[k], pltpu.HBM)
        specs = [pl.BlockSpec(memory_space=pltpu.SMEM)] * smem
        specs += [pl.BlockSpec(memory_space=pltpu.HBM)] * hbm
        specs += [whole(a.shape) for a in args[smem + hbm :]]
        shapes = [o[0] if isinstance(o, list) else pltpu.HBM(o.shape, o.dtype) for o in outs]
        return pl.pallas_call(
            body,
            out_shape=tuple(shapes),
            grid=(1,),
            in_specs=specs,
            out_specs=tuple(whole(o.shape) for o in shapes),
            scratch_shapes=scratch,
            compiler_params=pltpu.CompilerParams(vmem_limit_bytes=VMEM_LIMIT),
            name=name,
        )(*args)

    return run


def loose(values):
    return [[value] for value in values]


def in_group(q):
    return lax.rem(lax.axis_index("seq"), q)


def out(shape, dtype=F32):
    return jax.ShapeDtypeStruct(shape, dtype)


def iotas():
    rows = lax.broadcasted_iota(jnp.int32, (SPAN, SPAN), 0)
    cols = lax.broadcasted_iota(jnp.int32, (SPAN, SPAN), 1)
    return rows, cols


def columns(ref, start, width):
    return ref[:, pl.ds(pl.multiple_of(start, 128), width)]


def pack_body(q, group, first, width, x, g, own, *refs):
    packed, (stage, sems) = refs[: q - 1], refs[q - 1 :]
    y = in_group(q)
    copies = {}
    for r in list(range(1, q)) + [0]:
        at = pl.multiple_of(lax.rem(y + r, q) * group + first, 128)
        for k, source in enumerate((x, g)):
            target = stage.at[r - 1, k] if r else own.at[k]
            copy = pltpu.make_async_copy(source.at[:, pl.ds(at, width)], target, sems.at[r, k])
            copy.start()
            copies[r, k] = copy
    for r in range(1, q):
        for k in range(2):
            copies[r, k].wait()
            packed[r - 1][k] = stage[r - 1, k].astype(F32)
    for k in range(2):
        copies[0, k].wait()


def deal_body(rows, q, planes, tokens, *outs):
    n_dp = len(outs)
    each = q * planes * rows
    dp = lax.axis_index("dp")
    for r in range(n_dp - 1, -1, -1):
        cut = columns(tokens, lax.bitwise_xor(dp, r) * each, each).astype(F32)
        for k in range(q * planes):
            at = (k % planes * q + k // planes) * rows
            outs[r][:, k * rows : (k + 1) * rows] = cut[:, at : at + rows]


def hand_body(q, part, *refs):
    tokens, outs = refs[: 1 - q], refs[1 - q :]
    y = in_group(q)
    for r in range(1, q):
        for k, ref in enumerate(tokens):
            outs[r - 1][k] = columns(ref, lax.rem(y + r, q) * part, part)


def project_body(q, tokens, weight, decay, step, *bundles):
    proj = nn(tokens[...], weight[...]).astype(BF16).astype(F32)
    heads = HEADS // q
    y = in_group(q)
    for r in range(q):
        at = pl.multiple_of(lax.rem(y + r, q) * heads, heads)
        bundles[r][:SPAN, :] = proj
        bundles[r][SPAN:, :SPAN] = decay[pl.ds(at, heads), :]
        bundles[r][SPAN:, SPAN:] = step[pl.ds(at, heads), :]


def decays_body(q, heads, *refs):
    bundles = refs[:q]
    bcs, cums, a_cols, f1s, f2s, ds, steps = refs[q:]
    width = heads * HEAD_DIM
    y = in_group(q)
    for r in range(q):
        at = lax.rem(y - r + q, q)
        bcs[at] = bundles[r][:SPAN, :].astype(BF16)
        cums[at] = bundles[r][SPAN:, :SPAN]
        steps[at] = bundles[r][SPAN:, SPAN:]
    rows, cols = iotas()
    tri = jnp.where(rows <= cols, 1.0, 0.0).astype(BF16)
    head_of = lax.broadcasted_iota(jnp.int32, (heads, width), 1) // HEAD_DIM
    spread = head_of == lax.broadcasted_iota(jnp.int32, (heads, width), 0)
    spread = jnp.where(spread, 1.0, 0.0).astype(BF16)
    for b in range(q):
        cum = sum(nn(term, tri) for term in terms(cums[b]))
        a = cum - jnp.log(steps[b])
        cums[b] = cum
        cum_c, a_c = cum.T, a.T
        a_cols[b] = a_c
        cum_x = sum(nn(term, spread) for term in terms(cum_c))
        a_x = sum(nn(term, spread) for term in terms(a_c))
        total = cum_x[SPAN - 1 : SPAN, :]
        f1s[b] = jnp.exp(total - a_x)
        f2s[b] = jnp.exp(cum_x)
        ds[b] = jnp.exp(total)


def states_body(q, at, *refs):
    it = iter(refs)
    own = next(it)
    xg_in = [next(it) for _ in range(q - 1)]
    bcs, f1s, f2s, ds, xs, gs, ws, ss, own_s, own_g, total_s, total_g, plane = it
    y = in_group(q)
    xs[y] = own[0]
    gs[y] = own[1]
    for r in range(1, q):
        block = lax.rem(y - r + q, q)
        xs[block] = xg_in[r - 1][0].astype(BF16)
        gs[block] = xg_in[r - 1][1].astype(BF16)
    for b in range(q):
        ws[b] = (xs[b].astype(F32) * f1s[b, :, at]).astype(BF16)
        ss[b] = (gs[b].astype(F32) * f2s[b, :, at]).astype(BF16)
        own_s[b] = tn(bcs[b, :, :STATE], ws[b])
        own_g[b] = tn(bcs[b, :, STATE:], ss[b])
    forward, backward, through = own_s[0], own_g[q - 1], ds[0, :, at]
    for b in range(1, q):
        forward = ds[b, :, at] * forward + own_s[b]
        backward = ds[q - 1 - b, :, at] * backward + own_g[q - 1 - b]
        through = through * ds[b, :, at]
    total_s[...] = forward
    total_g[...] = backward
    plane[...] = through


def local_body(q, first, hc, skip, xs, gs, bcs, cums, a_cols, gx, gp):
    rows, cols = iotas()
    causal = rows <= cols
    low = lax.broadcasted_iota(jnp.int32, (SPAN, 128), 1) < HEAD_DIM
    skip_at = in_group(q) * (HEADS // q) + first
    for b in range(q):
        b_cols, c_cols = bcs[b, :, :STATE], bcs[b, :, STATE:]
        kernel = nt(b_cols, c_cols)
        mixing = jnp.zeros((SPAN, SPAN), F32)
        for pair in range(hc // 2):
            at = slice(pair * 128, pair * 128 + 128)
            x, g = xs[b, :, at], gs[b, :, at]
            parts = []
            for half in range(2):
                h = first + 2 * pair + half
                gap = cums[b, h : h + 1, :] - a_cols[b, :, h : h + 1]
                decay = jnp.exp(jnp.where(causal, gap, -jnp.inf))
                picked = jnp.where(low if half == 0 else ~low, x, jnp.zeros_like(x))
                mixing += decay * nt(picked, g)
                parts.append(nn((decay * kernel).astype(BF16), g))
            gains = jnp.where(low, skip[skip_at + 2 * pair], skip[skip_at + 2 * pair + 1])
            gx[b, :, at] = jnp.where(low, parts[0], parts[1]) + gains * g.astype(F32)
        mixed = mixing.astype(BF16)
        gp[b, :, :STATE] = nn(mixed, c_cols)
        gp[b, :, STATE:] = tn(mixed, b_cols)


def final_body(q, at, more, *refs):
    it = iter(refs)
    start, after, own_s, own_g, ds, ws, ss, f1s, bcs, gx, gp = [next(it) for _ in range(11)]
    before = next(it) if more else None
    gx_out = [next(it) for _ in range(q)]
    gp_out, gx_all = it
    y = in_group(q)
    state = start[...]
    for b in range(q):
        part = gp[b, :, STATE:] + nt(ss[b], state.astype(BF16))
        gp_out[b, :, STATE:] = part if before is None else part + before[b, :, STATE:]
        if b < q - 1:
            state = ds[b, :, at] * state + own_s[b]
    state = after[...]
    for b in range(q - 1, -1, -1):
        rounded = state.astype(BF16)
        gx_all[b] = gx[b] + f1s[b, :, at] * nn(bcs[b, :, :STATE], rounded)
        part = gp[b, :, :STATE] + nt(ws[b], rounded)
        gp_out[b, :, :STATE] = part if before is None else part + before[b, :, :STATE]
        if b > 0:
            state = ds[b, :, at] * state + own_g[b]
    for r in range(q):
        gx_out[r][...] = gx_all[lax.rem(y + r, q)]


def assemble_body(q, group, spans, *refs):
    parts, result = refs[:-1], refs[-1]
    y = in_group(q)
    for r in range(q):
        base = lax.rem(y - r + q, q) * group
        for c, (first, width) in enumerate(spans):
            at = pl.multiple_of(base + first, 128)
            result[:, pl.ds(at, width)] = parts[r * len(spans) + c][...].astype(BF16)


def weight_body(n_dp, q, planes, rows, scale, *refs):
    it = iter(refs)
    tokens = [next(it) for _ in range(n_dp)]
    swapped = [next(it) for _ in range(q - 1)]
    grads = [next(it) for _ in range(n_dp)]
    outs = [next(it) for _ in range(planes)]
    held, factors, products = it
    width = planes * rows
    seq = lax.axis_index("seq")
    y, z = lax.rem(seq, q), lax.div(seq, q)
    for r in range(n_dp):
        held[y, r] = columns(tokens[r], y * width, width).astype(BF16)
        for b in range(q):
            factors[b, r] = grads[r][b].astype(BF16)
    for k in range(1, q):
        at = lax.rem(y - k + q, q)
        for r in range(n_dp):
            held[at, r] = swapped[k - 1][r].astype(BF16)
    total = tn(
        held[...].reshape(q * n_dp * SPAN, width), factors[...].reshape(q * n_dp * SPAN, 2 * STATE)
    )
    products[...] = (total * scale).reshape(planes, rows, 2 * STATE)
    for r in range(planes):
        outs[r][...] = products[lax.rem(z + r, planes)]


def behind(value, *others):
    return lax.optimization_barrier((value,) + others)[0]


def on_device(layer_input, proj_weight, inputs, step_size, log_decay, skip_gain, grad_out):
    n_seq, n_dp = lax.axis_size("seq"), lax.axis_size("dp")
    q = group_size(n_seq)
    planes = n_seq // q
    heads = HEADS // q
    group = heads * HEAD_DIM
    chunks = head_chunks(heads)
    spans = [(first * HEAD_DIM, count * HEAD_DIM) for first, count in chunks]
    tokens, x, g = layer_input[0], inputs[0], grad_out[0]
    length, features = tokens.shape
    y, dp = in_group(q), lax.axis_index("dp")

    def swap(value, r):
        pairs = [(z * q + i, z * q + (i + r) % q) for z in range(planes) for i in range(q)]
        return lax.ppermute(value, "seq", pairs)

    def across(value, r):
        return lax.ppermute(value, "dp", [(i, i ^ r) for i in range(n_dp)])

    def pack(first, width):
        scratch = (pltpu.VMEM((q - 1, 2, SPAN, width), BF16), pltpu.SemaphoreType.DMA((q, 2)))
        outs = [out((2, SPAN, width), BF16)] + loose([out((2, SPAN, width))] * (q - 1))
        body = functools.partial(pack_body, q, group, first, width)
        return call(body, outs, scratch, name="pack", hbm=2)(x, g)

    packed = pack(*spans[0])
    own, xg_in = [packed[0]], [[swap(packed[r], r) for r in range(1, q)]]
    bundle_out = loose([out((SPAN + heads, 2 * STATE))] * q)
    bundles = call(functools.partial(project_body, q), bundle_out, name="project")(
        tokens, proj_weight, log_decay[0], step_size[0]
    )
    bundles = [bundles[0]] + [swap(bundles[r], r) for r in range(1, q)]
    columns_each = features // n_dp
    rows = columns_each // n_seq
    part = planes * rows

    shapes = [out((length, columns_each))] + loose([out((length, columns_each))] * (n_dp - 1))
    token_parts = list(call(functools.partial(deal_body, rows, q, planes), shapes, name="deal")(tokens))
    dealt = tuple(token_parts[1:])
    for r in range(n_dp - 1, 0, -1):
        token_parts[r] = across(token_parts[r], r)
    for c in range(1, PARTS):
        packed = pack(*spans[c])
        own.append(packed[0])
        ahead = dealt if c == 1 else xg_in[c - 2]
        got = [behind(packed[r], *ahead) for r in range(1, q)]
        xg_in.append([swap(got[r - 1], r) for r in range(1, q)])

    rows_of = (q, SPAN, group)
    bcs, cums, a_cols, f1s, f2s, ds = call(
        functools.partial(decays_body, q, heads),
        (
            out((q, SPAN, 2 * STATE), BF16), out((q, heads, SPAN)), out((q, SPAN, heads)),
            out(rows_of), out(rows_of), out((q, 1, group)),
        ),
        (pltpu.VMEM((q, heads, SPAN), F32),), name="decays",
    )(*loose(bundles))
    held = []
    for c, (first, width) in enumerate(spans):
        at = slice(first, first + width)
        wide, state = (q, SPAN, width), out((STATE, width))
        outs = [out(wide, BF16)] * 4 + [out(wide)] * 2 + loose([state, state, out((1, width))])
        args = [own[c]] + loose(xg_in[c]) + [bcs, f1s, f2s, ds]
        held.append(call(functools.partial(states_body, q, at), outs, name="states")(*args))

    ready = behind(tuple(token_parts), held[-1][6])
    handed = call(
        functools.partial(hand_body, q, part), loose([out((n_dp, length, part))] * (q - 1)), name="hand"
    )(ready[0], *loose(ready[1:]))
    swapped = [swap(handed[r - 1], r) for r in range(1, q)]

    local = []
    for c, (first, count) in enumerate(chunks):
        wide = (q, SPAN, count * HEAD_DIM)
        local.append(
            call(
                functools.partial(local_body, q, first, count),
                (out(wide), out((q, SPAN, 2 * STATE))), smem=1, name="local",
            )(skip_gain, held[c][0], held[c][1], bcs, cums, a_cols)
        )

    sent = [(h[6], h[7]) for h in held]
    entries = [(jnp.zeros_like(h[6]), jnp.zeros_like(h[7])) for h in held]
    for t in range(planes - 1):
        up = [(t * q + i, (t + 1) * q + i) for i in range(q)]
        top = planes - 1 - t
        down = [(top * q + i, (top - 1) * q + i) for i in range(q)]
        for c in range(PARTS):
            got_s = lax.ppermute(sent[c][0], "seq", up)
            got_g = lax.ppermute(sent[c][1], "seq", down)
            if t == planes - 2:
                got_s, got_g = behind((got_s, got_g), local[c])
            start, after = entries[c][0] + got_s, entries[c][1] + got_g
            entries[c] = start, after
            total_s, total_g, through = held[c][6:9]
            sent[c] = total_s + through * start, total_g + through * after

    before, gx_parts = [], {}
    for c, (first, width) in enumerate(spans):
        _, _, ws, ss, own_s, own_g, _, _, _ = held[c]
        gx, gp = local[c]
        start, after = entries[c]
        at = slice(first, first + width)
        outs = [out((SPAN, width))] + loose([out((SPAN, width))] * (q - 1) + [out((q, SPAN, 2 * STATE))])
        args = [[start], [after], own_s, own_g, ds, ws, ss, f1s, bcs, gx, gp] + loose(before)
        scratch = (pltpu.VMEM((q, SPAN, width), F32),)
        body = functools.partial(final_body, q, at, bool(before))
        done = call(body, outs, scratch, name="final")(*args)
        for r in range(q):
            gx_parts[r, c] = done[r]
        before = [done[q]]

    gp = before[0]
    for r in range(1, q):
        gp = gp + swap(before[0], r)
    grads = {0: gp}
    bit = n_dp // 2
    while bit:
        for r in list(grads):
            grads[r ^ bit] = across(grads[r], bit)
        bit //= 2
    scale = 1.0 / (length * n_seq)
    outs = loose([out((rows, 2 * STATE))] * planes)
    args = token_parts[:1] + loose(token_parts[1:] + swapped + [grads[r] for r in range(n_dp)])
    scratch = (
        pltpu.VMEM((q, n_dp, SPAN, part), BF16),
        pltpu.VMEM((q, n_dp, SPAN, 2 * STATE), BF16),
        pltpu.VMEM((planes, rows, 2 * STATE), F32),
    )
    body = functools.partial(weight_body, n_dp, q, planes, rows, scale)
    pieces = call(body, outs, scratch, name="weight")(*args)
    grad_weight = pieces[0]
    for r in range(1, planes):
        pairs = [(z * q + i, (z + r) % planes * q + i) for z in range(planes) for i in range(q)]
        grad_weight = grad_weight + lax.ppermute(pieces[r], "seq", pairs)

    parts = [gx_parts[0, c] for c in range(PARTS)]
    for r in range(1, q):
        parts += loose([swap(gx_parts[r, c], r) for c in range(PARTS)])
    (grad_x,) = call(
        functools.partial(assemble_body, q, group, spans), [[out((length, q * group), BF16)]], name="assemble"
    )(*parts)
    return grad_x[None], grad_weight


def solution(mesh):
    return jax.shard_map(
        on_device,
        mesh=mesh,
        in_specs=(
            P("dp", "seq", None),
            P(),
            P("dp", "seq", None),
            P("dp", None, "seq"),
            P("dp", None, "seq"),
            P(),
            P("dp", "seq", None),
        ),
        out_specs=(P("dp", "seq", None), P(("dp", "seq"), None)),
        check_vma=False,
    )
```

```python
import functools

import jax
import jax.numpy as jnp
from jax import lax
from jax.experimental import pallas as pl
from jax.experimental.pallas import tpu as pltpu
from jax.sharding import PartitionSpec as P

HEADS = 32
HEAD_DIM = 64
STATE = 128
SPAN = 128
PARTS = 2
F32 = jnp.float32
BF16 = jnp.bfloat16
VMEM_LIMIT = 16 * 1024 * 1024


def group_size(n_seq):
    q = 1
    while n_seq % (2 * q) == 0 and 4 * q * q <= n_seq:
        q *= 2
    return q


def nn(a, b):
    return lax.dot_general(a, b, (((1,), (0,)), ((), ())), preferred_element_type=F32)


def nt(a, b):
    return lax.dot_general(a, b, (((1,), (1,)), ((), ())), preferred_element_type=F32)


def tn(a, b):
    return lax.dot_general(a, b, (((0,), (0,)), ((), ())), preferred_element_type=F32)


def terms(a):
    high = a.astype(BF16)
    rest = a - high.astype(F32)
    mid = rest.astype(BF16)
    return high, mid, (rest - mid.astype(F32)).astype(BF16)


def head_chunks(heads):
    first = 2 * (heads * 5 // 16)
    return [(0, first), (first, heads - first)]


def call(body, outs, scratch=(), name=None, smem=0):
    def run(*args):
        specs = [pl.BlockSpec(memory_space=pltpu.SMEM)] * smem
        specs += [pl.BlockSpec(memory_space=pltpu.VMEM)] * (len(args) - smem)
        return pl.pallas_call(
            body,
            out_shape=tuple(outs),
            in_specs=specs,
            out_specs=tuple(pl.BlockSpec(memory_space=pltpu.VMEM) for _ in outs),
            scratch_shapes=scratch,
            compiler_params=pltpu.CompilerParams(vmem_limit_bytes=VMEM_LIMIT),
            name=name,
        )(*args)

    return run


def whole(shape):
    return pl.BlockSpec(shape, lambda i, rank=len(shape): (0,) * rank)


def staged(body, outs, scratch=(), name=None, smem=0, hbm=0):
    def run(*args):
        args = list(args)
        for k in range(smem, len(args)):
            if isinstance(args[k], list):
                args[k] = args[k][0]
            else:
                args[k] = pltpu.with_memory_space_constraint(args[k], pltpu.HBM)
        specs = [pl.BlockSpec(memory_space=pltpu.SMEM)] * smem
        specs += [pl.BlockSpec(memory_space=pltpu.HBM)] * hbm
        specs += [whole(a.shape) for a in args[smem + hbm :]]
        shapes = [o[0] if isinstance(o, list) else pltpu.HBM(o.shape, o.dtype) for o in outs]
        return pl.pallas_call(
            body,
            out_shape=tuple(shapes),
            grid=(1,),
            in_specs=specs,
            out_specs=tuple(whole(o.shape) for o in shapes),
            scratch_shapes=scratch,
            compiler_params=pltpu.CompilerParams(vmem_limit_bytes=VMEM_LIMIT),
            name=name,
        )(*args)

    return run


def loose(values):
    return [[value] for value in values]


def in_group(q):
    return lax.rem(lax.axis_index("seq"), q)


def out(shape, dtype=F32):
    return jax.ShapeDtypeStruct(shape, dtype)


def iotas():
    rows = lax.broadcasted_iota(jnp.int32, (SPAN, SPAN), 0)
    cols = lax.broadcasted_iota(jnp.int32, (SPAN, SPAN), 1)
    return rows, cols


def columns(ref, start, width):
    return ref[:, pl.ds(pl.multiple_of(start, 128), width)]


def pack_body(q, group, first, width, x, g, *refs):
    packed, (stage, sems) = refs[: q - 1], refs[q - 1 :]
    y = in_group(q)
    copies = {}
    for r in range(1, q):
        at = pl.multiple_of(lax.rem(y + r, q) * group + first, 128)
        for k, source in enumerate((x, g)):
            copies[r, k] = pltpu.make_async_copy(
                source.at[:, pl.ds(at, width)], stage.at[r - 1, k], sems.at[r - 1, k]
            )
            copies[r, k].start()
    for r in range(1, q):
        for k in range(2):
            copies[r, k].wait()
            packed[r - 1][k] = stage[r - 1, k].astype(F32)


def deal_body(rows, q, planes, tokens, *outs):
    n_dp = len(outs)
    each = q * planes * rows
    dp = lax.axis_index("dp")
    for r in range(n_dp - 1, -1, -1):
        cut = columns(tokens, lax.bitwise_xor(dp, r) * each, each).astype(F32)
        for k in range(q * planes):
            at = (k % planes * q + k // planes) * rows
            outs[r][:, k * rows : (k + 1) * rows] = cut[:, at : at + rows]


def hand_body(q, part, *refs):
    tokens, outs = refs[: 1 - q], refs[1 - q :]
    y = in_group(q)
    for r in range(1, q):
        for k, ref in enumerate(tokens):
            outs[r - 1][k] = columns(ref, lax.rem(y + r, q) * part, part)


def project_body(q, tokens, weight, decay, step, *bundles):
    proj = nn(tokens[...], weight[...]).astype(BF16).astype(F32)
    heads = HEADS // q
    y = in_group(q)
    for r in range(q):
        at = pl.multiple_of(lax.rem(y + r, q) * heads, heads)
        bundles[r][:SPAN, :] = proj
        bundles[r][SPAN:, :SPAN] = decay[pl.ds(at, heads), :]
        bundles[r][SPAN:, SPAN:] = step[pl.ds(at, heads), :]


def states_body(q, first, hc, *refs):
    it = iter(refs)
    x_ref, g_ref = next(it), next(it)
    xg_in = [next(it) for _ in range(q - 1)]
    bundles = [next(it) for _ in range(q)]
    rows16, states, f1s, ds, total_s, total_g, plane, bcs, cums, a_cols, steps = it
    width = hc * HEAD_DIM
    y = in_group(q)
    at = pl.multiple_of(y * (HEADS // q * HEAD_DIM) + first * HEAD_DIM, 128)
    for k, ref in enumerate((x_ref, g_ref)):
        rows16[k, y] = ref[:, pl.ds(at, width)]
    low = SPAN + first
    for r in range(q):
        block = lax.rem(y - r + q, q)
        if r > 0:
            for k in range(2):
                rows16[k, block] = xg_in[r - 1][k].astype(BF16)
        bcs[block] = bundles[r][:SPAN, :].astype(BF16)
        cums[block] = bundles[r][low : low + hc, :SPAN]
        steps[block] = bundles[r][low : low + hc, SPAN:]
    rows, cols = iotas()
    tri = jnp.where(rows <= cols, 1.0, 0.0).astype(BF16)
    head_of = lax.broadcasted_iota(jnp.int32, (hc, width), 1) // HEAD_DIM
    spread = head_of == lax.broadcasted_iota(jnp.int32, (hc, width), 0)
    spread = jnp.where(spread, 1.0, 0.0).astype(BF16)
    for b in range(q):
        cum = sum(nn(term, tri) for term in terms(cums[b]))
        a = cum - jnp.log(steps[b])
        cums[b] = cum
        cum_c, a_c = cum.T, a.T
        a_cols[b] = a_c
        cum_x = sum(nn(term, spread) for term in terms(cum_c))
        a_x = sum(nn(term, spread) for term in terms(a_c))
        total = cum_x[SPAN - 1 : SPAN, :]
        f1 = jnp.exp(total - a_x)
        f1s[b] = f1
        ds[b] = jnp.exp(total)
        weighted = (rows16[0, b].astype(F32) * f1).astype(BF16)
        scaled = (rows16[1, b].astype(F32) * jnp.exp(cum_x)).astype(BF16)
        rows16[2, b] = weighted
        rows16[3, b] = scaled
        states[0, b] = tn(bcs[b, :, :STATE], weighted)
        states[1, b] = tn(bcs[b, :, STATE:], scaled)
    forward, backward, through = states[0, 0], states[1, q - 1], ds[0]
    for b in range(1, q):
        forward = ds[b] * forward + states[0, b]
        backward = ds[q - 1 - b] * backward + states[1, q - 1 - b]
        through = through * ds[b]
    total_s[...] = forward
    total_g[...] = backward
    plane[...] = through


def local_body(q, first, hc, skip, rows16, bcs, cums, a_cols, gx, gp):
    rows, cols = iotas()
    causal = rows <= cols
    low = lax.broadcasted_iota(jnp.int32, (SPAN, 128), 1) < HEAD_DIM
    skip_at = in_group(q) * (HEADS // q) + first
    for b in range(q):
        b_cols, c_cols = bcs[b, :, :STATE], bcs[b, :, STATE:]
        kernel = nt(b_cols, c_cols)
        mixing = jnp.zeros((SPAN, SPAN), F32)
        for pair in range(hc // 2):
            at = slice(pair * 128, pair * 128 + 128)
            x, g = rows16[0, b, :, at], rows16[1, b, :, at]
            parts = []
            for half in range(2):
                h = 2 * pair + half
                gap = cums[b, h : h + 1, :] - a_cols[b, :, h : h + 1]
                decay = jnp.exp(jnp.where(causal, gap, -jnp.inf))
                picked = jnp.where(low if half == 0 else ~low, x, jnp.zeros_like(x))
                mixing += decay * nt(picked, g)
                parts.append(nn((decay * kernel).astype(BF16), g))
            gains = jnp.where(low, skip[skip_at + 2 * pair], skip[skip_at + 2 * pair + 1])
            gx[b, :, at] = jnp.where(low, parts[0], parts[1]) + gains * g.astype(F32)
        mixed = mixing.astype(BF16)
        gp[b, :, :STATE] = nn(mixed, c_cols)
        gp[b, :, STATE:] = tn(mixed, b_cols)


def final_body(q, planes, more, *refs):
    it = iter(refs)
    got = [next(it) for _ in range(planes - 1)]
    rows16, states, f1s, ds, bcs, gx, gp = [next(it) for _ in range(7)]
    before = next(it) if more else None
    gx_out = [next(it) for _ in range(q)]
    gp_out, gx_all = it
    y = in_group(q)
    z = lax.div(lax.axis_index("seq"), q)
    start = after = jnp.zeros(got[0].shape, F32)
    for t in range(planes - 1):
        came = got[t][...]
        start += jnp.where(z == t + 1, 1.0, 0.0) * came
        after += jnp.where(z == planes - 2 - t, 1.0, 0.0) * came
    for b in range(q):
        part = gp[b, :, STATE:] + nt(rows16[3, b], start.astype(BF16))
        gp_out[b, :, STATE:] = part if before is None else part + before[b, :, STATE:]
        if b < q - 1:
            start = ds[b] * start + states[0, b]
    for b in range(q - 1, -1, -1):
        rounded = after.astype(BF16)
        gx_all[b] = gx[b] + f1s[b] * nn(bcs[b, :, :STATE], rounded)
        part = gp[b, :, :STATE] + nt(rows16[2, b], rounded)
        gp_out[b, :, :STATE] = part if before is None else part + before[b, :, :STATE]
        if b > 0:
            after = ds[b] * after + states[1, b]
    for r in range(q):
        gx_out[r][...] = gx_all[lax.rem(y + r, q)]


def assemble_body(q, group, spans, *refs):
    parts, result = refs[:-1], refs[-1]
    y = in_group(q)
    for r in range(q):
        base = lax.rem(y - r + q, q) * group
        for c, (first, width) in enumerate(spans):
            at = pl.multiple_of(base + first, 128)
            result[:, pl.ds(at, width)] = parts[r * len(spans) + c][...].astype(BF16)


def weight_body(n_dp, q, planes, rows, scale, *refs):
    it = iter(refs)
    tokens = [next(it) for _ in range(n_dp)]
    swapped = [next(it) for _ in range(q - 1)]
    grads = [next(it) for _ in range(n_dp)]
    outs = [next(it) for _ in range(planes)]
    held, factors, products = it
    width = planes * rows
    seq = lax.axis_index("seq")
    y, z = lax.rem(seq, q), lax.div(seq, q)
    for r in range(n_dp):
        held[y, r] = columns(tokens[r], y * width, width).astype(BF16)
        for b in range(q):
            factors[b, r] = grads[r][b].astype(BF16)
    for k in range(1, q):
        at = lax.rem(y - k + q, q)
        for r in range(n_dp):
            held[at, r] = swapped[k - 1][r].astype(BF16)
    total = tn(
        held[...].reshape(q * n_dp * SPAN, width), factors[...].reshape(q * n_dp * SPAN, 2 * STATE)
    )
    products[...] = (total * scale).reshape(planes, rows, 2 * STATE)
    for r in range(planes):
        outs[r][...] = products[lax.rem(z + r, planes)]


def behind(value, *others):
    return lax.optimization_barrier((value,) + others)[0]


def on_device(layer_input, proj_weight, inputs, step_size, log_decay, skip_gain, grad_out):
    n_seq, n_dp = lax.axis_size("seq"), lax.axis_size("dp")
    q = group_size(n_seq)
    planes = n_seq // q
    heads = HEADS // q
    group = heads * HEAD_DIM
    chunks = head_chunks(heads)
    spans = [(first * HEAD_DIM, count * HEAD_DIM) for first, count in chunks]
    tokens, x, g = layer_input[0], inputs[0], grad_out[0]
    length, features = tokens.shape
    seq = lax.axis_index("seq")

    def swap(value, r):
        pairs = [(z * q + i, z * q + (i + r) % q) for z in range(planes) for i in range(q)]
        return lax.ppermute(value, "seq", pairs)

    def across(value, r):
        return lax.ppermute(value, "dp", [(i, i ^ r) for i in range(n_dp)])

    def pack(first, width):
        scratch = (pltpu.VMEM((q - 1, 2, SPAN, width), BF16), pltpu.SemaphoreType.DMA((q - 1, 2)))
        outs = loose([out((2, SPAN, width))] * (q - 1))
        body = functools.partial(pack_body, q, group, first, width)
        return staged(body, outs, scratch, name="pack", hbm=2)(x, g)

    packed = pack(*spans[0])
    xg_in = [[swap(packed[r - 1], r) for r in range(1, q)]]
    bundles = call(
        functools.partial(project_body, q), [out((SPAN + heads, 2 * STATE))] * q, name="project"
    )(tokens, proj_weight, log_decay[0], step_size[0])
    projected = bundles[0]
    bundles = [projected] + [swap(bundles[r], r) for r in range(1, q)]
    packed = pack(*spans[1])
    got = [behind(packed[r - 1], projected) for r in range(1, q)]
    xg_in.append([swap(got[r - 1], r) for r in range(1, q)])
    columns_each = features // n_dp
    rows = columns_each // n_seq
    part = planes * rows

    shapes = [out((length, columns_each))] + loose([out((length, columns_each))] * (n_dp - 1))
    token_parts = list(
        staged(functools.partial(deal_body, rows, q, planes), shapes, name="deal")(tokens)
    )
    for r in range(n_dp - 1, 0, -1):
        token_parts[r] = across(token_parts[r], r)

    held, local = [], []
    for c, (first, count) in enumerate(chunks):
        wide = (q, SPAN, count * HEAD_DIM)
        state = out((STATE, wide[2]))
        outs = [
            out((4,) + wide, BF16), out((2,) + wide), out(wide), out((q, 1, wide[2])),
            state, state, out((1, wide[2])),
            out((q, SPAN, 2 * STATE), BF16), out((q, count, SPAN)), out((q, SPAN, count)),
        ]
        scratch = (pltpu.VMEM((q, count, SPAN), F32),)
        body = functools.partial(states_body, q, first, count)
        held.append(call(body, outs, scratch, name="states")(x, g, *xg_in[c], *bundles))
        body = functools.partial(local_body, q, first, count)
        rows16, bcs, cums, a_cols = (held[c][k] for k in (0, 7, 8, 9))
        outs = [out(wide), out((q, SPAN, 2 * STATE))]
        local.append(call(body, outs, smem=1, name="local")(skip_gain, rows16, bcs, cums, a_cols))

    ready = behind(tuple(token_parts), held[-1][6])
    handed = staged(
        functools.partial(hand_body, q, part), loose([out((n_dp, length, part))] * (q - 1)), name="hand"
    )(ready[0], *loose(ready[1:]))
    swapped = [swap(handed[r - 1], r) for r in range(1, q)]

    z = seq // q
    sent = [jnp.where(z < planes // 2, h[4], h[5]) for h in held]
    arrived = [[] for _ in held]
    for t in range(planes - 1):
        top = planes - 1 - t
        pairs = [(t * q + i, (t + 1) * q + i) for i in range(q)]
        pairs += [(top * q + i, (top - 1) * q + i) for i in range(q)]
        for c in range(PARTS):
            if c == 0 and t == planes - 2:
                sent[c] = behind(sent[c], *handed)
            came = lax.ppermute(sent[c], "seq", pairs)
            if t == max(planes - 3, 0):
                came = behind(came, local[c])
            if c == PARTS - 1 and t == planes - 2:
                came = behind(came, *swapped)
            arrived[c].append(came)
            if t < planes - 2:
                sent[c] = jnp.where(z == t + 1, held[c][4], held[c][5]) + held[c][6] * came

    before, gx_parts = [], {}
    for c, (first, width) in enumerate(spans):
        rows16, states, f1s, ds, bcs = (held[c][k] for k in (0, 1, 2, 3, 7))
        outs = [out((SPAN, width))] * q + [out((q, SPAN, 2 * STATE))]
        scratch = (pltpu.VMEM((q, SPAN, width), F32),)
        body = functools.partial(final_body, q, planes, bool(before))
        done = call(body, outs, scratch, name="final")(
            *arrived[c], rows16, states, f1s, ds, bcs, *local[c], *before
        )
        for r in range(q):
            gx_parts[r, c] = done[r]
        before = [done[q]]

    gp = before[0]
    for r in range(1, q):
        gp = gp + swap(before[0], r)
    grads = {0: gp}
    bit = n_dp // 2
    while bit:
        for r in list(grads):
            grads[r ^ bit] = across(grads[r], bit)
        bit //= 2
    scale = 1.0 / (length * n_seq)
    outs = [out((rows, 2 * STATE))] * planes
    args = token_parts + swapped + [grads[r] for r in range(n_dp)]
    scratch = (
        pltpu.VMEM((q, n_dp, SPAN, part), BF16),
        pltpu.VMEM((q, n_dp, SPAN, 2 * STATE), BF16),
        pltpu.VMEM((planes, rows, 2 * STATE), F32),
    )
    body = functools.partial(weight_body, n_dp, q, planes, rows, scale)
    pieces = call(body, outs, scratch, name="weight")(*args)
    grad_weight = pieces[0]
    for r in range(1, planes):
        pairs = [(z * q + i, (z + r) % planes * q + i) for z in range(planes) for i in range(q)]
        grad_weight = grad_weight + lax.ppermute(pieces[r], "seq", pairs)

    parts = [gx_parts[0, c] for c in range(PARTS)]
    for r in range(1, q):
        parts += [swap(gx_parts[r, c], r) for c in range(PARTS)]
    body = functools.partial(assemble_body, q, group, spans)
    (grad_x,) = call(body, [out((length, q * group), BF16)], name="assemble")(*parts)
    return grad_x[None], grad_weight


def solution(mesh):
    return jax.shard_map(
        on_device,
        mesh=mesh,
        in_specs=(
            P("dp", "seq", None),
            P(),
            P("dp", "seq", None),
            P("dp", None, "seq"),
            P("dp", None, "seq"),
            P(),
            P("dp", "seq", None),
        ),
        out_specs=(P("dp", "seq", None), P(("dp", "seq"), None)),
        check_vma=False,
    )
```

```python
import functools

import jax
import jax.numpy as jnp
from jax import lax
from jax.experimental import pallas as pl
from jax.experimental.pallas import tpu as pltpu
from jax.sharding import PartitionSpec as P

HEADS = 32
HEAD_DIM = 64
STATE = 128
SPAN = 128
PARTS = 2
F32 = jnp.float32
BF16 = jnp.bfloat16
VMEM_LIMIT = 16 * 1024 * 1024


def group_size(n_seq):
    q = 1
    while n_seq % (2 * q) == 0 and 4 * q * q <= n_seq:
        q *= 2
    return q


def nn(a, b):
    return lax.dot_general(a, b, (((1,), (0,)), ((), ())), preferred_element_type=F32)


def nt(a, b):
    return lax.dot_general(a, b, (((1,), (1,)), ((), ())), preferred_element_type=F32)


def tn(a, b):
    return lax.dot_general(a, b, (((0,), (0,)), ((), ())), preferred_element_type=F32)


def terms(a):
    high = a.astype(BF16)
    rest = a - high.astype(F32)
    mid = rest.astype(BF16)
    return high, mid, (rest - mid.astype(F32)).astype(BF16)


def head_chunks(heads):
    first = 2 * (heads * 5 // 16)
    return [(0, first), (first, heads - first)]


def call(body, outs, scratch=(), name=None, smem=0, hbm=0):
    def run(*args):
        args = list(args)
        for k in range(smem, len(args)):
            if isinstance(args[k], list):
                args[k] = args[k][0]
            else:
                place = pltpu.HBM if k < smem + hbm else pltpu.VMEM
                args[k] = pltpu.with_memory_space_constraint(args[k], place)
        specs = [pl.BlockSpec(memory_space=pltpu.SMEM)] * smem
        specs += [pl.BlockSpec(memory_space=pltpu.HBM)] * hbm
        specs += [pl.BlockSpec(memory_space=pltpu.VMEM)] * (len(args) - smem - hbm)
        return pl.pallas_call(
            body,
            out_shape=tuple(o[0] if isinstance(o, list) else pltpu.VMEM(o.shape, o.dtype) for o in outs),
            in_specs=specs,
            out_specs=tuple(pl.BlockSpec(memory_space=pltpu.VMEM) for _ in outs),
            scratch_shapes=scratch,
            compiler_params=pltpu.CompilerParams(vmem_limit_bytes=VMEM_LIMIT),
            name=name,
        )(*args)

    return run


def loose(values):
    return [[value] for value in values]


def in_group(q):
    return lax.rem(lax.axis_index("seq"), q)


def out(shape, dtype=F32):
    return jax.ShapeDtypeStruct(shape, dtype)


def iotas():
    rows = lax.broadcasted_iota(jnp.int32, (SPAN, SPAN), 0)
    cols = lax.broadcasted_iota(jnp.int32, (SPAN, SPAN), 1)
    return rows, cols


def columns(ref, start, width):
    return ref[:, pl.ds(pl.multiple_of(start, 128), width)]


def pack_body(q, group, first, width, keep, x, g, *refs):
    packed, rest = refs[: q - 1], list(refs[q - 1 :])
    own = rest.pop(0) if keep else None
    stage, sems = rest
    y = in_group(q)
    copies = {}
    for r in range(1, q):
        at = pl.multiple_of(lax.rem(y + r, q) * group + first, 128)
        for k, source in enumerate((x, g)):
            copies[r, k] = pltpu.make_async_copy(
                source.at[:, pl.ds(at, width)], stage.at[r - 1, k], sems.at[r, k]
            )
            copies[r, k].start()
    if keep:
        at = pl.multiple_of(y * group, 128)
        for k, source in enumerate((x, g)):
            copies[0, k] = pltpu.make_async_copy(source.at[:, pl.ds(at, group)], own.at[k], sems.at[0, k])
            copies[0, k].start()
    for r in range(1, q):
        for k in range(2):
            copies[r, k].wait()
            packed[r - 1][k] = stage[r - 1, k].astype(F32)
    if keep:
        for k in range(2):
            copies[0, k].wait()


def deal_body(rows, q, planes, tokens, *outs):
    n_dp = len(outs)
    each = q * planes * rows
    dp = lax.axis_index("dp")
    for r in range(n_dp - 1, -1, -1):
        cut = columns(tokens, lax.bitwise_xor(dp, r) * each, each).astype(F32)
        for k in range(q * planes):
            at = (k % planes * q + k // planes) * rows
            outs[r][:, k * rows : (k + 1) * rows] = cut[:, at : at + rows]


def hand_body(q, part, *refs):
    tokens, outs = refs[: 1 - q], refs[1 - q :]
    y = in_group(q)
    for r in range(1, q):
        for k, ref in enumerate(tokens):
            outs[r - 1][k] = columns(ref, lax.rem(y + r, q) * part, part)


def project_body(q, tokens, weight, decay, step, *bundles):
    proj = nn(tokens[...], weight[...]).astype(BF16).astype(F32)
    heads = HEADS // q
    y = in_group(q)
    for r in range(q):
        at = pl.multiple_of(lax.rem(y + r, q) * heads, heads)
        bundles[r][:SPAN, :] = proj
        bundles[r][SPAN:, :SPAN] = decay[pl.ds(at, heads), :]
        bundles[r][SPAN:, SPAN:] = step[pl.ds(at, heads), :]


def states_body(q, planes, first, hc, *refs):
    it = iter(refs)
    own = next(it)
    xg_in = [next(it) for _ in range(q - 1)]
    bundles = [next(it) for _ in range(q)]
    rows16, states, f1s, ds, totals, sent, plane, bcs, cums, a_cols, steps = it
    width = hc * HEAD_DIM
    y = in_group(q)
    for k in range(2):
        rows16[k, y] = own[k, :, first * HEAD_DIM : first * HEAD_DIM + width]
    low = SPAN + first
    for r in range(q):
        block = lax.rem(y - r + q, q)
        if r > 0:
            for k in range(2):
                rows16[k, block] = xg_in[r - 1][k].astype(BF16)
        bcs[block] = bundles[r][:SPAN, :].astype(BF16)
        cums[block] = bundles[r][low : low + hc, :SPAN]
        steps[block] = bundles[r][low : low + hc, SPAN:]
    rows, cols = iotas()
    tri = jnp.where(rows <= cols, 1.0, 0.0).astype(BF16)
    head_of = lax.broadcasted_iota(jnp.int32, (hc, width), 1) // HEAD_DIM
    spread = head_of == lax.broadcasted_iota(jnp.int32, (hc, width), 0)
    spread = jnp.where(spread, 1.0, 0.0).astype(BF16)
    for b in range(q):
        cum = sum(nn(term, tri) for term in terms(cums[b]))
        a = cum - jnp.log(steps[b])
        cums[b] = cum
        cum_c, a_c = cum.T, a.T
        a_cols[b] = a_c
        cum_x = sum(nn(term, spread) for term in terms(cum_c))
        a_x = sum(nn(term, spread) for term in terms(a_c))
        total = cum_x[SPAN - 1 : SPAN, :]
        f1 = jnp.exp(total - a_x)
        f1s[b] = f1
        ds[b] = jnp.exp(total)
        weighted = (rows16[0, b].astype(F32) * f1).astype(BF16)
        scaled = (rows16[1, b].astype(F32) * jnp.exp(cum_x)).astype(BF16)
        rows16[2, b] = weighted
        rows16[3, b] = scaled
        states[0, b] = tn(bcs[b, :, :STATE], weighted)
        states[1, b] = tn(bcs[b, :, STATE:], scaled)
    forward, backward, through = states[0, 0], states[1, q - 1], ds[0]
    for b in range(1, q):
        forward = ds[b] * forward + states[0, b]
        backward = ds[q - 1 - b] * backward + states[1, q - 1 - b]
        through = through * ds[b]
    totals[0] = forward
    totals[1] = backward
    plane[...] = through
    sent[...] = jnp.where(lax.div(lax.axis_index("seq"), q) < planes // 2, forward, backward)


def relay_body(q, hop, came, totals, plane, sent):
    up = lax.div(lax.axis_index("seq"), q) == hop + 1
    sent[...] = jnp.where(up, totals[0], totals[1]) + plane[...] * came[...]


def local_body(q, first, hc, skip, rows16, bcs, cums, a_cols, gx, gp):
    rows, cols = iotas()
    causal = rows <= cols
    low = lax.broadcasted_iota(jnp.int32, (SPAN, 128), 1) < HEAD_DIM
    skip_at = in_group(q) * (HEADS // q) + first
    for b in range(q):
        b_cols, c_cols = bcs[b, :, :STATE], bcs[b, :, STATE:]
        kernel = nt(b_cols, c_cols)
        mixing = jnp.zeros((SPAN, SPAN), F32)
        for pair in range(hc // 2):
            at = slice(pair * 128, pair * 128 + 128)
            x, g = rows16[0, b, :, at], rows16[1, b, :, at]
            parts = []
            for half in range(2):
                h = 2 * pair + half
                gap = cums[b, h : h + 1, :] - a_cols[b, :, h : h + 1]
                decay = jnp.exp(jnp.where(causal, gap, -jnp.inf))
                picked = jnp.where(low if half == 0 else ~low, x, jnp.zeros_like(x))
                mixing += decay * nt(picked, g)
                parts.append(nn((decay * kernel).astype(BF16), g))
            gains = jnp.where(low, skip[skip_at + 2 * pair], skip[skip_at + 2 * pair + 1])
            gx[b, :, at] = jnp.where(low, parts[0], parts[1]) + gains * g.astype(F32)
        mixed = mixing.astype(BF16)
        gp[b, :, :STATE] = nn(mixed, c_cols)
        gp[b, :, STATE:] = tn(mixed, b_cols)


def final_body(q, planes, more, *refs):
    it = iter(refs)
    got = [next(it) for _ in range(planes - 1)]
    rows16, states, f1s, ds, bcs, gx, gp = [next(it) for _ in range(7)]
    before = next(it) if more else None
    gx_out = [next(it) for _ in range(q)]
    gp_out, gx_all = it
    y = in_group(q)
    z = lax.div(lax.axis_index("seq"), q)
    start = after = jnp.zeros(got[0].shape, F32)
    for t in range(planes - 1):
        came = got[t][...]
        start += jnp.where(z == t + 1, 1.0, 0.0) * came
        after += jnp.where(z == planes - 2 - t, 1.0, 0.0) * came
    for b in range(q):
        part = gp[b, :, STATE:] + nt(rows16[3, b], start.astype(BF16))
        gp_out[b, :, STATE:] = part if before is None else part + before[b, :, STATE:]
        if b < q - 1:
            start = ds[b] * start + states[0, b]
    for b in range(q - 1, -1, -1):
        rounded = after.astype(BF16)
        gx_all[b] = gx[b] + f1s[b] * nn(bcs[b, :, :STATE], rounded)
        part = gp[b, :, :STATE] + nt(rows16[2, b], rounded)
        gp_out[b, :, :STATE] = part if before is None else part + before[b, :, :STATE]
        if b > 0:
            after = ds[b] * after + states[1, b]
    for r in range(q):
        gx_out[r][...] = gx_all[lax.rem(y + r, q)]


def assemble_body(q, group, spans, *refs):
    parts, result = refs[:-1], refs[-1]
    y = in_group(q)
    for r in range(q):
        base = lax.rem(y - r + q, q) * group
        for c, (first, width) in enumerate(spans):
            at = pl.multiple_of(base + first, 128)
            result[:, pl.ds(at, width)] = parts[r * len(spans) + c][...].astype(BF16)


def weight_body(n_dp, q, planes, rows, scale, *refs):
    it = iter(refs)
    tokens = [next(it) for _ in range(n_dp)]
    swapped = [next(it) for _ in range(q - 1)]
    grads = [next(it) for _ in range(n_dp)]
    outs = [next(it) for _ in range(planes)]
    held, factors, products = it
    width = planes * rows
    seq = lax.axis_index("seq")
    y, z = lax.rem(seq, q), lax.div(seq, q)
    for r in range(n_dp):
        held[y, r] = columns(tokens[r], y * width, width).astype(BF16)
        for b in range(q):
            factors[b, r] = grads[r][b].astype(BF16)
    for k in range(1, q):
        at = lax.rem(y - k + q, q)
        for r in range(n_dp):
            held[at, r] = swapped[k - 1][r].astype(BF16)
    total = tn(
        held[...].reshape(q * n_dp * SPAN, width), factors[...].reshape(q * n_dp * SPAN, 2 * STATE)
    )
    products[...] = (total * scale).reshape(planes, rows, 2 * STATE)
    for r in range(planes):
        outs[r][...] = products[lax.rem(z + r, planes)]


def behind(value, *others):
    return lax.optimization_barrier((value,) + others)[0]


def on_device(layer_input, proj_weight, inputs, step_size, log_decay, skip_gain, grad_out):
    n_seq, n_dp = lax.axis_size("seq"), lax.axis_size("dp")
    q = group_size(n_seq)
    planes = n_seq // q
    heads = HEADS // q
    group = heads * HEAD_DIM
    chunks = head_chunks(heads)
    spans = [(first * HEAD_DIM, count * HEAD_DIM) for first, count in chunks]
    tokens, x, g = layer_input[0], inputs[0], grad_out[0]
    length, features = tokens.shape
    seq = lax.axis_index("seq")

    def swap(value, r):
        pairs = [(z * q + i, z * q + (i + r) % q) for z in range(planes) for i in range(q)]
        return lax.ppermute(value, "seq", pairs)

    def across(value, r):
        return lax.ppermute(value, "dp", [(i, i ^ r) for i in range(n_dp)])

    def pack(first, width, keep):
        scratch = (pltpu.VMEM((q - 1, 2, SPAN, width), BF16), pltpu.SemaphoreType.DMA((q, 2)))
        outs = [out((2, SPAN, width))] * (q - 1) + [out((2, SPAN, group), BF16)] * keep
        body = functools.partial(pack_body, q, group, first, width, keep)
        return call(body, outs, scratch, name="pack", hbm=2)(x, g)

    packed = pack(*spans[0], False)
    xg_in = [[swap(packed[r - 1], r) for r in range(1, q)]]
    bundles = call(
        functools.partial(project_body, q), [out((SPAN + heads, 2 * STATE))] * q, name="project"
    )(*loose([tokens, proj_weight, log_decay[0], step_size[0]]))
    projected = bundles[0]
    bundles = [projected] + [swap(bundles[r], r) for r in range(1, q)]
    packed = pack(*spans[1], True)
    own = packed[q - 1]
    got = [behind(packed[r - 1], projected) for r in range(1, q)]
    xg_in.append([swap(got[r - 1], r) for r in range(1, q)])
    columns_each = features // n_dp
    rows = columns_each // n_seq
    part = planes * rows

    shapes = [out((length, columns_each))] * n_dp
    token_parts = list(
        call(functools.partial(deal_body, rows, q, planes), shapes, name="deal")(
            [behind(tokens, own)]
        )
    )
    for r in range(n_dp - 1, 0, -1):
        token_parts[r] = across(token_parts[r], r)

    held, local = [], []
    for c, (first, count) in enumerate(chunks):
        wide = (q, SPAN, count * HEAD_DIM)
        state = out((STATE, wide[2]))
        outs = [
            out((4,) + wide, BF16), out((2,) + wide), out(wide), out((q, 1, wide[2])),
            out((2, STATE, wide[2])), state, out((1, wide[2])),
            out((q, SPAN, 2 * STATE), BF16), out((q, count, SPAN)), out((q, SPAN, count)),
        ]
        scratch = (pltpu.VMEM((q, count, SPAN), F32),)
        body = functools.partial(states_body, q, planes, first, count)
        if c > 0:
            xg_in[c] = [behind(v, held[c - 1][5]) for v in xg_in[c]]
        held.append(call(body, outs, scratch, name="states")(own, *xg_in[c], *bundles))
        body = functools.partial(local_body, q, first, count)
        rows16, bcs, cums, a_cols = (held[c][k] for k in (0, 7, 8, 9))
        outs = [out(wide), out((q, SPAN, 2 * STATE))]
        local.append(call(body, outs, smem=1, name="local")(skip_gain, rows16, bcs, cums, a_cols))

    sent = [h[5] for h in held]
    arrived = [[] for _ in held]
    for t in range(planes - 1):
        top = planes - 1 - t
        pairs = [(t * q + i, (t + 1) * q + i) for i in range(q)]
        pairs += [(top * q + i, (top - 1) * q + i) for i in range(q)]
        for c in range(PARTS):
            if c == 0 and t == planes - 2 and t > 0:
                sent[c] = behind(sent[c], *handed)
            came = lax.ppermute(sent[c], "seq", pairs)
            if t == max(planes - 3, 0):
                came = behind(came, local[c])
            if c == PARTS - 1 and t == planes - 2 and t > 0:
                came = behind(came, *swapped)
            if c > 0 and t < planes - 2:
                came = behind(came, sent[c - 1])
            arrived[c].append(came)
            if t < planes - 2:
                (sent[c],) = call(
                    functools.partial(relay_body, q, t), [out(came.shape)], name="relay"
                )(came, held[c][4], held[c][6])
        if t == 0:
            ready = behind(tuple(token_parts), sent[0], sent[-1])
            handed = call(
                functools.partial(hand_body, q, part), [out((n_dp, length, part))] * (q - 1), name="hand"
            )(*ready)
            swapped = [swap(handed[r - 1], r) for r in range(1, q)]

    before, gx_parts = [], {}
    for c, (first, width) in enumerate(spans):
        rows16, states, f1s, ds, bcs = (held[c][k] for k in (0, 1, 2, 3, 7))
        outs = [out((SPAN, width))] * q + [out((q, SPAN, 2 * STATE))]
        scratch = (pltpu.VMEM((q, SPAN, width), F32),)
        body = functools.partial(final_body, q, planes, bool(before))
        done = call(body, outs, scratch, name="final")(
            *arrived[c], rows16, states, f1s, ds, bcs, *local[c], *before
        )
        for r in range(q):
            gx_parts[r, c] = done[r]
        before = [done[q]]

    gp = before[0]
    for r in range(1, q):
        gp = gp + swap(before[0], r)
    grads = {0: gp}
    bit = n_dp // 2
    while bit:
        for r in list(grads):
            grads[r ^ bit] = across(grads[r], bit)
        bit //= 2
    scale = 1.0 / (length * n_seq)
    outs = [out((rows, 2 * STATE))] * planes
    args = token_parts + swapped + [grads[r] for r in range(n_dp)]
    scratch = (
        pltpu.VMEM((q, n_dp, SPAN, part), BF16),
        pltpu.VMEM((q, n_dp, SPAN, 2 * STATE), BF16),
        pltpu.VMEM((planes, rows, 2 * STATE), F32),
    )
    body = functools.partial(weight_body, n_dp, q, planes, rows, scale)
    pieces = call(body, outs, scratch, name="weight")(*args)
    grad_weight = pieces[0]
    for r in range(1, planes):
        pairs = [(z * q + i, (z + r) % planes * q + i) for z in range(planes) for i in range(q)]
        grad_weight = grad_weight + lax.ppermute(pieces[r], "seq", pairs)

    parts = [gx_parts[0, c] for c in range(PARTS)]
    for r in range(1, q):
        parts += [swap(gx_parts[r, c], r) for c in range(PARTS)]
    body = functools.partial(assemble_body, q, group, spans)
    (grad_x,) = call(body, [[out((length, q * group), BF16)]], name="assemble")(*parts)
    return grad_x[None], grad_weight


def solution(mesh):
    return jax.shard_map(
        on_device,
        mesh=mesh,
        in_specs=(
            P("dp", "seq", None),
            P(),
            P("dp", "seq", None),
            P("dp", None, "seq"),
            P("dp", None, "seq"),
            P(),
            P("dp", "seq", None),
        ),
        out_specs=(P("dp", "seq", None), P(("dp", "seq"), None)),
        check_vma=False,
    )
```

```python
import functools

import jax
import jax.numpy as jnp
from jax import lax
from jax.experimental import pallas as pl
from jax.experimental.pallas import tpu as pltpu
from jax.sharding import PartitionSpec as P

HEADS = 32
HEAD_DIM = 64
STATE = 128
SPAN = 128
PARTS = 2
F32 = jnp.float32
BF16 = jnp.bfloat16
VMEM_LIMIT = 16 * 1024 * 1024


def group_size(n_seq):
    q = 1
    while n_seq % (4 * q) == 0 and HEADS // (2 * q) >= 4:
        q *= 2
    return q


def nn(a, b):
    return lax.dot_general(a, b, (((1,), (0,)), ((), ())), preferred_element_type=F32)


def nt(a, b):
    return lax.dot_general(a, b, (((1,), (1,)), ((), ())), preferred_element_type=F32)


def tn(a, b):
    return lax.dot_general(a, b, (((0,), (0,)), ((), ())), preferred_element_type=F32)


def terms(a):
    high = a.astype(BF16)
    rest = a - high.astype(F32)
    mid = rest.astype(BF16)
    return high, mid, (rest - mid.astype(F32)).astype(BF16)


def head_chunks(heads):
    first = 2 * (heads * 5 // 16)
    return [(0, first), (first, heads - first)]


def call(body, outs, scratch=(), name=None, smem=0, hbm=0):
    def run(*args):
        args = list(args)
        for k in range(smem, len(args)):
            if isinstance(args[k], list):
                args[k] = args[k][0]
            else:
                place = pltpu.HBM if k < smem + hbm else pltpu.VMEM
                args[k] = pltpu.with_memory_space_constraint(args[k], place)
        specs = [pl.BlockSpec(memory_space=pltpu.SMEM)] * smem
        specs += [pl.BlockSpec(memory_space=pltpu.HBM)] * hbm
        specs += [pl.BlockSpec(memory_space=pltpu.VMEM)] * (len(args) - smem - hbm)
        return pl.pallas_call(
            body,
            out_shape=tuple(o[0] if isinstance(o, list) else pltpu.VMEM(o.shape, o.dtype) for o in outs),
            in_specs=specs,
            out_specs=tuple(pl.BlockSpec(memory_space=pltpu.VMEM) for _ in outs),
            scratch_shapes=scratch,
            compiler_params=pltpu.CompilerParams(vmem_limit_bytes=VMEM_LIMIT),
            name=name,
        )(*args)

    return run


def loose(values):
    return [[value] for value in values]


def in_group(q):
    return lax.rem(lax.axis_index("seq"), q)


def out(shape, dtype=F32):
    return jax.ShapeDtypeStruct(shape, dtype)


def iotas():
    rows = lax.broadcasted_iota(jnp.int32, (SPAN, SPAN), 0)
    cols = lax.broadcasted_iota(jnp.int32, (SPAN, SPAN), 1)
    return rows, cols


def columns(ref, start, width):
    return ref[:, pl.ds(pl.multiple_of(start, 128), width)]


def pack_body(q, group, first, width, x, g, *refs):
    packed, own, (stage, sems) = refs[: q - 1], refs[q - 1], refs[q:]
    y = in_group(q)
    copies = {}
    for r in range(1, q):
        at = pl.multiple_of(lax.bitwise_xor(y, r) * group + first, 128)
        for k, source in enumerate((x, g)):
            copies[r, k] = pltpu.make_async_copy(
                source.at[:, pl.ds(at, width)], stage.at[r - 1, k], sems.at[r, k]
            )
            copies[r, k].start()
    at = pl.multiple_of(y * group, 128)
    for k, source in enumerate((x, g)):
        copies[0, k] = pltpu.make_async_copy(source.at[:, pl.ds(at, group)], own.at[k], sems.at[0, k])
        copies[0, k].start()
    blocks = width // 128
    for r in range(1, q):
        for k in range(2):
            copies[r, k].wait()
            for b in range(blocks):
                at = (k * blocks + b) * SPAN
                packed[r - 1][at : at + SPAN, :] = stage[r - 1, k, :, b * 128 : b * 128 + 128].astype(F32)
    for k in range(2):
        copies[0, k].wait()


def deal_body(bit, offsets, *refs):
    sent = refs[-1]
    for k, (ref, offset) in enumerate(zip(refs, offsets)):
        sent[k * bit : (k + 1) * bit] = ref[offset + bit : offset + 2 * bit]


def open_body(q, n_dp, group, width, tokens, weight, x, g, decay, step, *refs):
    firsts, (bundle, kept, dealt, held_t, held_w, stage, sems) = refs[: q - 1], refs[q - 1 :]
    heads = HEADS // q
    y = in_group(q)
    copies = {}
    for r in range(1, q):
        at = pl.multiple_of(lax.bitwise_xor(y, r) * group, 128)
        for k, source in enumerate((x, g)):
            copies[r, k] = pltpu.make_async_copy(
                source.at[:, pl.ds(at, width)], stage.at[r - 1, k], sems.at[r, k]
            )
    copies[0, 0] = pltpu.make_async_copy(tokens, held_t, sems.at[0, 0])
    copies[0, 1] = pltpu.make_async_copy(weight, held_w, sems.at[0, 1])
    for copy in copies.values():
        copy.start()
    blocks = width // 128
    for r in range(1, q):
        for k in range(2):
            copies[r, k].wait()
            for b in range(blocks):
                at = (k * blocks + b) * SPAN
                firsts[r - 1][at : at + SPAN, :] = stage[r - 1, k, :, b * 128 : b * 128 + 128].astype(F32)
    copies[0, 0].wait()
    copies[0, 1].wait()
    proj = nn(held_t[...], held_w[...]).astype(BF16).astype(F32)
    base = 2 * blocks * SPAN
    for r in range(q):
        own = pl.multiple_of(lax.bitwise_xor(y, r) * heads, heads)
        target, at = (firsts[r - 1], base) if r else (bundle, 0)
        target[at : at + SPAN, :] = proj[:, :STATE]
        target[at + SPAN : at + 2 * SPAN, :] = proj[:, STATE:]
        target[at + 2 * SPAN : at + 2 * SPAN + heads, :] = decay[pl.ds(own, heads), :]
        target[at + 2 * SPAN + heads :, :] = step[pl.ds(own, heads), :]
    each = tokens.shape[1] // n_dp
    dp = lax.axis_index("dp")
    for r in range(n_dp):
        to, at = (kept, r) if r < n_dp // 2 else (dealt, r - n_dp // 2)
        to[at] = columns(held_t, lax.bitwise_xor(dp, r) * each, each).astype(F32)


def states_body(q, planes, first, hc, base, *refs):
    it = iter(refs)
    own = next(it)
    bundles = [next(it) for _ in range(q)]
    xg_in = [next(it) for _ in range(q - 1)] if first else bundles[1:]
    rows16, states, f1s, ds, totals, sent, plane, bcs, cums, a_cols, steps = it
    width = hc * HEAD_DIM
    heads = HEADS // q
    blocks = width // 128
    y = in_group(q)
    for k in range(2):
        rows16[k, y] = own[k, :, first * HEAD_DIM : first * HEAD_DIM + width]
    for r in range(q):
        block = lax.bitwise_xor(y, r)
        if r > 0:
            for k in range(2):
                for b in range(blocks):
                    at = (k * blocks + b) * SPAN
                    rows16[k, block, :, b * 128 : b * 128 + 128] = xg_in[r - 1][at : at + SPAN, :].astype(BF16)
        low = base if r else 0
        bcs[block, :, :STATE] = bundles[r][low : low + SPAN, :].astype(BF16)
        bcs[block, :, STATE:] = bundles[r][low + SPAN : low + 2 * SPAN, :].astype(BF16)
        low += 2 * SPAN + first
        cums[block] = bundles[r][low : low + hc, :]
        steps[block] = bundles[r][low + heads : low + heads + hc, :]
    rows, cols = iotas()
    tri = jnp.where(rows <= cols, 1.0, 0.0).astype(BF16)
    head_of = lax.broadcasted_iota(jnp.int32, (hc, width), 1) // HEAD_DIM
    spread = head_of == lax.broadcasted_iota(jnp.int32, (hc, width), 0)
    spread = jnp.where(spread, 1.0, 0.0).astype(BF16)
    for b in range(q):
        cum = sum(nn(term, tri) for term in terms(cums[b]))
        a = cum - jnp.log(steps[b])
        cums[b] = cum
        cum_c, a_c = cum.T, a.T
        a_cols[b] = a_c
        cum_x = sum(nn(term, spread) for term in terms(cum_c))
        a_x = sum(nn(term, spread) for term in terms(a_c))
        total = cum_x[SPAN - 1 : SPAN, :]
        f1 = jnp.exp(total - a_x)
        f1s[b] = f1
        ds[b] = jnp.exp(total)
        weighted = (rows16[0, b].astype(F32) * f1).astype(BF16)
        scaled = (rows16[1, b].astype(F32) * jnp.exp(cum_x)).astype(BF16)
        rows16[2, b] = weighted
        rows16[3, b] = scaled
        states[0, b] = tn(bcs[b, :, :STATE], weighted)
        states[1, b] = tn(bcs[b, :, STATE:], scaled)
    forward, backward, through = states[0, 0], states[1, q - 1], ds[0]
    for b in range(1, q):
        forward = ds[b] * forward + states[0, b]
        backward = ds[q - 1 - b] * backward + states[1, q - 1 - b]
        through = through * ds[b]
    totals[0] = forward
    totals[1] = backward
    plane[...] = through
    sent[...] = jnp.where(lax.div(lax.axis_index("seq"), q) < planes // 2, forward, backward)


def relay_body(q, hop, came, totals, plane, sent):
    up = lax.div(lax.axis_index("seq"), q) == hop + 1
    sent[...] = jnp.where(up, totals[0], totals[1]) + plane[...] * came[...]


def local_body(q, first, hc, skip, rows16, bcs, cums, a_cols, gx, gp):
    rows, cols = iotas()
    causal = rows <= cols
    low = lax.broadcasted_iota(jnp.int32, (SPAN, 128), 1) < HEAD_DIM
    skip_at = in_group(q) * (HEADS // q) + first
    for b in range(q):
        b_cols, c_cols = bcs[b, :, :STATE], bcs[b, :, STATE:]
        kernel = nt(b_cols, c_cols)
        mixing = jnp.zeros((SPAN, SPAN), F32)
        for pair in range(hc // 2):
            at = slice(pair * 128, pair * 128 + 128)
            x, g = rows16[0, b, :, at], rows16[1, b, :, at]
            parts = []
            for half in range(2):
                h = 2 * pair + half
                gap = cums[b, h : h + 1, :] - a_cols[b, :, h : h + 1]
                decay = jnp.exp(jnp.where(causal, gap, -jnp.inf))
                picked = jnp.where(low if half == 0 else ~low, x, jnp.zeros_like(x))
                mixing += decay * nt(picked, g)
                parts.append(nn((decay * kernel).astype(BF16), g))
            gains = jnp.where(low, skip[skip_at + 2 * pair], skip[skip_at + 2 * pair + 1])
            gx[b, :, at] = jnp.where(low, parts[0], parts[1]) + gains * g.astype(F32)
        mixed = mixing.astype(BF16)
        gp[b, :, :STATE] = nn(mixed, c_cols)
        gp[b, :, STATE:] = tn(mixed, b_cols)


def final_body(q, planes, more, *refs):
    it = iter(refs)
    got = [next(it) for _ in range(planes - 1)]
    rows16, states, f1s, ds, bcs, gx, gp = [next(it) for _ in range(7)]
    before = next(it) if more else None
    gx_out = [next(it) for _ in range(q)]
    gp_sent = [next(it) for _ in range(q)] if more else []
    gp_out, gx_all = it
    y = in_group(q)
    z = lax.div(lax.axis_index("seq"), q)
    start = after = jnp.zeros(got[0].shape, F32)
    for t in range(planes - 1):
        came = got[t][...]
        start += jnp.where(z == t + 1, 1.0, 0.0) * came
        after += jnp.where(z == planes - 2 - t, 1.0, 0.0) * came
    for b in range(q):
        part = gp[b, :, STATE:] + nt(rows16[3, b], start.astype(BF16))
        gp_out[b, :, STATE:] = part if before is None else part + before[b, :, STATE:]
        if b < q - 1:
            start = ds[b] * start + states[0, b]
    for b in range(q - 1, -1, -1):
        rounded = after.astype(BF16)
        gx_all[b] = gx[b] + f1s[b] * nn(bcs[b, :, :STATE], rounded)
        part = gp[b, :, :STATE] + nt(rows16[2, b], rounded)
        gp_out[b, :, :STATE] = part if before is None else part + before[b, :, :STATE]
        if b > 0:
            after = ds[b] * after + states[1, b]
    for r in range(q):
        gx_out[r][...] = gx_all[lax.bitwise_xor(y, r)]
        if more:
            gp_sent[r][...] = gp_out[lax.bitwise_xor(y, r)]


def assemble_body(q, group, spans, *refs):
    parts, result = refs[:-1], refs[-1]
    y = in_group(q)
    for r in range(q):
        for c, (first, width) in enumerate(spans):
            at = pl.multiple_of(lax.bitwise_xor(y, r) * group + first, 128)
            result[:, pl.ds(at, width)] = parts[c * q + r][...].astype(BF16)


def weight_body(n_dp, n_seq, rows, scale, places, *refs):
    arrays = 1 + max(k for k, _ in places)
    tokens, grads, refs = refs[:arrays], refs[arrays : arrays + n_dp], refs[arrays + n_dp :]
    outs, (held, factors, products) = refs[:4], refs[4:]
    width = n_seq * rows
    half = n_seq // 4
    seq = lax.axis_index("seq")
    for r in range(n_dp):
        held[r] = tokens[places[r][0]][places[r][1]].astype(BF16)
        factors[r] = grads[r][...].astype(BF16)
    total = tn(held[...].reshape(n_dp * SPAN, width), factors[...].reshape(n_dp * SPAN, 2 * STATE))
    products[...] = (total * scale).reshape(n_seq, rows, 2 * STATE)
    for k in range(2 * half):
        near, at = 1 - k // half, k % half
        for other in range(2):
            outs[2 * near + other][at] = products[lax.bitwise_xor(seq, 2 * k + other)]


def behind(value, *others):
    return lax.optimization_barrier((value,) + others)[0]


def on_device(layer_input, proj_weight, inputs, step_size, log_decay, skip_gain, grad_out):
    n_seq, n_dp = lax.axis_size("seq"), lax.axis_size("dp")
    q = group_size(n_seq)
    planes = n_seq // q
    heads = HEADS // q
    group = heads * HEAD_DIM
    chunks = head_chunks(heads)
    spans = [(first * HEAD_DIM, count * HEAD_DIM) for first, count in chunks]
    tokens, x, g = layer_input[0], inputs[0], grad_out[0]
    length, features = tokens.shape
    seq = lax.axis_index("seq")

    def swap(value, r):
        return lax.ppermute(value, "seq", [(i, i ^ r) for i in range(n_seq)])

    def across(value, r):
        return lax.ppermute(value, "dp", [(i, i ^ r) for i in range(n_dp)])

    widths = [width for _, width in spans]
    base = 2 * widths[0]
    tail = 2 * SPAN + 2 * heads
    columns_each = features // n_dp
    rows = columns_each // n_seq
    body = functools.partial(open_body, q, n_dp, group, widths[0])
    scratch = (
        pltpu.VMEM(tokens.shape, BF16), pltpu.VMEM(proj_weight.shape, BF16),
        pltpu.VMEM((q - 1, 2, SPAN, widths[0]), BF16), pltpu.SemaphoreType.DMA((q, 2)),
    )
    outs = [out((base + tail, 128))] * (q - 1) + [out((tail, 128))]
    outs += [out((n_dp // 2, length, columns_each))] * 2
    opened = call(body, outs, scratch, name="open", hbm=4)(
        tokens, proj_weight, x, g, [log_decay[0]], [step_size[0]]
    )
    bundles = [opened[q - 1]] + [swap(opened[r - 1], r) for r in range(1, q)]
    body = functools.partial(pack_body, q, group, *spans[1])
    scratch = (pltpu.VMEM((q - 1, 2, SPAN, widths[1]), BF16), pltpu.SemaphoreType.DMA((q, 2)))
    outs = [out((2 * widths[1], 128))] * (q - 1) + [out((2, SPAN, group), BF16)]
    packed = call(body, outs, scratch, name="pack", hbm=2)(x, g)
    own = packed[q - 1]
    bit = n_dp // 2
    sources = {0: (opened[q], 0), bit: (across(opened[q + 1], bit), 0)}
    second = [swap(behind(packed[r - 1], opened[q - 1]), r) for r in range(1, q)]

    def hop(value, t):
        top = planes - 1 - t
        pairs = [(t * q + i, (t + 1) * q + i) for i in range(q)]
        pairs += [(top * q + i, (top - 1) * q + i) for i in range(q)]
        return lax.ppermute(value, "seq", pairs)

    held, local, extra = [], [], []
    for c, (first, count) in enumerate(chunks):
        wide = (q, SPAN, count * HEAD_DIM)
        state = out((STATE, wide[2]))
        outs = [
            out((4,) + wide, BF16), out((2,) + wide), out(wide), out((q, 1, wide[2])),
            out((2, STATE, wide[2])), state, out((1, wide[2])),
            out((q, SPAN, 2 * STATE), BF16), out((q, count, SPAN)), out((q, SPAN, count)),
        ]
        scratch = (pltpu.VMEM((q, count, SPAN), F32),)
        body = functools.partial(states_body, q, planes, first, count, base)
        if c > 0:
            ahead = hop(held[0][5], 0)
            extra = [behind(v, *local[0]) for v in second]
        held.append(call(body, outs, scratch, name="states")(own, *bundles, *extra))
        body = functools.partial(local_body, q, first, count)
        rows16, bcs, cums, a_cols = (held[c][k] for k in (0, 7, 8, 9))
        outs = [out(wide), out((q, SPAN, 2 * STATE))]
        local.append(call(body, outs, smem=1, name="local")(skip_gain, rows16, bcs, cums, a_cols))

    sent = [h[5] for h in held]
    arrived = [[] for _ in held]
    for t in range(planes - 1):
        for c in range(PARTS):
            if c == 1 and t == 0:
                sent[c] = behind(sent[c], ahead)
            came = ahead if c == t == 0 else hop(sent[c], t)
            if t == max(planes - 3, 0):
                came = behind(came, local[c])
            if c > 0 and t < planes - 2:
                came = behind(came, sent[c - 1])
            arrived[c].append(came)
            if t < planes - 2:
                (sent[c],) = call(
                    functools.partial(relay_body, q, t), [out(came.shape)], name="relay"
                )(came, held[c][4], held[c][6])

    before, gx_parts, returned = [], [], []
    for c, (first, width) in enumerate(spans):
        rows16, states, f1s, ds, bcs = (held[c][k] for k in (0, 1, 2, 3, 7))
        block, all_blocks = (SPAN, 2 * STATE), (q, SPAN, 2 * STATE)
        outs = [out((SPAN, width))] * q + ([out(block)] * q if before else [out(all_blocks)])
        scratch = (pltpu.VMEM((q, SPAN, width), F32),)
        if before:
            scratch = (pltpu.VMEM(all_blocks, F32),) + scratch
        body = functools.partial(final_body, q, planes, bool(before))
        done = call(body, outs, scratch, name="final")(
            *arrived[c], rows16, states, f1s, ds, bcs, *local[c], *before
        )
        gx_parts.append(list(done[:q]))
        before = list(done[q:])
        if c == 0:
            returned.append([swap(done[r], r) for r in range(1, q)])
            arrived[1][-1] = behind(arrived[1][-1], *returned[0])

    while bit > 1:
        bit //= 2
        order = list(sources)
        arrays = behind(tuple(sources[r][0] for r in order), before[0])
        body = functools.partial(deal_body, bit, [sources[r][1] for r in order])
        shape = (len(order) * bit, length, columns_each)
        (dealt,) = call(body, [out(shape)], name="deal")(*arrays)
        got = across(dealt, bit)
        for k, r in enumerate(order):
            sources[r ^ bit] = got, k * bit

    gp = before[0]
    for r in range(1, q):
        gp = gp + swap(before[r], r)
    returned.append([swap(behind(gx_parts[1][r], gp), r) for r in range(1, q)])
    grads = {0: behind(gp, *(v for v, _ in sources.values()))}
    bit = n_dp // 2
    while bit:
        for r in list(grads):
            grads[r ^ bit] = across(grads[r], bit)
        bit //= 2
    scale = 1.0 / (length * n_seq)
    arrays = list({id(v): v for v, _ in sources.values()}.values())
    places = [([v is a for a in arrays].index(True), at) for v, at in (sources[r] for r in range(n_dp))]
    args = arrays + [behind(grads[0], *returned[1])] + [grads[r] for r in range(1, n_dp)]
    scratch = (
        pltpu.VMEM((n_dp, SPAN, columns_each), BF16),
        pltpu.VMEM((n_dp, SPAN, 2 * STATE), BF16),
        pltpu.VMEM((n_seq, rows, 2 * STATE), F32),
    )
    body = functools.partial(weight_body, n_dp, n_seq, rows, scale, places)
    half = n_seq // 4
    far, far_sent, near, near_sent = call(body, [out((half, rows, 2 * STATE))] * 4, scratch, name="weight")(*args)
    far_in = swap(far_sent, 1)
    near_in = swap(behind(near_sent, far_sent), 1)
    far = far + far_in
    came = [swap(far[k], 2 * (half + k)) for k in range(half)]
    near = near + near_in
    came += [swap(near[k], 2 * k) for k in range(1, half)]
    grad_weight = near[0]
    for part in came:
        grad_weight = grad_weight + part

    body = functools.partial(assemble_body, q, group, spans)
    parts = [v for c in range(PARTS) for v in (gx_parts[c][0], *returned[c])]
    (grad_x,) = call(body, [[out((length, q * group), BF16)]], name="assemble")(*parts)
    return grad_x[None], grad_weight


def solution(mesh):
    return jax.shard_map(
        on_device,
        mesh=mesh,
        in_specs=(
            P("dp", "seq", None),
            P(),
            P("dp", "seq", None),
            P("dp", None, "seq"),
            P("dp", None, "seq"),
            P(),
            P("dp", "seq", None),
        ),
        out_specs=(P("dp", "seq", None), P(("dp", "seq"), None)),
        check_vma=False,
    )
```

```python
import functools

import jax
import jax.numpy as jnp
from jax import lax
from jax.experimental import pallas as pl
from jax.experimental.pallas import tpu as pltpu
from jax.sharding import PartitionSpec as P

HEADS = 32
HEAD_DIM = 64
STATE = 128
SPAN = 128
PARTS = 2
F32 = jnp.float32
BF16 = jnp.bfloat16
VMEM_LIMIT = 16 * 1024 * 1024


def group_size(n_seq):
    q = 1
    while n_seq % (4 * q) == 0 and HEADS // (2 * q) >= 4:
        q *= 2
    return q


def nn(a, b):
    return lax.dot_general(a, b, (((1,), (0,)), ((), ())), preferred_element_type=F32)


def nt(a, b):
    return lax.dot_general(a, b, (((1,), (1,)), ((), ())), preferred_element_type=F32)


def tn(a, b):
    return lax.dot_general(a, b, (((0,), (0,)), ((), ())), preferred_element_type=F32)


def terms(a):
    high = a.astype(BF16)
    rest = a - high.astype(F32)
    mid = rest.astype(BF16)
    return high, mid, (rest - mid.astype(F32)).astype(BF16)


def head_chunks(heads):
    first = 2 * (heads * 5 // 16)
    return [(0, first), (first, heads - first)]


def call(body, outs, scratch=(), name=None, smem=0, hbm=0):
    def run(*args):
        args = list(args)
        for k in range(smem, len(args)):
            if isinstance(args[k], list):
                args[k] = args[k][0]
            else:
                place = pltpu.HBM if k < smem + hbm else pltpu.VMEM
                args[k] = pltpu.with_memory_space_constraint(args[k], place)
        specs = [pl.BlockSpec(memory_space=pltpu.SMEM)] * smem
        specs += [pl.BlockSpec(memory_space=pltpu.HBM)] * hbm
        specs += [pl.BlockSpec(memory_space=pltpu.VMEM)] * (len(args) - smem - hbm)
        return pl.pallas_call(
            body,
            out_shape=tuple(o[0] if isinstance(o, list) else pltpu.VMEM(o.shape, o.dtype) for o in outs),
            in_specs=specs,
            out_specs=tuple(pl.BlockSpec(memory_space=pltpu.VMEM) for _ in outs),
            scratch_shapes=scratch,
            compiler_params=pltpu.CompilerParams(vmem_limit_bytes=VMEM_LIMIT),
            name=name,
        )(*args)

    return run


def loose(values):
    return [[value] for value in values]


def in_group(q):
    return lax.rem(lax.axis_index("seq"), q)


def out(shape, dtype=F32):
    return jax.ShapeDtypeStruct(shape, dtype)


def iotas():
    rows = lax.broadcasted_iota(jnp.int32, (SPAN, SPAN), 0)
    cols = lax.broadcasted_iota(jnp.int32, (SPAN, SPAN), 1)
    return rows, cols


def columns(ref, start, width):
    return ref[:, pl.ds(pl.multiple_of(start, 128), width)]


def pack_body(q, group, first, width, keep, x, g, *refs):
    packed, rest = refs[: q - 1], list(refs[q - 1 :])
    own = rest.pop(0) if keep else None
    stage, sems = rest
    y = in_group(q)
    copies = {}
    for r in range(1, q):
        at = pl.multiple_of(lax.bitwise_xor(y, r) * group + first, 128)
        for k, source in enumerate((x, g)):
            copies[r, k] = pltpu.make_async_copy(
                source.at[:, pl.ds(at, width)], stage.at[r - 1, k], sems.at[r, k]
            )
            copies[r, k].start()
    if keep:
        at = pl.multiple_of(y * group, 128)
        for k, source in enumerate((x, g)):
            copies[0, k] = pltpu.make_async_copy(source.at[:, pl.ds(at, group)], own.at[k], sems.at[0, k])
            copies[0, k].start()
    for r in range(1, q):
        for k in range(2):
            copies[r, k].wait()
            packed[r - 1][k] = stage[r - 1, k].astype(F32)
    if keep:
        for k in range(2):
            copies[0, k].wait()


def deal_body(bit, offsets, *refs):
    sent = refs[-1]
    for k, (ref, offset) in enumerate(zip(refs, offsets)):
        sent[k * bit : (k + 1) * bit] = ref[offset + bit : offset + 2 * bit]


def project_body(q, n_dp, tokens, weight, decay, step, *refs):
    bundles, (kept, dealt, held_t, held_w, held_d, held_s, sems) = refs[:q], refs[q:]
    copies = [
        pltpu.make_async_copy(source, target, sems.at[k])
        for k, (source, target) in enumerate(
            ((tokens, held_t), (weight, held_w), (decay, held_d), (step, held_s))
        )
    ]
    for copy in copies:
        copy.start()
    for copy in copies:
        copy.wait()
    heads = HEADS // q
    y = in_group(q)
    proj = nn(held_t[...], held_w[...]).astype(BF16).astype(F32)
    for r in range(q):
        at = pl.multiple_of(lax.bitwise_xor(y, r) * heads, heads)
        bundles[r][:SPAN, :] = proj
        bundles[r][SPAN:, :SPAN] = held_d[pl.ds(at, heads), :]
        bundles[r][SPAN:, SPAN:] = held_s[pl.ds(at, heads), :]
    each = tokens.shape[1] // n_dp
    dp = lax.axis_index("dp")
    for r in range(n_dp):
        to, at = (kept, r) if r < n_dp // 2 else (dealt, r - n_dp // 2)
        to[at] = columns(held_t, lax.bitwise_xor(dp, r) * each, each).astype(F32)


def decays_body(q, heads, *refs):
    bundles = refs[:q]
    bcs, cums, a_cols, f1s, f2s, ds, steps = refs[q:]
    width = heads * HEAD_DIM
    y = in_group(q)
    for r in range(q):
        at = lax.bitwise_xor(y, r)
        bcs[at] = bundles[r][:SPAN, :].astype(BF16)
        cums[at] = bundles[r][SPAN:, :SPAN]
        steps[at] = bundles[r][SPAN:, SPAN:]
    rows, cols = iotas()
    tri = jnp.where(rows <= cols, 1.0, 0.0).astype(BF16)
    head_of = lax.broadcasted_iota(jnp.int32, (heads, width), 1) // HEAD_DIM
    spread = head_of == lax.broadcasted_iota(jnp.int32, (heads, width), 0)
    spread = jnp.where(spread, 1.0, 0.0).astype(BF16)
    for b in range(q):
        cum = sum(nn(term, tri) for term in terms(cums[b]))
        a = cum - jnp.log(steps[b])
        cums[b] = cum
        cum_c, a_c = cum.T, a.T
        a_cols[b] = a_c
        cum_x = sum(nn(term, spread) for term in terms(cum_c))
        a_x = sum(nn(term, spread) for term in terms(a_c))
        total = cum_x[SPAN - 1 : SPAN, :]
        f1s[b] = jnp.exp(total - a_x)
        f2s[b] = jnp.exp(cum_x)
        ds[b] = jnp.exp(total)


def states_body(q, planes, at, *refs):
    it = iter(refs)
    own = next(it)
    xg_in = [next(it) for _ in range(q - 1)]
    bcs, f1s, f2s, ds, rows16, states, totals, sent, plane = it
    y = in_group(q)
    for k in range(2):
        rows16[k, y] = own[k, :, at]
        for r in range(1, q):
            rows16[k, lax.bitwise_xor(y, r)] = xg_in[r - 1][k].astype(BF16)
    for b in range(q):
        rows16[2, b] = (rows16[0, b].astype(F32) * f1s[b, :, at]).astype(BF16)
        rows16[3, b] = (rows16[1, b].astype(F32) * f2s[b, :, at]).astype(BF16)
        states[0, b] = tn(bcs[b, :, :STATE], rows16[2, b])
        states[1, b] = tn(bcs[b, :, STATE:], rows16[3, b])
    forward, backward, through = states[0, 0], states[1, q - 1], ds[0, :, at]
    for b in range(1, q):
        forward = ds[b, :, at] * forward + states[0, b]
        backward = ds[q - 1 - b, :, at] * backward + states[1, q - 1 - b]
        through = through * ds[b, :, at]
    totals[0] = forward
    totals[1] = backward
    plane[...] = through
    sent[...] = jnp.where(lax.div(lax.axis_index("seq"), q) < planes // 2, forward, backward)


def relay_body(q, hop, came, totals, plane, sent):
    up = lax.div(lax.axis_index("seq"), q) == hop + 1
    sent[...] = jnp.where(up, totals[0], totals[1]) + plane[...] * came[...]


def local_body(q, first, hc, skip, rows16, bcs, cums, a_cols, gx, gp):
    rows, cols = iotas()
    causal = rows <= cols
    low = lax.broadcasted_iota(jnp.int32, (SPAN, 128), 1) < HEAD_DIM
    skip_at = in_group(q) * (HEADS // q) + first
    for b in range(q):
        b_cols, c_cols = bcs[b, :, :STATE], bcs[b, :, STATE:]
        kernel = nt(b_cols, c_cols)
        mixing = jnp.zeros((SPAN, SPAN), F32)
        for pair in range(hc // 2):
            at = slice(pair * 128, pair * 128 + 128)
            x, g = rows16[0, b, :, at], rows16[1, b, :, at]
            parts = []
            for half in range(2):
                h = first + 2 * pair + half
                gap = cums[b, h : h + 1, :] - a_cols[b, :, h : h + 1]
                decay = jnp.exp(jnp.where(causal, gap, -jnp.inf))
                picked = jnp.where(low if half == 0 else ~low, x, jnp.zeros_like(x))
                mixing += decay * nt(picked, g)
                parts.append(nn((decay * kernel).astype(BF16), g))
            gains = jnp.where(low, skip[skip_at + 2 * pair], skip[skip_at + 2 * pair + 1])
            gx[b, :, at] = jnp.where(low, parts[0], parts[1]) + gains * g.astype(F32)
        mixed = mixing.astype(BF16)
        gp[b, :, :STATE] = nn(mixed, c_cols)
        gp[b, :, STATE:] = tn(mixed, b_cols)


def final_body(q, planes, at, more, *refs):
    it = iter(refs)
    got = [next(it) for _ in range(planes - 1)]
    rows16, states, f1s, ds, bcs, gx, gp = [next(it) for _ in range(7)]
    before = next(it) if more else None
    gx_out = [next(it) for _ in range(q)]
    gp_sent = [next(it) for _ in range(q)] if more else []
    gp_out, gx_all = it
    y = in_group(q)
    z = lax.div(lax.axis_index("seq"), q)
    start = after = jnp.zeros(got[0].shape, F32)
    for t in range(planes - 1):
        came = got[t][...]
        start += jnp.where(z == t + 1, 1.0, 0.0) * came
        after += jnp.where(z == planes - 2 - t, 1.0, 0.0) * came
    for b in range(q):
        part = gp[b, :, STATE:] + nt(rows16[3, b], start.astype(BF16))
        gp_out[b, :, STATE:] = part if before is None else part + before[b, :, STATE:]
        if b < q - 1:
            start = ds[b, :, at] * start + states[0, b]
    for b in range(q - 1, -1, -1):
        rounded = after.astype(BF16)
        gx_all[b] = gx[b] + f1s[b, :, at] * nn(bcs[b, :, :STATE], rounded)
        part = gp[b, :, :STATE] + nt(rows16[2, b], rounded)
        gp_out[b, :, :STATE] = part if before is None else part + before[b, :, :STATE]
        if b > 0:
            after = ds[b, :, at] * after + states[1, b]
    for r in range(q):
        gx_out[r][...] = gx_all[lax.bitwise_xor(y, r)]
        if more:
            gp_sent[r][...] = gp_out[lax.bitwise_xor(y, r)]


def assemble_body(q, group, spans, *refs):
    parts, result = refs[:-1], refs[-1]
    y = in_group(q)
    for r in range(q):
        for c, (first, width) in enumerate(spans):
            at = pl.multiple_of(lax.bitwise_xor(y, r) * group + first, 128)
            result[:, pl.ds(at, width)] = parts[c * q + r][...].astype(BF16)


def weight_body(n_dp, n_seq, rows, scale, places, *refs):
    arrays = 1 + max(k for k, _ in places)
    tokens, grads, refs = refs[:arrays], refs[arrays : arrays + n_dp], refs[arrays + n_dp :]
    outs, (held, factors, products) = refs[:4], refs[4:]
    width = n_seq * rows
    half = n_seq // 4
    seq = lax.axis_index("seq")
    for r in range(n_dp):
        held[r] = tokens[places[r][0]][places[r][1]].astype(BF16)
        factors[r] = grads[r][...].astype(BF16)
    total = tn(held[...].reshape(n_dp * SPAN, width), factors[...].reshape(n_dp * SPAN, 2 * STATE))
    products[...] = (total * scale).reshape(n_seq, rows, 2 * STATE)
    for k in range(2 * half):
        near, at = 1 - k // half, k % half
        for other in range(2):
            outs[2 * near + other][at] = products[lax.bitwise_xor(seq, 2 * k + other)]


def behind(value, *others):
    return lax.optimization_barrier((value,) + others)[0]


def on_device(layer_input, proj_weight, inputs, step_size, log_decay, skip_gain, grad_out):
    n_seq, n_dp = lax.axis_size("seq"), lax.axis_size("dp")
    q = group_size(n_seq)
    planes = n_seq // q
    heads = HEADS // q
    group = heads * HEAD_DIM
    chunks = head_chunks(heads)
    spans = [(first * HEAD_DIM, count * HEAD_DIM) for first, count in chunks]
    tokens, x, g = layer_input[0], inputs[0], grad_out[0]
    length, features = tokens.shape
    seq = lax.axis_index("seq")

    def swap(value, r):
        return lax.ppermute(value, "seq", [(i, i ^ r) for i in range(n_seq)])

    def across(value, r):
        return lax.ppermute(value, "dp", [(i, i ^ r) for i in range(n_dp)])

    columns_each = features // n_dp
    rows = columns_each // n_seq

    def pack(first, width, keep):
        scratch = (pltpu.VMEM((q - 1, 2, SPAN, width), BF16), pltpu.SemaphoreType.DMA((q, 2)))
        outs = [out((2, SPAN, width))] * (q - 1) + [out((2, SPAN, group), BF16)] * keep
        body = functools.partial(pack_body, q, group, first, width, keep)
        return call(body, outs, scratch, name="pack", hbm=2)(x, g)

    packed = pack(*spans[0], False)
    xg_in = [[swap(packed[r - 1], r) for r in range(1, q)]]
    scratch = (
        pltpu.VMEM(tokens.shape, BF16), pltpu.VMEM(proj_weight.shape, BF16),
        pltpu.VMEM((HEADS, SPAN), F32), pltpu.VMEM((HEADS, SPAN), F32), pltpu.SemaphoreType.DMA((4,)),
    )
    outs = [out((SPAN + heads, 2 * STATE))] * q + [out((n_dp // 2, length, columns_each))] * 2
    opened = call(functools.partial(project_body, q, n_dp), outs, scratch, name="project", hbm=4)(
        behind(tokens, packed[0]), proj_weight, log_decay[0], step_size[0]
    )
    bundles = [opened[0]] + [swap(opened[r], r) for r in range(1, q)]
    packed = pack(*spans[1], True)
    own = packed[q - 1]
    xg_in.append([swap(behind(packed[r - 1], opened[0]), r) for r in range(1, q)])
    bit = n_dp // 2
    sources = {0: (opened[q], 0), bit: (across(behind(opened[q + 1], *xg_in[0]), bit), 0)}

    rows_of = (q, SPAN, group)
    outs = [
        out((q, SPAN, 2 * STATE), BF16), out((q, heads, SPAN)), out((q, SPAN, heads)),
        out(rows_of), out(rows_of), out((q, 1, group)),
    ]
    body = functools.partial(decays_body, q, heads)
    bcs, cums, a_cols, f1s, f2s, ds = call(body, outs, (pltpu.VMEM((q, heads, SPAN), F32),), name="decays")(
        behind(bundles[0], *xg_in[0]), *bundles[1:]
    )

    def hop(value, t):
        top = planes - 1 - t
        pairs = [(t * q + i, (t + 1) * q + i) for i in range(q)]
        pairs += [(top * q + i, (top - 1) * q + i) for i in range(q)]
        return lax.ppermute(value, "seq", pairs)

    held, local = [], []
    for c, (first, count) in enumerate(chunks):
        wide = (q, SPAN, count * HEAD_DIM)
        state = out((STATE, wide[2]))
        at = slice(first * HEAD_DIM, (first + count) * HEAD_DIM)
        if c > 0:
            ahead = hop(held[0][3], 0)
            xg_in[c] = [behind(v, *local[0]) for v in xg_in[c]]
        outs = [out((4,) + wide, BF16), out((2,) + wide), out((2, STATE, wide[2])), state, out((1, wide[2]))]
        body = functools.partial(states_body, q, planes, at)
        held.append(call(body, outs, name="states")(own, *xg_in[c], bcs, f1s, f2s, ds))
        body = functools.partial(local_body, q, first, count)
        outs = [out(wide), out((q, SPAN, 2 * STATE))]
        local.append(call(body, outs, smem=1, name="local")(skip_gain, held[c][0], bcs, cums, a_cols))

    sent = [h[3] for h in held]
    arrived = [[] for _ in held]
    for t in range(planes - 1):
        for c in range(PARTS):
            if c == 1 and t == 0:
                sent[c] = behind(sent[c], ahead)
            came = ahead if c == t == 0 else hop(sent[c], t)
            if t == max(planes - 3, 0):
                came = behind(came, local[c])
            if c > 0 and t < planes - 2:
                came = behind(came, sent[c - 1])
            arrived[c].append(came)
            if t < planes - 2:
                (sent[c],) = call(
                    functools.partial(relay_body, q, t), [out(came.shape)], name="relay"
                )(came, held[c][2], held[c][4])

    before, gx_parts, returned = [], [], []
    for c, (first, width) in enumerate(spans):
        rows16, states = held[c][:2]
        block, all_blocks = (SPAN, 2 * STATE), (q, SPAN, 2 * STATE)
        outs = [out((SPAN, width))] * q + ([out(block)] * q if before else [out(all_blocks)])
        scratch = (pltpu.VMEM((q, SPAN, width), F32),)
        if before:
            scratch = (pltpu.VMEM(all_blocks, F32),) + scratch
        body = functools.partial(final_body, q, planes, slice(first, first + width), bool(before))
        done = call(body, outs, scratch, name="final")(
            *arrived[c], rows16, states, f1s, ds, bcs, *local[c], *before
        )
        gx_parts.append(list(done[:q]))
        before = list(done[q:])
        if c == 0:
            returned.append([swap(done[r], r) for r in range(1, q)])
            arrived[1][-1] = behind(arrived[1][-1], *returned[0])

    while bit > 1:
        bit //= 2
        order = list(sources)
        arrays = behind(tuple(sources[r][0] for r in order), before[0])
        body = functools.partial(deal_body, bit, [sources[r][1] for r in order])
        shape = (len(order) * bit, length, columns_each)
        (dealt,) = call(body, [out(shape)], name="deal")(*arrays)
        got = across(dealt, bit)
        for k, r in enumerate(order):
            sources[r ^ bit] = got, k * bit

    gp = before[0]
    for r in range(1, q):
        gp = gp + swap(before[r], r)
    returned.append([swap(behind(gx_parts[1][r], gp), r) for r in range(1, q)])
    grads = {0: behind(gp, *(v for v, _ in sources.values()))}
    bit = n_dp // 2
    while bit:
        for r in list(grads):
            grads[r ^ bit] = across(grads[r], bit)
        bit //= 2
    scale = 1.0 / (length * n_seq)
    arrays = list({id(v): v for v, _ in sources.values()}.values())
    places = [([v is a for a in arrays].index(True), at) for v, at in (sources[r] for r in range(n_dp))]
    args = arrays + [behind(grads[0], *returned[1])] + [grads[r] for r in range(1, n_dp)]
    scratch = (
        pltpu.VMEM((n_dp, SPAN, columns_each), BF16),
        pltpu.VMEM((n_dp, SPAN, 2 * STATE), BF16),
        pltpu.VMEM((n_seq, rows, 2 * STATE), F32),
    )
    body = functools.partial(weight_body, n_dp, n_seq, rows, scale, places)
    half = n_seq // 4
    far, far_sent, near, near_sent = call(body, [out((half, rows, 2 * STATE))] * 4, scratch, name="weight")(*args)
    far_in = swap(far_sent, 1)
    near_in = swap(behind(near_sent, far_sent), 1)
    far = far + far_in
    came = [swap(far[k], 2 * (half + k)) for k in range(half)]
    near = near + near_in
    came += [swap(near[k], 2 * k) for k in range(1, half)]
    grad_weight = near[0]
    for part in came:
        grad_weight = grad_weight + part

    body = functools.partial(assemble_body, q, group, spans)
    parts = [v for c in range(PARTS) for v in (gx_parts[c][0], *returned[c])]
    (grad_x,) = call(body, [[out((length, q * group), BF16)]], name="assemble")(*parts)
    return grad_x[None], grad_weight


def solution(mesh):
    return jax.shard_map(
        on_device,
        mesh=mesh,
        in_specs=(
            P("dp", "seq", None),
            P(),
            P("dp", "seq", None),
            P("dp", None, "seq"),
            P("dp", None, "seq"),
            P(),
            P("dp", "seq", None),
        ),
        out_specs=(P("dp", "seq", None), P(("dp", "seq"), None)),
        check_vma=False,
    )
```

```python
import functools

import jax
import jax.numpy as jnp
from jax import lax
from jax.experimental import pallas as pl
from jax.experimental.pallas import tpu as pltpu
from jax.sharding import PartitionSpec as P

HEADS = 32
HEAD_DIM = 64
STATE = 128
SPAN = 128
PARTS = 2
F32 = jnp.float32
BF16 = jnp.bfloat16
VMEM_LIMIT = 16 * 1024 * 1024


def group_size(n_seq):
    q = 1
    while n_seq % (4 * q) == 0 and HEADS // (2 * q) >= 4:
        q *= 2
    return q


def nn(a, b):
    return lax.dot_general(a, b, (((1,), (0,)), ((), ())), preferred_element_type=F32)


def nt(a, b):
    return lax.dot_general(a, b, (((1,), (1,)), ((), ())), preferred_element_type=F32)


def tn(a, b):
    return lax.dot_general(a, b, (((0,), (0,)), ((), ())), preferred_element_type=F32)


def terms(a):
    high = a.astype(BF16)
    rest = a - high.astype(F32)
    mid = rest.astype(BF16)
    return high, mid, (rest - mid.astype(F32)).astype(BF16)


def head_chunks(heads):
    first = 2 * (heads * 5 // 16)
    return [(0, first), (first, heads - first)]


def call(body, outs, scratch=(), name=None, smem=0, hbm=0):
    def run(*args):
        args = list(args)
        for k in range(smem, len(args)):
            if isinstance(args[k], list):
                args[k] = args[k][0]
            else:
                place = pltpu.HBM if k < smem + hbm else pltpu.VMEM
                args[k] = pltpu.with_memory_space_constraint(args[k], place)
        specs = [pl.BlockSpec(memory_space=pltpu.SMEM)] * smem
        specs += [pl.BlockSpec(memory_space=pltpu.HBM)] * hbm
        specs += [pl.BlockSpec(memory_space=pltpu.VMEM)] * (len(args) - smem - hbm)
        return pl.pallas_call(
            body,
            out_shape=tuple(o[0] if isinstance(o, list) else pltpu.VMEM(o.shape, o.dtype) for o in outs),
            in_specs=specs,
            out_specs=tuple(pl.BlockSpec(memory_space=pltpu.VMEM) for _ in outs),
            scratch_shapes=scratch,
            compiler_params=pltpu.CompilerParams(vmem_limit_bytes=VMEM_LIMIT),
            name=name,
        )(*args)

    return run


def loose(values):
    return [[value] for value in values]


def in_group(q):
    return lax.rem(lax.axis_index("seq"), q)


def out(shape, dtype=F32):
    return jax.ShapeDtypeStruct(shape, dtype)


def iotas():
    rows = lax.broadcasted_iota(jnp.int32, (SPAN, SPAN), 0)
    cols = lax.broadcasted_iota(jnp.int32, (SPAN, SPAN), 1)
    return rows, cols


def columns(ref, start, width):
    return ref[:, pl.ds(pl.multiple_of(start, 128), width)]


def pack_body(q, group, first, width, keep, x, g, *refs):
    packed, rest = refs[: q - 1], list(refs[q - 1 :])
    own = rest.pop(0) if keep else None
    stage, sems = rest
    y = in_group(q)
    copies = {}
    for r in range(1, q):
        at = pl.multiple_of(lax.bitwise_xor(y, r) * group + first, 128)
        for k, source in enumerate((x, g)):
            copies[r, k] = pltpu.make_async_copy(
                source.at[:, pl.ds(at, width)], stage.at[r - 1, k], sems.at[r, k]
            )
            copies[r, k].start()
    if keep:
        at = pl.multiple_of(y * group, 128)
        for k, source in enumerate((x, g)):
            copies[0, k] = pltpu.make_async_copy(source.at[:, pl.ds(at, group)], own.at[k], sems.at[0, k])
            copies[0, k].start()
    for r in range(1, q):
        for k in range(2):
            copies[r, k].wait()
            packed[r - 1][k] = stage[r - 1, k].astype(F32)
    if keep:
        for k in range(2):
            copies[0, k].wait()


def deal_body(bit, offsets, *refs):
    sent = refs[-1]
    for k, (ref, offset) in enumerate(zip(refs, offsets)):
        sent[k * bit : (k + 1) * bit] = ref[offset + bit : offset + 2 * bit]


def split_body(tokens, kept, dealt, held, sem):
    copy = pltpu.make_async_copy(tokens, held, sem)
    copy.start()
    copy.wait()
    half, _, each = kept.shape
    dp = lax.axis_index("dp")
    for r in range(2 * half):
        to, at = (kept, r) if r < half else (dealt, r - half)
        to[at] = columns(held, lax.bitwise_xor(dp, r) * each, each).astype(F32)


def project_body(q, tokens, weight, decay, step, *refs):
    bundles, (held_t, held_w, held_d, held_s, sems) = refs[:q], refs[q:]
    copies = [
        pltpu.make_async_copy(source, target, sems.at[k])
        for k, (source, target) in enumerate(
            ((tokens, held_t), (weight, held_w), (decay, held_d), (step, held_s))
        )
    ]
    for copy in copies:
        copy.start()
    for copy in copies:
        copy.wait()
    heads = HEADS // q
    y = in_group(q)
    proj = nn(held_t[...], held_w[...]).astype(BF16).astype(F32)
    for r in range(q):
        at = pl.multiple_of(lax.bitwise_xor(y, r) * heads, heads)
        bundles[r][:SPAN, :] = proj
        bundles[r][SPAN:, :SPAN] = held_d[pl.ds(at, heads), :]
        bundles[r][SPAN:, SPAN:] = held_s[pl.ds(at, heads), :]


def decays_body(q, heads, *refs):
    bundles = refs[:q]
    bcs, cums, a_cols, f1s, f2s, ds, steps = refs[q:]
    width = heads * HEAD_DIM
    y = in_group(q)
    for r in range(q):
        at = lax.bitwise_xor(y, r)
        bcs[at] = bundles[r][:SPAN, :].astype(BF16)
        cums[at] = bundles[r][SPAN:, :SPAN]
        steps[at] = bundles[r][SPAN:, SPAN:]
    rows, cols = iotas()
    tri = jnp.where(rows <= cols, 1.0, 0.0).astype(BF16)
    head_of = lax.broadcasted_iota(jnp.int32, (heads, width), 1) // HEAD_DIM
    spread = head_of == lax.broadcasted_iota(jnp.int32, (heads, width), 0)
    spread = jnp.where(spread, 1.0, 0.0).astype(BF16)
    for b in range(q):
        cum = sum(nn(term, tri) for term in terms(cums[b]))
        a = cum - jnp.log(steps[b])
        cums[b] = cum
        cum_c, a_c = cum.T, a.T
        a_cols[b] = a_c
        cum_x = sum(nn(term, spread) for term in terms(cum_c))
        a_x = sum(nn(term, spread) for term in terms(a_c))
        total = cum_x[SPAN - 1 : SPAN, :]
        f1s[b] = jnp.exp(total - a_x)
        f2s[b] = jnp.exp(cum_x)
        ds[b] = jnp.exp(total)


def states_body(q, planes, at, *refs):
    it = iter(refs)
    own = next(it)
    xg_in = [next(it) for _ in range(q - 1)]
    bcs, f1s, f2s, ds, rows16, states, totals, sent, plane = it
    y = in_group(q)
    for k in range(2):
        rows16[k, y] = own[k, :, at]
        for r in range(1, q):
            rows16[k, lax.bitwise_xor(y, r)] = xg_in[r - 1][k].astype(BF16)
    for b in range(q):
        rows16[2, b] = (rows16[0, b].astype(F32) * f1s[b, :, at]).astype(BF16)
        rows16[3, b] = (rows16[1, b].astype(F32) * f2s[b, :, at]).astype(BF16)
        states[0, b] = tn(bcs[b, :, :STATE], rows16[2, b])
        states[1, b] = tn(bcs[b, :, STATE:], rows16[3, b])
    forward, backward, through = states[0, 0], states[1, q - 1], ds[0, :, at]
    for b in range(1, q):
        forward = ds[b, :, at] * forward + states[0, b]
        backward = ds[q - 1 - b, :, at] * backward + states[1, q - 1 - b]
        through = through * ds[b, :, at]
    totals[0] = forward
    totals[1] = backward
    plane[...] = through
    sent[...] = jnp.where(lax.div(lax.axis_index("seq"), q) < planes // 2, forward, backward)


def relay_body(q, hop, came, totals, plane, sent):
    up = lax.div(lax.axis_index("seq"), q) == hop + 1
    sent[...] = jnp.where(up, totals[0], totals[1]) + plane[...] * came[...]


def local_body(q, first, hc, skip, rows16, bcs, cums, a_cols, gx, gp):
    rows, cols = iotas()
    causal = rows <= cols
    low = lax.broadcasted_iota(jnp.int32, (SPAN, 128), 1) < HEAD_DIM
    skip_at = in_group(q) * (HEADS // q) + first
    for b in range(q):
        b_cols, c_cols = bcs[b, :, :STATE], bcs[b, :, STATE:]
        kernel = nt(b_cols, c_cols)
        mixing = jnp.zeros((SPAN, SPAN), F32)
        for pair in range(hc // 2):
            at = slice(pair * 128, pair * 128 + 128)
            x, g = rows16[0, b, :, at], rows16[1, b, :, at]
            parts = []
            for half in range(2):
                h = first + 2 * pair + half
                gap = cums[b, h : h + 1, :] - a_cols[b, :, h : h + 1]
                decay = jnp.exp(jnp.where(causal, gap, -jnp.inf))
                picked = jnp.where(low if half == 0 else ~low, x, jnp.zeros_like(x))
                mixing += decay * nt(picked, g)
                parts.append(nn((decay * kernel).astype(BF16), g))
            gains = jnp.where(low, skip[skip_at + 2 * pair], skip[skip_at + 2 * pair + 1])
            gx[b, :, at] = jnp.where(low, parts[0], parts[1]) + gains * g.astype(F32)
        mixed = mixing.astype(BF16)
        gp[b, :, :STATE] = nn(mixed, c_cols)
        gp[b, :, STATE:] = tn(mixed, b_cols)


def final_body(q, planes, at, more, *refs):
    it = iter(refs)
    got = [next(it) for _ in range(planes - 1)]
    rows16, states, f1s, ds, bcs, gx, gp = [next(it) for _ in range(7)]
    before = next(it) if more else None
    gx_out = [next(it) for _ in range(q)]
    gp_sent = [next(it) for _ in range(q)] if more else []
    gp_out, gx_all = it
    y = in_group(q)
    z = lax.div(lax.axis_index("seq"), q)
    start = after = jnp.zeros(got[0].shape, F32)
    for t in range(planes - 1):
        came = got[t][...]
        start += jnp.where(z == t + 1, 1.0, 0.0) * came
        after += jnp.where(z == planes - 2 - t, 1.0, 0.0) * came
    for b in range(q):
        part = gp[b, :, STATE:] + nt(rows16[3, b], start.astype(BF16))
        gp_out[b, :, STATE:] = part if before is None else part + before[b, :, STATE:]
        if b < q - 1:
            start = ds[b, :, at] * start + states[0, b]
    for b in range(q - 1, -1, -1):
        rounded = after.astype(BF16)
        gx_all[b] = gx[b] + f1s[b, :, at] * nn(bcs[b, :, :STATE], rounded)
        part = gp[b, :, :STATE] + nt(rows16[2, b], rounded)
        gp_out[b, :, :STATE] = part if before is None else part + before[b, :, :STATE]
        if b > 0:
            after = ds[b, :, at] * after + states[1, b]
    for r in range(q):
        gx_out[r][...] = gx_all[lax.bitwise_xor(y, r)]
        if more:
            gp_sent[r][...] = gp_out[lax.bitwise_xor(y, r)]


def assemble_body(q, group, spans, *refs):
    parts, result = refs[:-1], refs[-1]
    y = in_group(q)
    for r in range(q):
        for c, (first, width) in enumerate(spans):
            at = pl.multiple_of(lax.bitwise_xor(y, r) * group + first, 128)
            result[:, pl.ds(at, width)] = parts[c * q + r][...].astype(BF16)


def weight_body(n_dp, n_seq, rows, scale, places, *refs):
    arrays = 1 + max(k for k, _ in places)
    tokens, grads, refs = refs[:arrays], refs[arrays : arrays + n_dp], refs[arrays + n_dp :]
    outs, (held, factors, products) = refs[:4], refs[4:]
    width = n_seq * rows
    half = n_seq // 4
    seq = lax.axis_index("seq")
    for r in range(n_dp):
        held[r] = tokens[places[r][0]][places[r][1]].astype(BF16)
        factors[r] = grads[r][...].astype(BF16)
    total = tn(held[...].reshape(n_dp * SPAN, width), factors[...].reshape(n_dp * SPAN, 2 * STATE))
    products[...] = (total * scale).reshape(n_seq, rows, 2 * STATE)
    for k in range(2 * half):
        near, at = 1 - k // half, k % half
        for other in range(2):
            outs[2 * near + other][at] = products[lax.bitwise_xor(seq, 2 * k + other)]


def behind(value, *others):
    return lax.optimization_barrier((value,) + others)[0]


def on_device(layer_input, proj_weight, inputs, step_size, log_decay, skip_gain, grad_out):
    n_seq, n_dp = lax.axis_size("seq"), lax.axis_size("dp")
    q = group_size(n_seq)
    planes = n_seq // q
    heads = HEADS // q
    group = heads * HEAD_DIM
    chunks = head_chunks(heads)
    spans = [(first * HEAD_DIM, count * HEAD_DIM) for first, count in chunks]
    tokens, x, g = layer_input[0], inputs[0], grad_out[0]
    length, features = tokens.shape
    seq = lax.axis_index("seq")

    def swap(value, r):
        return lax.ppermute(value, "seq", [(i, i ^ r) for i in range(n_seq)])

    def across(value, r):
        return lax.ppermute(value, "dp", [(i, i ^ r) for i in range(n_dp)])

    columns_each = features // n_dp
    rows = columns_each // n_seq

    def pack(first, width, keep):
        scratch = (pltpu.VMEM((q - 1, 2, SPAN, width), BF16), pltpu.SemaphoreType.DMA((q, 2)))
        outs = [out((2, SPAN, width))] * (q - 1) + [out((2, SPAN, group), BF16)] * keep
        body = functools.partial(pack_body, q, group, first, width, keep)
        return call(body, outs, scratch, name="pack", hbm=2)(x, g)

    packed = pack(*spans[0], False)
    xg_in = [[swap(packed[r - 1], r) for r in range(1, q)]]
    scratch = (
        pltpu.VMEM(tokens.shape, BF16), pltpu.VMEM(proj_weight.shape, BF16),
        pltpu.VMEM((HEADS, SPAN), F32), pltpu.VMEM((HEADS, SPAN), F32), pltpu.SemaphoreType.DMA((4,)),
    )
    outs = [out((SPAN + heads, 2 * STATE))] * q
    opened = call(functools.partial(project_body, q), outs, scratch, name="project", hbm=4)(
        behind(tokens, packed[0]), proj_weight, log_decay[0], step_size[0]
    )
    bundles = [opened[0]] + [swap(opened[r], r) for r in range(1, q)]
    packed = pack(*spans[1], True)
    own = packed[q - 1]
    xg_in.append([swap(behind(packed[r - 1], opened[0]), r) for r in range(1, q)])
    bit = n_dp // 2
    rows_of = (q, SPAN, group)
    outs = [
        out((q, SPAN, 2 * STATE), BF16), out((q, heads, SPAN)), out((q, SPAN, heads)),
        out(rows_of), out(rows_of), out((q, 1, group)),
    ]
    body = functools.partial(decays_body, q, heads)
    bcs, cums, a_cols, f1s, f2s, ds = call(body, outs, (pltpu.VMEM((q, heads, SPAN), F32),), name="decays")(
        *bundles
    )

    def hop(value, t):
        top = planes - 1 - t
        pairs = [(t * q + i, (t + 1) * q + i) for i in range(q)]
        pairs += [(top * q + i, (top - 1) * q + i) for i in range(q)]
        return lax.ppermute(value, "seq", pairs)

    held, local = [], []
    for c, (first, count) in enumerate(chunks):
        wide = (q, SPAN, count * HEAD_DIM)
        state = out((STATE, wide[2]))
        at = slice(first * HEAD_DIM, (first + count) * HEAD_DIM)
        if c > 0:
            ahead = hop(held[0][3], 0)
            xg_in[c] = [behind(v, *local[0]) for v in xg_in[c]]
        outs = [out((4,) + wide, BF16), out((2,) + wide), out((2, STATE, wide[2])), state, out((1, wide[2]))]
        body = functools.partial(states_body, q, planes, at)
        held.append(call(body, outs, name="states")(own, *xg_in[c], bcs, f1s, f2s, ds))
        body = functools.partial(local_body, q, first, count)
        outs = [out(wide), out((q, SPAN, 2 * STATE))]
        local.append(call(body, outs, smem=1, name="local")(skip_gain, held[c][0], bcs, cums, a_cols))

    outs = [out((bit, length, columns_each))] * 2
    scratch = (pltpu.VMEM(tokens.shape, BF16), pltpu.SemaphoreType.DMA)
    kept, dealt = call(split_body, outs, scratch, name="split", hbm=1)(behind(tokens, ahead, held[1][3]))
    sources = {0: (kept, 0), bit: (across(dealt, bit), 0)}

    sent = [h[3] for h in held]
    arrived = [[] for _ in held]
    for t in range(planes - 1):
        for c in range(PARTS):
            if c == 1 and t == 0:
                sent[c] = behind(sent[c], ahead)
            came = ahead if c == t == 0 else hop(sent[c], t)
            if t == max(planes - 3, 0):
                came = behind(came, local[c])
            if c > 0 and t < planes - 2:
                came = behind(came, sent[c - 1])
            arrived[c].append(came)
            if t < planes - 2:
                (sent[c],) = call(
                    functools.partial(relay_body, q, t), [out(came.shape)], name="relay"
                )(came, held[c][2], held[c][4])

    before, gx_parts, returned = [], [], []
    for c, (first, width) in enumerate(spans):
        rows16, states = held[c][:2]
        block, all_blocks = (SPAN, 2 * STATE), (q, SPAN, 2 * STATE)
        outs = [out((SPAN, width))] * q + ([out(block)] * q if before else [out(all_blocks)])
        scratch = (pltpu.VMEM((q, SPAN, width), F32),)
        if before:
            scratch = (pltpu.VMEM(all_blocks, F32),) + scratch
        body = functools.partial(final_body, q, planes, slice(first, first + width), bool(before))
        done = call(body, outs, scratch, name="final")(
            *arrived[c], rows16, states, f1s, ds, bcs, *local[c], *before
        )
        gx_parts.append(list(done[:q]))
        before = list(done[q:])
        if c == 0:
            returned.append([swap(done[r], r) for r in range(1, q)])
            arrived[1][-1] = behind(arrived[1][-1], *returned[0])

    gp = before[0]
    for r in range(1, q):
        gp = gp + swap(before[r], r)
    while bit > 1:
        bit //= 2
        order = list(sources)
        arrays = behind(tuple(sources[r][0] for r in order), gp)
        body = functools.partial(deal_body, bit, [sources[r][1] for r in order])
        shape = (len(order) * bit, length, columns_each)
        (dealt,) = call(body, [out(shape)], name="deal")(*arrays)
        got = across(dealt, bit)
        for k, r in enumerate(order):
            sources[r ^ bit] = got, k * bit

    returned.append([swap(behind(gx_parts[1][r], gp), r) for r in range(1, q)])
    grads = {0: gp}
    bit = n_dp // 2
    while bit:
        for r in list(grads):
            grads[r ^ bit] = across(grads[r], bit)
        bit //= 2
    scale = 1.0 / (length * n_seq)
    arrays = list({id(v): v for v, _ in sources.values()}.values())
    places = [([v is a for a in arrays].index(True), at) for v, at in (sources[r] for r in range(n_dp))]
    args = arrays + [behind(grads[0], *returned[1])] + [grads[r] for r in range(1, n_dp)]
    scratch = (
        pltpu.VMEM((n_dp, SPAN, columns_each), BF16),
        pltpu.VMEM((n_dp, SPAN, 2 * STATE), BF16),
        pltpu.VMEM((n_seq, rows, 2 * STATE), F32),
    )
    body = functools.partial(weight_body, n_dp, n_seq, rows, scale, places)
    half = n_seq // 4
    far, far_sent, near, near_sent = call(body, [out((half, rows, 2 * STATE))] * 4, scratch, name="weight")(*args)
    far_in = swap(far_sent, 1)
    near_in = swap(behind(near_sent, far_in), 1)
    far = far + far_in
    came = [swap(far[k], 2 * (half + k)) for k in range(half)]
    near = near + near_in
    came += [swap(near[k], 2 * k) for k in range(1, half)]
    grad_weight = near[0]
    for part in came:
        grad_weight = grad_weight + part

    body = functools.partial(assemble_body, q, group, spans)
    parts = [v for c in range(PARTS) for v in (gx_parts[c][0], *returned[c])]
    (grad_x,) = call(body, [[out((length, q * group), BF16)]], name="assemble")(*parts)
    return grad_x[None], grad_weight


def solution(mesh):
    return jax.shard_map(
        on_device,
        mesh=mesh,
        in_specs=(
            P("dp", "seq", None),
            P(),
            P("dp", "seq", None),
            P("dp", None, "seq"),
            P("dp", None, "seq"),
            P(),
            P("dp", "seq", None),
        ),
        out_specs=(P("dp", "seq", None), P(("dp", "seq"), None)),
        check_vma=False,
    )
```

```python
import functools

import jax
import jax.numpy as jnp
from jax import lax
from jax.experimental import pallas as pl
from jax.experimental.pallas import tpu as pltpu
from jax.sharding import PartitionSpec as P

HEADS = 32
HEAD_DIM = 64
STATE = 128
SPAN = 128
F32 = jnp.float32
BF16 = jnp.bfloat16
VMEM_LIMIT = 16 * 1024 * 1024


def group_size(n_seq):
    q = 1
    while n_seq % (4 * q) == 0 and HEADS // (2 * q) >= 4:
        q *= 2
    return q


def nn(a, b):
    return lax.dot_general(a, b, (((1,), (0,)), ((), ())), preferred_element_type=F32)


def nt(a, b):
    return lax.dot_general(a, b, (((1,), (1,)), ((), ())), preferred_element_type=F32)


def tn(a, b):
    return lax.dot_general(a, b, (((0,), (0,)), ((), ())), preferred_element_type=F32)


def terms(a):
    high = a.astype(BF16)
    rest = a - high.astype(F32)
    mid = rest.astype(BF16)
    return high, mid, (rest - mid.astype(F32)).astype(BF16)


def call(body, outs, scratch=(), name=None, smem=0, hbm=0):
    def run(*args):
        args = list(args)
        for k in range(smem, len(args)):
            if isinstance(args[k], list):
                args[k] = args[k][0]
            else:
                place = pltpu.HBM if k < smem + hbm else pltpu.VMEM
                args[k] = pltpu.with_memory_space_constraint(args[k], place)
        specs = [pl.BlockSpec(memory_space=pltpu.SMEM)] * smem
        specs += [pl.BlockSpec(memory_space=pltpu.HBM)] * hbm
        specs += [pl.BlockSpec(memory_space=pltpu.VMEM)] * (len(args) - smem - hbm)
        return pl.pallas_call(
            body,
            out_shape=tuple(o[0] if isinstance(o, list) else pltpu.VMEM(o.shape, o.dtype) for o in outs),
            in_specs=specs,
            out_specs=tuple(pl.BlockSpec(memory_space=pltpu.VMEM) for _ in outs),
            scratch_shapes=scratch,
            compiler_params=pltpu.CompilerParams(vmem_limit_bytes=VMEM_LIMIT),
            name=name,
        )(*args)

    return run


def loose(values):
    return [[value] for value in values]


def in_group(q):
    return lax.rem(lax.axis_index("seq"), q)


def out(shape, dtype=F32):
    return jax.ShapeDtypeStruct(shape, dtype)


def iotas():
    rows = lax.broadcasted_iota(jnp.int32, (SPAN, SPAN), 0)
    cols = lax.broadcasted_iota(jnp.int32, (SPAN, SPAN), 1)
    return rows, cols


def columns(ref, start, width):
    return ref[:, pl.ds(pl.multiple_of(start, 128), width)]


def pack_body(q, group, x, g, *refs):
    packed, own, (stage, sems) = refs[: q - 1], refs[q - 1], refs[q:]
    y = in_group(q)
    copies = {}
    for r in range(1, q):
        at = pl.multiple_of(lax.bitwise_xor(y, r) * group, 128)
        for k, source in enumerate((x, g)):
            copies[r, k] = pltpu.make_async_copy(
                source.at[:, pl.ds(at, group)], stage.at[r - 1, k], sems.at[r, k]
            )
            copies[r, k].start()
    at = pl.multiple_of(y * group, 128)
    for k, source in enumerate((x, g)):
        copies[0, k] = pltpu.make_async_copy(source.at[:, pl.ds(at, group)], own.at[k], sems.at[0, k])
        copies[0, k].start()
    for r in range(1, q):
        for k in range(2):
            copies[r, k].wait()
            packed[r - 1][k] = stage[r - 1, k].astype(F32)
    for k in range(2):
        copies[0, k].wait()


def deal_body(bit, offsets, *refs):
    sent = refs[-1]
    for k, (ref, offset) in enumerate(zip(refs, offsets)):
        sent[k * bit : (k + 1) * bit] = ref[offset + bit : offset + 2 * bit]


def split_body(tokens, kept, dealt, held, sem):
    copy = pltpu.make_async_copy(tokens, held, sem)
    copy.start()
    copy.wait()
    half, _, each = kept.shape
    dp = lax.axis_index("dp")
    for r in range(2 * half):
        to, at = (kept, r) if r < half else (dealt, r - half)
        to[at] = columns(held, lax.bitwise_xor(dp, r) * each, each).astype(F32)


def project_body(q, tokens, weight, decay, step, *refs):
    bundles, (held_t, held_w, held_d, held_s, sems) = refs[:q], refs[q:]
    copies = [
        pltpu.make_async_copy(source, target, sems.at[k])
        for k, (source, target) in enumerate(
            ((tokens, held_t), (weight, held_w), (decay, held_d), (step, held_s))
        )
    ]
    for copy in copies:
        copy.start()
    for copy in copies:
        copy.wait()
    heads = HEADS // q
    y = in_group(q)
    proj = nn(held_t[...], held_w[...]).astype(BF16).astype(F32)
    for r in range(q):
        at = pl.multiple_of(lax.bitwise_xor(y, r) * heads, heads)
        bundles[r][:SPAN, :] = proj
        bundles[r][SPAN:, :SPAN] = held_d[pl.ds(at, heads), :]
        bundles[r][SPAN:, SPAN:] = held_s[pl.ds(at, heads), :]


def decays_body(q, heads, *refs):
    bundles = refs[:q]
    bcs, cums, a_cols, f1s, f2s, ds, steps = refs[q:]
    width = heads * HEAD_DIM
    y = in_group(q)
    for r in range(q):
        at = lax.bitwise_xor(y, r)
        bcs[at] = bundles[r][:SPAN, :].astype(BF16)
        cums[at] = bundles[r][SPAN:, :SPAN]
        steps[at] = bundles[r][SPAN:, SPAN:]
    rows, cols = iotas()
    tri = jnp.where(rows <= cols, 1.0, 0.0).astype(BF16)
    head_of = lax.broadcasted_iota(jnp.int32, (heads, width), 1) // HEAD_DIM
    spread = head_of == lax.broadcasted_iota(jnp.int32, (heads, width), 0)
    spread = jnp.where(spread, 1.0, 0.0).astype(BF16)
    for b in range(q):
        cum = sum(nn(term, tri) for term in terms(cums[b]))
        a = cum - jnp.log(steps[b])
        cums[b] = cum
        cum_c, a_c = cum.T, a.T
        a_cols[b] = a_c
        cum_x = sum(nn(term, spread) for term in terms(cum_c))
        a_x = sum(nn(term, spread) for term in terms(a_c))
        total = cum_x[SPAN - 1 : SPAN, :]
        f1s[b] = jnp.exp(total - a_x)
        f2s[b] = jnp.exp(cum_x)
        ds[b] = jnp.exp(total)


def states_body(q, planes, *refs):
    it = iter(refs)
    own = next(it)
    xg_in = [next(it) for _ in range(q - 1)]
    bcs, f1s, f2s, ds, rows16, states, totals, sent, plane = it
    y = in_group(q)
    for k in range(2):
        rows16[k, y] = own[k]
        for r in range(1, q):
            rows16[k, lax.bitwise_xor(y, r)] = xg_in[r - 1][k].astype(BF16)
    for b in range(q):
        rows16[2, b] = (rows16[0, b].astype(F32) * f1s[b]).astype(BF16)
        rows16[3, b] = (rows16[1, b].astype(F32) * f2s[b]).astype(BF16)
        states[0, b] = tn(bcs[b, :, :STATE], rows16[2, b])
        states[1, b] = tn(bcs[b, :, STATE:], rows16[3, b])
    forward, backward, through = states[0, 0], states[1, q - 1], ds[0]
    for b in range(1, q):
        forward = ds[b] * forward + states[0, b]
        backward = ds[q - 1 - b] * backward + states[1, q - 1 - b]
        through = through * ds[b]
    totals[0] = forward
    totals[1] = backward
    plane[...] = through
    sent[...] = jnp.where(lax.div(lax.axis_index("seq"), q) < planes // 2, forward, backward)


def relay_body(q, hop, came, totals, plane, sent):
    up = lax.div(lax.axis_index("seq"), q) == hop + 1
    sent[...] = jnp.where(up, totals[0], totals[1]) + plane[...] * came[...]


def local_body(q, hc, skip, rows16, bcs, cums, a_cols, gx, gp):
    rows, cols = iotas()
    causal = rows <= cols
    low = lax.broadcasted_iota(jnp.int32, (SPAN, 128), 1) < HEAD_DIM
    skip_at = in_group(q) * hc
    for b in range(q):
        b_cols, c_cols = bcs[b, :, :STATE], bcs[b, :, STATE:]
        kernel = nt(b_cols, c_cols)
        mixing = jnp.zeros((SPAN, SPAN), F32)
        for pair in range(hc // 2):
            at = slice(pair * 128, pair * 128 + 128)
            x, g = rows16[0, b, :, at], rows16[1, b, :, at]
            parts = []
            for half in range(2):
                h = 2 * pair + half
                gap = cums[b, h : h + 1, :] - a_cols[b, :, h : h + 1]
                decay = jnp.exp(jnp.where(causal, gap, -jnp.inf))
                picked = jnp.where(low if half == 0 else ~low, x, jnp.zeros_like(x))
                mixing += decay * nt(picked, g)
                parts.append(nn((decay * kernel).astype(BF16), g))
            gains = jnp.where(low, skip[skip_at + 2 * pair], skip[skip_at + 2 * pair + 1])
            gx[b, :, at] = jnp.where(low, parts[0], parts[1]) + gains * g.astype(F32)
        mixed = mixing.astype(BF16)
        gp[b, :, :STATE] = nn(mixed, c_cols)
        gp[b, :, STATE:] = tn(mixed, b_cols)


def final_body(q, planes, *refs):
    it = iter(refs)
    got = [next(it) for _ in range(planes - 1)]
    rows16, states, f1s, ds, bcs, gx, gp = [next(it) for _ in range(7)]
    gx_out = [next(it) for _ in range(q)]
    gp_sent = [next(it) for _ in range(q)]
    gp_out, gx_all = it
    y = in_group(q)
    z = lax.div(lax.axis_index("seq"), q)
    start = after = jnp.zeros(got[0].shape, F32)
    for t in range(planes - 1):
        came = got[t][...]
        start += jnp.where(z == t + 1, 1.0, 0.0) * came
        after += jnp.where(z == planes - 2 - t, 1.0, 0.0) * came
    for b in range(q):
        part = gp[b, :, STATE:] + nt(rows16[3, b], start.astype(BF16))
        gp_out[b, :, STATE:] = part
        if b < q - 1:
            start = ds[b] * start + states[0, b]
    for b in range(q - 1, -1, -1):
        rounded = after.astype(BF16)
        gx_all[b] = gx[b] + f1s[b] * nn(bcs[b, :, :STATE], rounded)
        part = gp[b, :, :STATE] + nt(rows16[2, b], rounded)
        gp_out[b, :, :STATE] = part
        if b > 0:
            after = ds[b] * after + states[1, b]
    for r in range(q):
        gx_out[r][...] = gx_all[lax.bitwise_xor(y, r)]
        gp_sent[r][...] = gp_out[lax.bitwise_xor(y, r)]


def assemble_body(q, group, *refs):
    parts, result = refs[:-1], refs[-1]
    y = in_group(q)
    for r in range(q):
        at = pl.multiple_of(lax.bitwise_xor(y, r) * group, 128)
        result[:, pl.ds(at, group)] = parts[r][...].astype(BF16)


def weight_body(n_dp, n_seq, rows, scale, places, *refs):
    arrays = 1 + max(k for k, _ in places)
    tokens, grads, refs = refs[:arrays], refs[arrays : arrays + n_dp], refs[arrays + n_dp :]
    outs, (held, factors, products) = refs[:4], refs[4:]
    width = n_seq * rows
    half = n_seq // 4
    seq = lax.axis_index("seq")
    for r in range(n_dp):
        held[r] = tokens[places[r][0]][places[r][1]].astype(BF16)
        factors[r] = grads[r][...].astype(BF16)
    total = tn(held[...].reshape(n_dp * SPAN, width), factors[...].reshape(n_dp * SPAN, 2 * STATE))
    products[...] = (total * scale).reshape(n_seq, rows, 2 * STATE)
    for k in range(2 * half):
        near, at = 1 - k // half, k % half
        for other in range(2):
            outs[2 * near + other][at] = products[lax.bitwise_xor(seq, 2 * k + other)]


def behind(value, *others):
    return lax.optimization_barrier((value,) + others)[0]


def on_device(layer_input, proj_weight, inputs, step_size, log_decay, skip_gain, grad_out):
    n_seq, n_dp = lax.axis_size("seq"), lax.axis_size("dp")
    q = group_size(n_seq)
    planes = n_seq // q
    heads = HEADS // q
    group = heads * HEAD_DIM
    tokens, x, g = layer_input[0], inputs[0], grad_out[0]
    length, features = tokens.shape
    seq = lax.axis_index("seq")

    def swap(value, r):
        return lax.ppermute(value, "seq", [(i, i ^ r) for i in range(n_seq)])

    def across(value, r):
        return lax.ppermute(value, "dp", [(i, i ^ r) for i in range(n_dp)])

    columns_each = features // n_dp
    rows = columns_each // n_seq

    scratch = (pltpu.VMEM((q - 1, 2, SPAN, group), BF16), pltpu.SemaphoreType.DMA((q, 2)))
    outs = [out((2, SPAN, group))] * (q - 1) + [out((2, SPAN, group), BF16)]
    packed = call(functools.partial(pack_body, q, group), outs, scratch, name="pack", hbm=2)(x, g)
    own = packed[q - 1]
    xg_in = [swap(packed[r - 1], r) for r in range(1, q)]
    scratch = (
        pltpu.VMEM(tokens.shape, BF16), pltpu.VMEM(proj_weight.shape, BF16),
        pltpu.VMEM((HEADS, SPAN), F32), pltpu.VMEM((HEADS, SPAN), F32), pltpu.SemaphoreType.DMA((4,)),
    )
    outs = [out((SPAN + heads, 2 * STATE))] * q
    opened = call(functools.partial(project_body, q), outs, scratch, name="project", hbm=4)(
        behind(tokens, packed[0]), proj_weight, log_decay[0], step_size[0]
    )
    bundles = [opened[0]] + [swap(opened[r], r) for r in range(1, q)]
    bit = n_dp // 2
    rows_of = (q, SPAN, group)
    outs = [
        out((q, SPAN, 2 * STATE), BF16), out((q, heads, SPAN)), out((q, SPAN, heads)),
        out(rows_of), out(rows_of), out((q, 1, group)),
    ]
    body = functools.partial(decays_body, q, heads)
    bcs, cums, a_cols, f1s, f2s, ds = call(body, outs, (pltpu.VMEM((q, heads, SPAN), F32),), name="decays")(
        *bundles
    )

    def hop(value, t):
        top = planes - 1 - t
        pairs = [(t * q + i, (t + 1) * q + i) for i in range(q)]
        pairs += [(top * q + i, (top - 1) * q + i) for i in range(q)]
        return lax.ppermute(value, "seq", pairs)

    state = (STATE, group)
    outs = [out((4,) + rows_of, BF16), out((2,) + rows_of), out((2,) + state), out(state), out((1, group))]
    body = functools.partial(states_body, q, planes)
    rows16, states, totals, sent, through = call(body, outs, name="states")(own, *xg_in, bcs, f1s, f2s, ds)
    arrived = []
    for t in range(planes - 1):
        arrived.append(hop(sent, t))
        if t < planes - 2:
            body = functools.partial(relay_body, q, t)
            (sent,) = call(body, [out(state)], name="relay")(arrived[t], totals, through)
    body = functools.partial(local_body, q, heads)
    outs = [out(rows_of), out((q, SPAN, 2 * STATE))]
    local = call(body, outs, smem=1, name="local")(skip_gain, rows16, bcs, cums, a_cols)

    outs = [out((bit, length, columns_each))] * 2
    scratch = (pltpu.VMEM(tokens.shape, BF16), pltpu.SemaphoreType.DMA)
    kept, dealt = call(split_body, outs, scratch, name="split", hbm=1)(behind(tokens, bcs))
    sources = {0: (kept, 0), bit: (across(dealt, bit), 0)}

    all_blocks = (q, SPAN, 2 * STATE)
    outs = [out((SPAN, group))] * q + [out(all_blocks[1:])] * q
    scratch = (pltpu.VMEM(all_blocks, F32), pltpu.VMEM(rows_of, F32))
    body = functools.partial(final_body, q, planes)
    done = call(body, outs, scratch, name="final")(*arrived, rows16, states, f1s, ds, bcs, *local)
    gx_parts, before = done[:q], done[q:]

    gp = before[0]
    for r in range(1, q):
        gp = gp + swap(before[r], r)
    while bit > 1:
        bit //= 2
        order = list(sources)
        arrays = behind(tuple(sources[r][0] for r in order), gp)
        body = functools.partial(deal_body, bit, [sources[r][1] for r in order])
        shape = (len(order) * bit, length, columns_each)
        (dealt,) = call(body, [out(shape)], name="deal")(*arrays)
        got = across(dealt, bit)
        for k, r in enumerate(order):
            sources[r ^ bit] = got, k * bit

    returned = [swap(gx_parts[r], r) for r in range(1, q)]
    grads = {0: gp}
    bit = n_dp // 2
    while bit:
        for r in list(grads):
            grads[r ^ bit] = across(grads[r], bit)
        bit //= 2
    scale = 1.0 / (length * n_seq)
    arrays = list({id(v): v for v, _ in sources.values()}.values())
    places = [([v is a for a in arrays].index(True), at) for v, at in (sources[r] for r in range(n_dp))]
    args = arrays + [behind(grads[0], *returned)] + [grads[r] for r in range(1, n_dp)]
    scratch = (
        pltpu.VMEM((n_dp, SPAN, columns_each), BF16),
        pltpu.VMEM((n_dp, SPAN, 2 * STATE), BF16),
        pltpu.VMEM((n_seq, rows, 2 * STATE), F32),
    )
    body = functools.partial(weight_body, n_dp, n_seq, rows, scale, places)
    half = n_seq // 4
    far, far_sent, near, near_sent = call(body, [out((half, rows, 2 * STATE))] * 4, scratch, name="weight")(*args)
    far_in = swap(far_sent, 1)
    near_in = swap(behind(near_sent, far_in), 1)
    far = far + far_in
    came = [swap(far[k], 2 * (half + k)) for k in range(half)]
    near = near + near_in
    came += [swap(near[k], 2 * k) for k in range(1, half)]
    grad_weight = near[0]
    for part in came:
        grad_weight = grad_weight + part

    body = functools.partial(assemble_body, q, group)
    parts = [gx_parts[0], *returned]
    (grad_x,) = call(body, [[out((length, q * group), BF16)]], name="assemble")(*parts)
    return grad_x[None], grad_weight


def solution(mesh):
    return jax.shard_map(
        on_device,
        mesh=mesh,
        in_specs=(
            P("dp", "seq", None),
            P(),
            P("dp", "seq", None),
            P("dp", None, "seq"),
            P("dp", None, "seq"),
            P(),
            P("dp", "seq", None),
        ),
        out_specs=(P("dp", "seq", None), P(("dp", "seq"), None)),
        check_vma=False,
    )
```

```python
import functools

import jax
import jax.numpy as jnp
from jax import lax
from jax.experimental import pallas as pl
from jax.experimental.pallas import tpu as pltpu
from jax.sharding import PartitionSpec as P

HEADS = 32
HEAD_DIM = 64
STATE = 128
SPAN = 128
PARTS = 2
F32 = jnp.float32
BF16 = jnp.bfloat16
VMEM_LIMIT = 16 * 1024 * 1024


def group_size(n_seq):
    q = 1
    while n_seq % (2 * q) == 0 and 4 * q * q <= n_seq:
        q *= 2
    return q


def nn(a, b):
    return lax.dot_general(a, b, (((1,), (0,)), ((), ())), preferred_element_type=F32)


def nt(a, b):
    return lax.dot_general(a, b, (((1,), (1,)), ((), ())), preferred_element_type=F32)


def tn(a, b):
    return lax.dot_general(a, b, (((0,), (0,)), ((), ())), preferred_element_type=F32)


def terms(a):
    high = a.astype(BF16)
    rest = a - high.astype(F32)
    mid = rest.astype(BF16)
    return high, mid, (rest - mid.astype(F32)).astype(BF16)


def head_chunks(heads):
    first = 2 * (heads * 5 // 16)
    return [(0, first), (first, heads - first)]


def call(body, outs, scratch=(), name=None, smem=0, hbm=0):
    def run(*args):
        args = list(args)
        for k in range(smem, len(args)):
            if isinstance(args[k], list):
                args[k] = args[k][0]
            else:
                place = pltpu.HBM if k < smem + hbm else pltpu.VMEM
                args[k] = pltpu.with_memory_space_constraint(args[k], place)
        specs = [pl.BlockSpec(memory_space=pltpu.SMEM)] * smem
        specs += [pl.BlockSpec(memory_space=pltpu.HBM)] * hbm
        specs += [pl.BlockSpec(memory_space=pltpu.VMEM)] * (len(args) - smem - hbm)
        return pl.pallas_call(
            body,
            out_shape=tuple(o[0] if isinstance(o, list) else pltpu.VMEM(o.shape, o.dtype) for o in outs),
            in_specs=specs,
            out_specs=tuple(pl.BlockSpec(memory_space=pltpu.VMEM) for _ in outs),
            scratch_shapes=scratch,
            compiler_params=pltpu.CompilerParams(vmem_limit_bytes=VMEM_LIMIT),
            name=name,
        )(*args)

    return run


def loose(values):
    return [[value] for value in values]


def in_group(q):
    return lax.rem(lax.axis_index("seq"), q)


def out(shape, dtype=F32):
    return jax.ShapeDtypeStruct(shape, dtype)


def iotas():
    rows = lax.broadcasted_iota(jnp.int32, (SPAN, SPAN), 0)
    cols = lax.broadcasted_iota(jnp.int32, (SPAN, SPAN), 1)
    return rows, cols


def columns(ref, start, width):
    return ref[:, pl.ds(pl.multiple_of(start, 128), width)]


def pack_body(q, group, first, width, keep, x, g, *refs):
    packed, rest = refs[: q - 1], list(refs[q - 1 :])
    own = rest.pop(0) if keep else None
    stage, sems = rest
    y = in_group(q)
    copies = {}
    for r in range(1, q):
        at = pl.multiple_of(lax.rem(y + r, q) * group + first, 128)
        for k, source in enumerate((x, g)):
            copies[r, k] = pltpu.make_async_copy(
                source.at[:, pl.ds(at, width)], stage.at[r - 1, k], sems.at[r, k]
            )
            copies[r, k].start()
    if keep:
        at = pl.multiple_of(y * group, 128)
        for k, source in enumerate((x, g)):
            copies[0, k] = pltpu.make_async_copy(source.at[:, pl.ds(at, group)], own.at[k], sems.at[0, k])
            copies[0, k].start()
    for r in range(1, q):
        for k in range(2):
            copies[r, k].wait()
            packed[r - 1][k] = stage[r - 1, k].astype(F32)
    if keep:
        for k in range(2):
            copies[0, k].wait()


def deal_body(rows, q, planes, tokens, *outs):
    n_dp = len(outs)
    each = q * planes * rows
    dp = lax.axis_index("dp")
    for r in range(n_dp - 1, -1, -1):
        cut = columns(tokens, lax.bitwise_xor(dp, r) * each, each).astype(F32)
        for k in range(q * planes):
            at = (k % planes * q + k // planes) * rows
            outs[r][:, k * rows : (k + 1) * rows] = cut[:, at : at + rows]


def hand_body(q, part, *refs):
    tokens, outs = refs[: 1 - q], refs[1 - q :]
    y = in_group(q)
    for r in range(1, q):
        for k, ref in enumerate(tokens):
            outs[r - 1][k] = columns(ref, lax.rem(y + r, q) * part, part)


def project_body(q, tokens, weight, decay, step, *bundles):
    proj = nn(tokens[...], weight[...]).astype(BF16).astype(F32)
    heads = HEADS // q
    y = in_group(q)
    for r in range(q):
        at = pl.multiple_of(lax.rem(y + r, q) * heads, heads)
        bundles[r][:SPAN, :] = proj
        bundles[r][SPAN:, :SPAN] = decay[pl.ds(at, heads), :]
        bundles[r][SPAN:, SPAN:] = step[pl.ds(at, heads), :]


def states_body(q, planes, first, hc, *refs):
    it = iter(refs)
    own = next(it)
    xg_in = [next(it) for _ in range(q - 1)]
    bundles = [next(it) for _ in range(q)]
    rows16, states, f1s, ds, totals, sent, plane, bcs, cums, a_cols, steps = it
    width = hc * HEAD_DIM
    y = in_group(q)
    for k in range(2):
        rows16[k, y] = own[k, :, first * HEAD_DIM : first * HEAD_DIM + width]
    low = SPAN + first
    for r in range(q):
        block = lax.rem(y - r + q, q)
        if r > 0:
            for k in range(2):
                rows16[k, block] = xg_in[r - 1][k].astype(BF16)
        bcs[block] = bundles[r][:SPAN, :].astype(BF16)
        cums[block] = bundles[r][low : low + hc, :SPAN]
        steps[block] = bundles[r][low : low + hc, SPAN:]
    rows, cols = iotas()
    tri = jnp.where(rows <= cols, 1.0, 0.0).astype(BF16)
    head_of = lax.broadcasted_iota(jnp.int32, (hc, width), 1) // HEAD_DIM
    spread = head_of == lax.broadcasted_iota(jnp.int32, (hc, width), 0)
    spread = jnp.where(spread, 1.0, 0.0).astype(BF16)
    for b in range(q):
        cum = sum(nn(term, tri) for term in terms(cums[b]))
        a = cum - jnp.log(steps[b])
        cums[b] = cum
        cum_c, a_c = cum.T, a.T
        a_cols[b] = a_c
        cum_x = sum(nn(term, spread) for term in terms(cum_c))
        a_x = sum(nn(term, spread) for term in terms(a_c))
        total = cum_x[SPAN - 1 : SPAN, :]
        f1 = jnp.exp(total - a_x)
        f1s[b] = f1
        ds[b] = jnp.exp(total)
        weighted = (rows16[0, b].astype(F32) * f1).astype(BF16)
        scaled = (rows16[1, b].astype(F32) * jnp.exp(cum_x)).astype(BF16)
        rows16[2, b] = weighted
        rows16[3, b] = scaled
        states[0, b] = tn(bcs[b, :, :STATE], weighted)
        states[1, b] = tn(bcs[b, :, STATE:], scaled)
    forward, backward, through = states[0, 0], states[1, q - 1], ds[0]
    for b in range(1, q):
        forward = ds[b] * forward + states[0, b]
        backward = ds[q - 1 - b] * backward + states[1, q - 1 - b]
        through = through * ds[b]
    totals[0] = forward
    totals[1] = backward
    plane[...] = through
    sent[...] = jnp.where(lax.div(lax.axis_index("seq"), q) < planes // 2, forward, backward)


def relay_body(q, hop, came, totals, plane, sent):
    up = lax.div(lax.axis_index("seq"), q) == hop + 1
    sent[...] = jnp.where(up, totals[0], totals[1]) + plane[...] * came[...]


def local_body(q, first, hc, skip, rows16, bcs, cums, a_cols, gx, gp):
    rows, cols = iotas()
    causal = rows <= cols
    low = lax.broadcasted_iota(jnp.int32, (SPAN, 128), 1) < HEAD_DIM
    skip_at = in_group(q) * (HEADS // q) + first
    for b in range(q):
        b_cols, c_cols = bcs[b, :, :STATE], bcs[b, :, STATE:]
        kernel = nt(b_cols, c_cols)
        mixing = jnp.zeros((SPAN, SPAN), F32)
        for pair in range(hc // 2):
            at = slice(pair * 128, pair * 128 + 128)
            x, g = rows16[0, b, :, at], rows16[1, b, :, at]
            parts = []
            for half in range(2):
                h = 2 * pair + half
                gap = cums[b, h : h + 1, :] - a_cols[b, :, h : h + 1]
                decay = jnp.exp(jnp.where(causal, gap, -jnp.inf))
                picked = jnp.where(low if half == 0 else ~low, x, jnp.zeros_like(x))
                mixing += decay * nt(picked, g)
                parts.append(nn((decay * kernel).astype(BF16), g))
            gains = jnp.where(low, skip[skip_at + 2 * pair], skip[skip_at + 2 * pair + 1])
            gx[b, :, at] = jnp.where(low, parts[0], parts[1]) + gains * g.astype(F32)
        mixed = mixing.astype(BF16)
        gp[b, :, :STATE] = nn(mixed, c_cols)
        gp[b, :, STATE:] = tn(mixed, b_cols)


def final_body(q, planes, more, *refs):
    it = iter(refs)
    got = [next(it) for _ in range(planes - 1)]
    rows16, states, f1s, ds, bcs, gx, gp = [next(it) for _ in range(7)]
    before = next(it) if more else None
    gx_out = [next(it) for _ in range(q)]
    gp_out, gx_all = it
    y = in_group(q)
    z = lax.div(lax.axis_index("seq"), q)
    start = after = jnp.zeros(got[0].shape, F32)
    for t in range(planes - 1):
        came = got[t][...]
        start += jnp.where(z == t + 1, 1.0, 0.0) * came
        after += jnp.where(z == planes - 2 - t, 1.0, 0.0) * came
    for b in range(q):
        part = gp[b, :, STATE:] + nt(rows16[3, b], start.astype(BF16))
        gp_out[b, :, STATE:] = part if before is None else part + before[b, :, STATE:]
        if b < q - 1:
            start = ds[b] * start + states[0, b]
    for b in range(q - 1, -1, -1):
        rounded = after.astype(BF16)
        gx_all[b] = gx[b] + f1s[b] * nn(bcs[b, :, :STATE], rounded)
        part = gp[b, :, :STATE] + nt(rows16[2, b], rounded)
        gp_out[b, :, :STATE] = part if before is None else part + before[b, :, :STATE]
        if b > 0:
            after = ds[b] * after + states[1, b]
    for r in range(q):
        gx_out[r][...] = gx_all[lax.rem(y + r, q)]


def assemble_body(q, group, spans, *refs):
    parts, result = refs[:-1], refs[-1]
    y = in_group(q)
    for r in range(q):
        base = lax.rem(y - r + q, q) * group
        for c, (first, width) in enumerate(spans):
            at = pl.multiple_of(base + first, 128)
            result[:, pl.ds(at, width)] = parts[r * len(spans) + c][...].astype(BF16)


def weight_body(n_dp, q, planes, rows, scale, *refs):
    it = iter(refs)
    tokens = [next(it) for _ in range(n_dp)]
    swapped = [next(it) for _ in range(q - 1)]
    grads = [next(it) for _ in range(n_dp)]
    outs = [next(it) for _ in range(planes)]
    held, factors, products = it
    width = planes * rows
    seq = lax.axis_index("seq")
    y, z = lax.rem(seq, q), lax.div(seq, q)
    for r in range(n_dp):
        held[y, r] = columns(tokens[r], y * width, width).astype(BF16)
        for b in range(q):
            factors[b, r] = grads[r][b].astype(BF16)
    for k in range(1, q):
        at = lax.rem(y - k + q, q)
        for r in range(n_dp):
            held[at, r] = swapped[k - 1][r].astype(BF16)
    total = tn(
        held[...].reshape(q * n_dp * SPAN, width), factors[...].reshape(q * n_dp * SPAN, 2 * STATE)
    )
    products[...] = (total * scale).reshape(planes, rows, 2 * STATE)
    for r in range(planes):
        outs[r][...] = products[lax.rem(z + r, planes)]


def behind(value, *others):
    return lax.optimization_barrier((value,) + others)[0]


def on_device(layer_input, proj_weight, inputs, step_size, log_decay, skip_gain, grad_out):
    n_seq, n_dp = lax.axis_size("seq"), lax.axis_size("dp")
    q = group_size(n_seq)
    planes = n_seq // q
    heads = HEADS // q
    group = heads * HEAD_DIM
    chunks = head_chunks(heads)
    spans = [(first * HEAD_DIM, count * HEAD_DIM) for first, count in chunks]
    tokens, x, g = layer_input[0], inputs[0], grad_out[0]
    length, features = tokens.shape
    seq = lax.axis_index("seq")

    def swap(value, r):
        pairs = [(z * q + i, z * q + (i + r) % q) for z in range(planes) for i in range(q)]
        return lax.ppermute(value, "seq", pairs)

    def across(value, r):
        return lax.ppermute(value, "dp", [(i, i ^ r) for i in range(n_dp)])

    def pack(first, width, keep):
        scratch = (pltpu.VMEM((q - 1, 2, SPAN, width), BF16), pltpu.SemaphoreType.DMA((q, 2)))
        outs = [out((2, SPAN, width))] * (q - 1) + [out((2, SPAN, group), BF16)] * keep
        body = functools.partial(pack_body, q, group, first, width, keep)
        return call(body, outs, scratch, name="pack", hbm=2)(x, g)

    packed = pack(*spans[0], False)
    xg_in = [[swap(packed[r - 1], r) for r in range(1, q)]]
    bundles = call(
        functools.partial(project_body, q), [out((SPAN + heads, 2 * STATE))] * q, name="project"
    )(*loose([tokens, proj_weight, log_decay[0], step_size[0]]))
    projected = bundles[0]
    bundles = [projected] + [swap(bundles[r], r) for r in range(1, q)]
    packed = pack(*spans[1], True)
    own = packed[q - 1]
    got = [behind(packed[r - 1], projected) for r in range(1, q)]
    xg_in.append([swap(got[r - 1], r) for r in range(1, q)])
    columns_each = features // n_dp
    rows = columns_each // n_seq
    part = planes * rows

    shapes = [out((length, columns_each))] * n_dp
    token_parts = list(
        call(functools.partial(deal_body, rows, q, planes), shapes, name="deal")(
            [behind(tokens, own)]
        )
    )
    for r in range(n_dp - 1, 0, -1):
        token_parts[r] = across(token_parts[r], r)

    held, local = [], []
    for c, (first, count) in enumerate(chunks):
        wide = (q, SPAN, count * HEAD_DIM)
        state = out((STATE, wide[2]))
        outs = [
            out((4,) + wide, BF16), out((2,) + wide), out(wide), out((q, 1, wide[2])),
            out((2, STATE, wide[2])), state, out((1, wide[2])),
            out((q, SPAN, 2 * STATE), BF16), out((q, count, SPAN)), out((q, SPAN, count)),
        ]
        scratch = (pltpu.VMEM((q, count, SPAN), F32),)
        body = functools.partial(states_body, q, planes, first, count)
        if c > 0:
            xg_in[c] = [behind(v, held[c - 1][5]) for v in xg_in[c]]
        held.append(call(body, outs, scratch, name="states")(own, *xg_in[c], *bundles))
        body = functools.partial(local_body, q, first, count)
        rows16, bcs, cums, a_cols = (held[c][k] for k in (0, 7, 8, 9))
        outs = [out(wide), out((q, SPAN, 2 * STATE))]
        local.append(call(body, outs, smem=1, name="local")(skip_gain, rows16, bcs, cums, a_cols))

    sent = [h[5] for h in held]
    arrived = [[] for _ in held]
    for t in range(planes - 1):
        top = planes - 1 - t
        pairs = [(t * q + i, (t + 1) * q + i) for i in range(q)]
        pairs += [(top * q + i, (top - 1) * q + i) for i in range(q)]
        for c in range(PARTS):
            came = lax.ppermute(sent[c], "seq", pairs)
            if t == max(planes - 3, 0):
                came = behind(came, local[c])
            if c > 0 and t < planes - 2:
                came = behind(came, sent[c - 1])
            if c == 0 and t > 0:
                came = behind(came, sent[PARTS - 1])
            if c == 0 and t == 0:
                came = behind(came, held[-1][5], *token_parts[1:])
            arrived[c].append(came)
            if t < planes - 2:
                (sent[c],) = call(
                    functools.partial(relay_body, q, t), [out(came.shape)], name="relay"
                )(came, held[c][4], held[c][6])
        if t == max(planes - 3, 0):
            ready = behind(tuple(token_parts), sent[0])
            handed = call(
                functools.partial(hand_body, q, part), [out((n_dp, length, part))] * (q - 1), name="hand"
            )(*ready)
            swapped = [swap(handed[r - 1], r) for r in range(1, q)]

    before, gx_parts = [], {}
    for c, (first, width) in enumerate(spans):
        rows16, states, f1s, ds, bcs = (held[c][k] for k in (0, 1, 2, 3, 7))
        outs = [out((SPAN, width))] * q + [out((q, SPAN, 2 * STATE))]
        scratch = (pltpu.VMEM((q, SPAN, width), F32),)
        body = functools.partial(final_body, q, planes, bool(before))
        done = call(body, outs, scratch, name="final")(
            *arrived[c], rows16, states, f1s, ds, bcs, *local[c], *before
        )
        for r in range(q):
            gx_parts[r, c] = done[r]
        before = [done[q]]

    gp = before[0]
    for r in range(1, q):
        gp = gp + behind(swap(before[0], r), swapped[r - 1])
    grads = {0: gp}
    bit = n_dp // 2
    while bit:
        for r in list(grads):
            grads[r ^ bit] = across(grads[r], bit)
        bit //= 2
    scale = 1.0 / (length * n_seq)
    outs = [out((rows, 2 * STATE))] * planes
    args = token_parts + swapped + [grads[r] for r in range(n_dp)]
    scratch = (
        pltpu.VMEM((q, n_dp, SPAN, part), BF16),
        pltpu.VMEM((q, n_dp, SPAN, 2 * STATE), BF16),
        pltpu.VMEM((planes, rows, 2 * STATE), F32),
    )
    body = functools.partial(weight_body, n_dp, q, planes, rows, scale)
    pieces = call(body, outs, scratch, name="weight")(*args)
    grad_weight = pieces[0]
    for r in range(1, planes):
        pairs = [(z * q + i, (z + r) % planes * q + i) for z in range(planes) for i in range(q)]
        grad_weight = grad_weight + lax.ppermute(pieces[r], "seq", pairs)

    parts = [gx_parts[0, c] for c in range(PARTS)]
    for r in range(1, q):
        parts += [swap(gx_parts[r, c], r) for c in range(PARTS)]
    body = functools.partial(assemble_body, q, group, spans)
    (grad_x,) = call(body, [[out((length, q * group), BF16)]], name="assemble")(*parts)
    return grad_x[None], grad_weight


def solution(mesh):
    return jax.shard_map(
        on_device,
        mesh=mesh,
        in_specs=(
            P("dp", "seq", None),
            P(),
            P("dp", "seq", None),
            P("dp", None, "seq"),
            P("dp", None, "seq"),
            P(),
            P("dp", "seq", None),
        ),
        out_specs=(P("dp", "seq", None), P(("dp", "seq"), None)),
        check_vma=False,
    )
```

```python
import functools

import jax
import jax.numpy as jnp
from jax import lax
from jax.experimental import pallas as pl
from jax.experimental.pallas import tpu as pltpu
from jax.sharding import PartitionSpec as P

HEADS = 32
HEAD_DIM = 64
STATE = 128
SPAN = 128
PARTS = 2
F32 = jnp.float32
BF16 = jnp.bfloat16
VMEM_LIMIT = 16 * 1024 * 1024


def group_size(n_seq):
    q = 1
    while n_seq % (2 * q) == 0 and 4 * q * q <= n_seq:
        q *= 2
    return q


def nn(a, b):
    return lax.dot_general(a, b, (((1,), (0,)), ((), ())), preferred_element_type=F32)


def nt(a, b):
    return lax.dot_general(a, b, (((1,), (1,)), ((), ())), preferred_element_type=F32)


def tn(a, b):
    return lax.dot_general(a, b, (((0,), (0,)), ((), ())), preferred_element_type=F32)


def terms(a):
    high = a.astype(BF16)
    rest = a - high.astype(F32)
    mid = rest.astype(BF16)
    return high, mid, (rest - mid.astype(F32)).astype(BF16)


def head_chunks(heads):
    first = 2 * (heads * 5 // 16)
    return [(0, first), (first, heads - first)]


def call(body, outs, scratch=(), name=None, smem=0, hbm=0):
    def run(*args):
        args = list(args)
        for k in range(smem, len(args)):
            if isinstance(args[k], list):
                args[k] = args[k][0]
            else:
                place = pltpu.HBM if k < smem + hbm else pltpu.VMEM
                args[k] = pltpu.with_memory_space_constraint(args[k], place)
        specs = [pl.BlockSpec(memory_space=pltpu.SMEM)] * smem
        specs += [pl.BlockSpec(memory_space=pltpu.HBM)] * hbm
        specs += [pl.BlockSpec(memory_space=pltpu.VMEM)] * (len(args) - smem - hbm)
        return pl.pallas_call(
            body,
            out_shape=tuple(o[0] if isinstance(o, list) else pltpu.VMEM(o.shape, o.dtype) for o in outs),
            in_specs=specs,
            out_specs=tuple(pl.BlockSpec(memory_space=pltpu.VMEM) for _ in outs),
            scratch_shapes=scratch,
            compiler_params=pltpu.CompilerParams(vmem_limit_bytes=VMEM_LIMIT),
            name=name,
        )(*args)

    return run


def loose(values):
    return [[value] for value in values]


def in_group(q):
    return lax.rem(lax.axis_index("seq"), q)


def out(shape, dtype=F32):
    return jax.ShapeDtypeStruct(shape, dtype)


def iotas():
    rows = lax.broadcasted_iota(jnp.int32, (SPAN, SPAN), 0)
    cols = lax.broadcasted_iota(jnp.int32, (SPAN, SPAN), 1)
    return rows, cols


def columns(ref, start, width):
    return ref[:, pl.ds(pl.multiple_of(start, 128), width)]


def pack_body(q, group, first, width, keep, x, g, *refs):
    packed, rest = refs[: q - 1], list(refs[q - 1 :])
    own = rest.pop(0) if keep else None
    stage, sems = rest
    y = in_group(q)
    copies = {}
    for r in range(1, q):
        at = pl.multiple_of(lax.rem(y + r, q) * group + first, 128)
        for k, source in enumerate((x, g)):
            copies[r, k] = pltpu.make_async_copy(
                source.at[:, pl.ds(at, width)], stage.at[r - 1, k], sems.at[r, k]
            )
            copies[r, k].start()
    if keep:
        at = pl.multiple_of(y * group, 128)
        for k, source in enumerate((x, g)):
            copies[0, k] = pltpu.make_async_copy(source.at[:, pl.ds(at, group)], own.at[k], sems.at[0, k])
            copies[0, k].start()
    for r in range(1, q):
        for k in range(2):
            copies[r, k].wait()
            packed[r - 1][k] = stage[r - 1, k].astype(F32)
    if keep:
        for k in range(2):
            copies[0, k].wait()


def deal_body(rows, q, planes, tokens, *outs):
    n_dp = len(outs)
    each = q * planes * rows
    dp = lax.axis_index("dp")
    for r in range(n_dp - 1, -1, -1):
        cut = columns(tokens, lax.bitwise_xor(dp, r) * each, each).astype(F32)
        for k in range(q * planes):
            at = (k % planes * q + k // planes) * rows
            outs[r][:, k * rows : (k + 1) * rows] = cut[:, at : at + rows]


def hand_body(q, part, *refs):
    tokens, outs = refs[: 1 - q], refs[1 - q :]
    y = in_group(q)
    for r in range(1, q):
        for k, ref in enumerate(tokens):
            outs[r - 1][k] = columns(ref, lax.rem(y + r, q) * part, part)


def project_body(q, tokens, weight, decay, step, *bundles):
    proj = nn(tokens[...], weight[...]).astype(BF16).astype(F32)
    heads = HEADS // q
    y = in_group(q)
    for r in range(q):
        at = pl.multiple_of(lax.rem(y + r, q) * heads, heads)
        bundles[r][:SPAN, :] = proj
        bundles[r][SPAN:, :SPAN] = decay[pl.ds(at, heads), :]
        bundles[r][SPAN:, SPAN:] = step[pl.ds(at, heads), :]


def states_body(q, planes, first, hc, *refs):
    it = iter(refs)
    own = next(it)
    xg_in = [next(it) for _ in range(q - 1)]
    bundles = [next(it) for _ in range(q)]
    rows16, states, f1s, ds, totals, sent, plane, bcs, cums, a_cols, steps = it
    width = hc * HEAD_DIM
    y = in_group(q)
    for k in range(2):
        rows16[k, y] = own[k, :, first * HEAD_DIM : first * HEAD_DIM + width]
    low = SPAN + first
    for r in range(q):
        block = lax.rem(y - r + q, q)
        if r > 0:
            for k in range(2):
                rows16[k, block] = xg_in[r - 1][k].astype(BF16)
        bcs[block] = bundles[r][:SPAN, :].astype(BF16)
        cums[block] = bundles[r][low : low + hc, :SPAN]
        steps[block] = bundles[r][low : low + hc, SPAN:]
    rows, cols = iotas()
    tri = jnp.where(rows <= cols, 1.0, 0.0).astype(BF16)
    head_of = lax.broadcasted_iota(jnp.int32, (hc, width), 1) // HEAD_DIM
    spread = head_of == lax.broadcasted_iota(jnp.int32, (hc, width), 0)
    spread = jnp.where(spread, 1.0, 0.0).astype(BF16)
    for b in range(q):
        cum = sum(nn(term, tri) for term in terms(cums[b]))
        a = cum - jnp.log(steps[b])
        cums[b] = cum
        cum_c, a_c = cum.T, a.T
        a_cols[b] = a_c
        cum_x = sum(nn(term, spread) for term in terms(cum_c))
        a_x = sum(nn(term, spread) for term in terms(a_c))
        total = cum_x[SPAN - 1 : SPAN, :]
        f1 = jnp.exp(total - a_x)
        f1s[b] = f1
        ds[b] = jnp.exp(total)
        weighted = (rows16[0, b].astype(F32) * f1).astype(BF16)
        scaled = (rows16[1, b].astype(F32) * jnp.exp(cum_x)).astype(BF16)
        rows16[2, b] = weighted
        rows16[3, b] = scaled
        states[0, b] = tn(bcs[b, :, :STATE], weighted)
        states[1, b] = tn(bcs[b, :, STATE:], scaled)
    forward, backward, through = states[0, 0], states[1, q - 1], ds[0]
    for b in range(1, q):
        forward = ds[b] * forward + states[0, b]
        backward = ds[q - 1 - b] * backward + states[1, q - 1 - b]
        through = through * ds[b]
    totals[0] = forward
    totals[1] = backward
    plane[...] = through
    sent[...] = jnp.where(lax.div(lax.axis_index("seq"), q) < planes // 2, forward, backward)


def relay_body(q, hop, came, totals, plane, sent):
    up = lax.div(lax.axis_index("seq"), q) == hop + 1
    sent[...] = jnp.where(up, totals[0], totals[1]) + plane[...] * came[...]


def local_body(q, first, hc, skip, rows16, bcs, cums, a_cols, gx, gp):
    rows, cols = iotas()
    causal = rows <= cols
    low = lax.broadcasted_iota(jnp.int32, (SPAN, 128), 1) < HEAD_DIM
    skip_at = in_group(q) * (HEADS // q) + first
    for b in range(q):
        b_cols, c_cols = bcs[b, :, :STATE], bcs[b, :, STATE:]
        kernel = nt(b_cols, c_cols)
        mixing = jnp.zeros((SPAN, SPAN), F32)
        for pair in range(hc // 2):
            at = slice(pair * 128, pair * 128 + 128)
            x, g = rows16[0, b, :, at], rows16[1, b, :, at]
            parts = []
            for half in range(2):
                h = 2 * pair + half
                gap = cums[b, h : h + 1, :] - a_cols[b, :, h : h + 1]
                decay = jnp.exp(jnp.where(causal, gap, -jnp.inf))
                picked = jnp.where(low if half == 0 else ~low, x, jnp.zeros_like(x))
                mixing += decay * nt(picked, g)
                parts.append(nn((decay * kernel).astype(BF16), g))
            gains = jnp.where(low, skip[skip_at + 2 * pair], skip[skip_at + 2 * pair + 1])
            gx[b, :, at] = jnp.where(low, parts[0], parts[1]) + gains * g.astype(F32)
        mixed = mixing.astype(BF16)
        gp[b, :, :STATE] = nn(mixed, c_cols)
        gp[b, :, STATE:] = tn(mixed, b_cols)


def final_body(q, planes, more, *refs):
    it = iter(refs)
    got = [next(it) for _ in range(planes - 1)]
    rows16, states, f1s, ds, bcs, gx, gp = [next(it) for _ in range(7)]
    before = next(it) if more else None
    gx_out = [next(it) for _ in range(q)]
    gp_out, gx_all = it
    y = in_group(q)
    z = lax.div(lax.axis_index("seq"), q)
    start = after = jnp.zeros(got[0].shape, F32)
    for t in range(planes - 1):
        came = got[t][...]
        start += jnp.where(z == t + 1, 1.0, 0.0) * came
        after += jnp.where(z == planes - 2 - t, 1.0, 0.0) * came
    for b in range(q):
        part = gp[b, :, STATE:] + nt(rows16[3, b], start.astype(BF16))
        gp_out[b, :, STATE:] = part if before is None else part + before[b, :, STATE:]
        if b < q - 1:
            start = ds[b] * start + states[0, b]
    for b in range(q - 1, -1, -1):
        rounded = after.astype(BF16)
        gx_all[b] = gx[b] + f1s[b] * nn(bcs[b, :, :STATE], rounded)
        part = gp[b, :, :STATE] + nt(rows16[2, b], rounded)
        gp_out[b, :, :STATE] = part if before is None else part + before[b, :, :STATE]
        if b > 0:
            after = ds[b] * after + states[1, b]
    for r in range(q):
        gx_out[r][...] = gx_all[lax.rem(y + r, q)]


def assemble_body(q, group, spans, *refs):
    parts, result = refs[:-1], refs[-1]
    y = in_group(q)
    for r in range(q):
        base = lax.rem(y - r + q, q) * group
        for c, (first, width) in enumerate(spans):
            at = pl.multiple_of(base + first, 128)
            result[:, pl.ds(at, width)] = parts[r * len(spans) + c][...].astype(BF16)


def weight_body(n_dp, q, planes, rows, scale, *refs):
    it = iter(refs)
    tokens = [next(it) for _ in range(n_dp)]
    swapped = [next(it) for _ in range(q - 1)]
    grads = [next(it) for _ in range(n_dp)]
    outs = [next(it) for _ in range(planes)]
    held, factors, products = it
    width = planes * rows
    seq = lax.axis_index("seq")
    y, z = lax.rem(seq, q), lax.div(seq, q)
    for r in range(n_dp):
        held[y, r] = columns(tokens[r], y * width, width).astype(BF16)
        for b in range(q):
            factors[b, r] = grads[r][b].astype(BF16)
    for k in range(1, q):
        at = lax.rem(y - k + q, q)
        for r in range(n_dp):
            held[at, r] = swapped[k - 1][r].astype(BF16)
    total = tn(
        held[...].reshape(q * n_dp * SPAN, width), factors[...].reshape(q * n_dp * SPAN, 2 * STATE)
    )
    products[...] = (total * scale).reshape(planes, rows, 2 * STATE)
    for r in range(planes):
        outs[r][...] = products[lax.rem(z + r, planes)]


def behind(value, *others):
    return lax.optimization_barrier((value,) + others)[0]


def on_device(layer_input, proj_weight, inputs, step_size, log_decay, skip_gain, grad_out):
    n_seq, n_dp = lax.axis_size("seq"), lax.axis_size("dp")
    q = group_size(n_seq)
    planes = n_seq // q
    heads = HEADS // q
    group = heads * HEAD_DIM
    chunks = head_chunks(heads)
    spans = [(first * HEAD_DIM, count * HEAD_DIM) for first, count in chunks]
    tokens, x, g = layer_input[0], inputs[0], grad_out[0]
    length, features = tokens.shape
    seq = lax.axis_index("seq")

    def swap(value, r):
        pairs = [(z * q + i, z * q + (i + r) % q) for z in range(planes) for i in range(q)]
        return lax.ppermute(value, "seq", pairs)

    def across(value, r):
        return lax.ppermute(value, "dp", [(i, i ^ r) for i in range(n_dp)])

    def pack(first, width, keep):
        scratch = (pltpu.VMEM((q - 1, 2, SPAN, width), BF16), pltpu.SemaphoreType.DMA((q, 2)))
        outs = [out((2, SPAN, width))] * (q - 1) + [out((2, SPAN, group), BF16)] * keep
        body = functools.partial(pack_body, q, group, first, width, keep)
        return call(body, outs, scratch, name="pack", hbm=2)(x, g)

    packed = pack(*spans[0], False)
    xg_in = [[swap(packed[r - 1], r) for r in range(1, q)]]
    bundles = call(
        functools.partial(project_body, q), [out((SPAN + heads, 2 * STATE))] * q, name="project"
    )(*loose([tokens, proj_weight, log_decay[0], step_size[0]]))
    projected = bundles[0]
    bundles = [projected] + [swap(bundles[r], r) for r in range(1, q)]
    packed = pack(*spans[1], True)
    own = packed[q - 1]
    got = [behind(packed[r - 1], projected) for r in range(1, q)]
    xg_in.append([swap(got[r - 1], r) for r in range(1, q)])
    columns_each = features // n_dp
    rows = columns_each // n_seq
    part = planes * rows

    shapes = [out((length, columns_each))] * n_dp
    token_parts = list(
        call(functools.partial(deal_body, rows, q, planes), shapes, name="deal")(
            [behind(tokens, own)]
        )
    )
    for r in range(n_dp - 1, 0, -1):
        token_parts[r] = across(token_parts[r], r)

    held, local = [], []
    for c, (first, count) in enumerate(chunks):
        wide = (q, SPAN, count * HEAD_DIM)
        state = out((STATE, wide[2]))
        outs = [
            out((4,) + wide, BF16), out((2,) + wide), out(wide), out((q, 1, wide[2])),
            out((2, STATE, wide[2])), state, out((1, wide[2])),
            out((q, SPAN, 2 * STATE), BF16), out((q, count, SPAN)), out((q, SPAN, count)),
        ]
        scratch = (pltpu.VMEM((q, count, SPAN), F32),)
        body = functools.partial(states_body, q, planes, first, count)
        if c > 0:
            xg_in[c] = [behind(v, held[c - 1][5]) for v in xg_in[c]]
        held.append(call(body, outs, scratch, name="states")(own, *xg_in[c], *bundles))
        body = functools.partial(local_body, q, first, count)
        rows16, bcs, cums, a_cols = (held[c][k] for k in (0, 7, 8, 9))
        outs = [out(wide), out((q, SPAN, 2 * STATE))]
        local.append(call(body, outs, smem=1, name="local")(skip_gain, rows16, bcs, cums, a_cols))

    sent = [h[5] for h in held]
    arrived = [[] for _ in held]
    for t in range(planes - 1):
        top = planes - 1 - t
        pairs = [(t * q + i, (t + 1) * q + i) for i in range(q)]
        pairs += [(top * q + i, (top - 1) * q + i) for i in range(q)]
        for c in range(PARTS):
            came = lax.ppermute(sent[c], "seq", pairs)
            if t == max(planes - 3, 0):
                came = behind(came, local[c])
            if c > 0 and t < planes - 2:
                came = behind(came, sent[c - 1])
            if c == 0 and t > 0:
                came = behind(came, sent[PARTS - 1])
            if c == 0 and t == 0:
                came = behind(came, held[-1][5], *token_parts[1:])
            arrived[c].append(came)
            if t < planes - 2:
                (sent[c],) = call(
                    functools.partial(relay_body, q, t), [out(came.shape)], name="relay"
                )(came, held[c][4], held[c][6])
        if t == 0:
            ready = behind(tuple(token_parts), sent[0])
            handed = call(
                functools.partial(hand_body, q, part), [out((n_dp, length, part))] * (q - 1), name="hand"
            )(*ready)
            swapped = [swap(handed[r - 1], r) for r in range(1, q)]

    before, gx_parts = [], {}
    for c, (first, width) in enumerate(spans):
        rows16, states, f1s, ds, bcs = (held[c][k] for k in (0, 1, 2, 3, 7))
        outs = [out((SPAN, width))] * q + [out((q, SPAN, 2 * STATE))]
        scratch = (pltpu.VMEM((q, SPAN, width), F32),)
        body = functools.partial(final_body, q, planes, bool(before))
        done = call(body, outs, scratch, name="final")(
            *arrived[c], rows16, states, f1s, ds, bcs, *local[c], *before
        )
        for r in range(q):
            gx_parts[r, c] = done[r]
        before = [done[q]]

    gp = before[0]
    for r in range(1, q):
        gp = gp + behind(swap(before[0], r), swapped[r - 1])
    grads = {0: gp}
    bit = n_dp // 2
    while bit:
        for r in list(grads):
            grads[r ^ bit] = across(grads[r], bit)
        bit //= 2
    scale = 1.0 / (length * n_seq)
    outs = [out((rows, 2 * STATE))] * planes
    args = token_parts + swapped + [grads[r] for r in range(n_dp)]
    scratch = (
        pltpu.VMEM((q, n_dp, SPAN, part), BF16),
        pltpu.VMEM((q, n_dp, SPAN, 2 * STATE), BF16),
        pltpu.VMEM((planes, rows, 2 * STATE), F32),
    )
    body = functools.partial(weight_body, n_dp, q, planes, rows, scale)
    pieces = call(body, outs, scratch, name="weight")(*args)
    grad_weight = pieces[0]
    for r in range(1, planes):
        pairs = [(z * q + i, (z + r) % planes * q + i) for z in range(planes) for i in range(q)]
        grad_weight = grad_weight + lax.ppermute(pieces[r], "seq", pairs)

    parts = [gx_parts[0, c] for c in range(PARTS)]
    for r in range(1, q):
        parts += [swap(gx_parts[r, c], r) for c in range(PARTS)]
    body = functools.partial(assemble_body, q, group, spans)
    (grad_x,) = call(body, [[out((length, q * group), BF16)]], name="assemble")(*parts)
    return grad_x[None], grad_weight


def solution(mesh):
    return jax.shard_map(
        on_device,
        mesh=mesh,
        in_specs=(
            P("dp", "seq", None),
            P(),
            P("dp", "seq", None),
            P("dp", None, "seq"),
            P("dp", None, "seq"),
            P(),
            P("dp", "seq", None),
        ),
        out_specs=(P("dp", "seq", None), P(("dp", "seq"), None)),
        check_vma=False,
    )
```

```python
import functools

import jax
import jax.numpy as jnp
from jax import lax
from jax.experimental import pallas as pl
from jax.experimental.pallas import tpu as pltpu
from jax.sharding import PartitionSpec as P

HEADS = 32
HEAD_DIM = 64
STATE = 128
SPAN = 128
PARTS = 2
F32 = jnp.float32
BF16 = jnp.bfloat16
VMEM_LIMIT = 16 * 1024 * 1024


def group_size(n_seq):
    q = 1
    while n_seq % (2 * q) == 0 and 4 * q * q <= n_seq:
        q *= 2
    return q


def nn(a, b):
    return lax.dot_general(a, b, (((1,), (0,)), ((), ())), preferred_element_type=F32)


def nt(a, b):
    return lax.dot_general(a, b, (((1,), (1,)), ((), ())), preferred_element_type=F32)


def tn(a, b):
    return lax.dot_general(a, b, (((0,), (0,)), ((), ())), preferred_element_type=F32)


def terms(a):
    high = a.astype(BF16)
    rest = a - high.astype(F32)
    mid = rest.astype(BF16)
    return high, mid, (rest - mid.astype(F32)).astype(BF16)


def head_chunks(heads):
    first = 2 * (heads * 5 // 16)
    return [(0, first), (first, heads - first)]


def call(body, outs, scratch=(), name=None, smem=0, hbm=0):
    def run(*args):
        args = list(args)
        for k in range(smem, len(args)):
            if isinstance(args[k], list):
                args[k] = args[k][0]
            else:
                place = pltpu.HBM if k < smem + hbm else pltpu.VMEM
                args[k] = pltpu.with_memory_space_constraint(args[k], place)
        specs = [pl.BlockSpec(memory_space=pltpu.SMEM)] * smem
        specs += [pl.BlockSpec(memory_space=pltpu.HBM)] * hbm
        specs += [pl.BlockSpec(memory_space=pltpu.VMEM)] * (len(args) - smem - hbm)
        return pl.pallas_call(
            body,
            out_shape=tuple(o[0] if isinstance(o, list) else pltpu.VMEM(o.shape, o.dtype) for o in outs),
            in_specs=specs,
            out_specs=tuple(pl.BlockSpec(memory_space=pltpu.VMEM) for _ in outs),
            scratch_shapes=scratch,
            compiler_params=pltpu.CompilerParams(vmem_limit_bytes=VMEM_LIMIT),
            name=name,
        )(*args)

    return run


def loose(values):
    return [[value] for value in values]


def in_group(q):
    return lax.rem(lax.axis_index("seq"), q)


def out(shape, dtype=F32):
    return jax.ShapeDtypeStruct(shape, dtype)


def iotas():
    rows = lax.broadcasted_iota(jnp.int32, (SPAN, SPAN), 0)
    cols = lax.broadcasted_iota(jnp.int32, (SPAN, SPAN), 1)
    return rows, cols


def columns(ref, start, width):
    return ref[:, pl.ds(pl.multiple_of(start, 128), width)]


def pack_body(q, group, first, width, keep, x, g, *refs):
    packed, rest = refs[: q - 1], list(refs[q - 1 :])
    own = rest.pop(0) if keep else None
    stage, sems = rest
    y = in_group(q)
    copies = {}
    for r in range(1, q):
        at = pl.multiple_of(lax.rem(y + r, q) * group + first, 128)
        for k, source in enumerate((x, g)):
            copies[r, k] = pltpu.make_async_copy(
                source.at[:, pl.ds(at, width)], stage.at[r - 1, k], sems.at[r, k]
            )
            copies[r, k].start()
    if keep:
        at = pl.multiple_of(y * group, 128)
        for k, source in enumerate((x, g)):
            copies[0, k] = pltpu.make_async_copy(source.at[:, pl.ds(at, group)], own.at[k], sems.at[0, k])
            copies[0, k].start()
    for r in range(1, q):
        for k in range(2):
            copies[r, k].wait()
            packed[r - 1][k] = stage[r - 1, k].astype(F32)
    if keep:
        for k in range(2):
            copies[0, k].wait()


def deal_body(rows, q, planes, tokens, *outs):
    n_dp = len(outs)
    each = q * planes * rows
    dp = lax.axis_index("dp")
    for r in range(n_dp - 1, -1, -1):
        cut = columns(tokens, lax.bitwise_xor(dp, r) * each, each).astype(F32)
        for k in range(q * planes):
            at = (k % planes * q + k // planes) * rows
            outs[r][:, k * rows : (k + 1) * rows] = cut[:, at : at + rows]


def hand_body(q, part, *refs):
    tokens, outs = refs[: 1 - q], refs[1 - q :]
    y = in_group(q)
    for r in range(1, q):
        for k, ref in enumerate(tokens):
            outs[r - 1][k] = columns(ref, lax.rem(y + r, q) * part, part)


def project_body(q, tokens, weight, decay, step, *bundles):
    proj = nn(tokens[...], weight[...]).astype(BF16).astype(F32)
    heads = HEADS // q
    y = in_group(q)
    for r in range(q):
        at = pl.multiple_of(lax.rem(y + r, q) * heads, heads)
        bundles[r][:SPAN, :] = proj
        bundles[r][SPAN:, :SPAN] = decay[pl.ds(at, heads), :]
        bundles[r][SPAN:, SPAN:] = step[pl.ds(at, heads), :]


def states_body(q, planes, first, hc, *refs):
    it = iter(refs)
    own = next(it)
    xg_in = [next(it) for _ in range(q - 1)]
    bundles = [next(it) for _ in range(q)]
    rows16, states, f1s, ds, totals, sent, plane, bcs, cums, a_cols, steps = it
    width = hc * HEAD_DIM
    y = in_group(q)
    for k in range(2):
        rows16[k, y] = own[k, :, first * HEAD_DIM : first * HEAD_DIM + width]
    low = SPAN + first
    for r in range(q):
        block = lax.rem(y - r + q, q)
        if r > 0:
            for k in range(2):
                rows16[k, block] = xg_in[r - 1][k].astype(BF16)
        bcs[block] = bundles[r][:SPAN, :].astype(BF16)
        cums[block] = bundles[r][low : low + hc, :SPAN]
        steps[block] = bundles[r][low : low + hc, SPAN:]
    rows, cols = iotas()
    tri = jnp.where(rows <= cols, 1.0, 0.0).astype(BF16)
    head_of = lax.broadcasted_iota(jnp.int32, (hc, width), 1) // HEAD_DIM
    spread = head_of == lax.broadcasted_iota(jnp.int32, (hc, width), 0)
    spread = jnp.where(spread, 1.0, 0.0).astype(BF16)
    for b in range(q):
        cum = sum(nn(term, tri) for term in terms(cums[b]))
        a = cum - jnp.log(steps[b])
        cums[b] = cum
        cum_c, a_c = cum.T, a.T
        a_cols[b] = a_c
        cum_x = sum(nn(term, spread) for term in terms(cum_c))
        a_x = sum(nn(term, spread) for term in terms(a_c))
        total = cum_x[SPAN - 1 : SPAN, :]
        f1 = jnp.exp(total - a_x)
        f1s[b] = f1
        ds[b] = jnp.exp(total)
        weighted = (rows16[0, b].astype(F32) * f1).astype(BF16)
        scaled = (rows16[1, b].astype(F32) * jnp.exp(cum_x)).astype(BF16)
        rows16[2, b] = weighted
        rows16[3, b] = scaled
        states[0, b] = tn(bcs[b, :, :STATE], weighted)
        states[1, b] = tn(bcs[b, :, STATE:], scaled)
    forward, backward, through = states[0, 0], states[1, q - 1], ds[0]
    for b in range(1, q):
        forward = ds[b] * forward + states[0, b]
        backward = ds[q - 1 - b] * backward + states[1, q - 1 - b]
        through = through * ds[b]
    totals[0] = forward
    totals[1] = backward
    plane[...] = through
    sent[...] = jnp.where(lax.div(lax.axis_index("seq"), q) < planes // 2, forward, backward)


def relay_body(q, hop, came, totals, plane, sent):
    up = lax.div(lax.axis_index("seq"), q) == hop + 1
    sent[...] = jnp.where(up, totals[0], totals[1]) + plane[...] * came[...]


def local_body(q, first, hc, skip, rows16, bcs, cums, a_cols, gx, gp):
    rows, cols = iotas()
    causal = rows <= cols
    low = lax.broadcasted_iota(jnp.int32, (SPAN, 128), 1) < HEAD_DIM
    skip_at = in_group(q) * (HEADS // q) + first
    for b in range(q):
        b_cols, c_cols = bcs[b, :, :STATE], bcs[b, :, STATE:]
        kernel = nt(b_cols, c_cols)
        mixing = jnp.zeros((SPAN, SPAN), F32)
        for pair in range(hc // 2):
            at = slice(pair * 128, pair * 128 + 128)
            x, g = rows16[0, b, :, at], rows16[1, b, :, at]
            parts = []
            for half in range(2):
                h = 2 * pair + half
                gap = cums[b, h : h + 1, :] - a_cols[b, :, h : h + 1]
                decay = jnp.exp(jnp.where(causal, gap, -jnp.inf))
                picked = jnp.where(low if half == 0 else ~low, x, jnp.zeros_like(x))
                mixing += decay * nt(picked, g)
                parts.append(nn((decay * kernel).astype(BF16), g))
            gains = jnp.where(low, skip[skip_at + 2 * pair], skip[skip_at + 2 * pair + 1])
            gx[b, :, at] = jnp.where(low, parts[0], parts[1]) + gains * g.astype(F32)
        mixed = mixing.astype(BF16)
        gp[b, :, :STATE] = nn(mixed, c_cols)
        gp[b, :, STATE:] = tn(mixed, b_cols)


def final_body(q, planes, more, *refs):
    it = iter(refs)
    got = [next(it) for _ in range(planes - 1)]
    rows16, states, f1s, ds, bcs, gx, gp = [next(it) for _ in range(7)]
    before = next(it) if more else None
    gx_out = [next(it) for _ in range(q)]
    gp_out, gx_all = it
    y = in_group(q)
    z = lax.div(lax.axis_index("seq"), q)
    start = after = jnp.zeros(got[0].shape, F32)
    for t in range(planes - 1):
        came = got[t][...]
        start += jnp.where(z == t + 1, 1.0, 0.0) * came
        after += jnp.where(z == planes - 2 - t, 1.0, 0.0) * came
    for b in range(q):
        part = gp[b, :, STATE:] + nt(rows16[3, b], start.astype(BF16))
        gp_out[b, :, STATE:] = part if before is None else part + before[b, :, STATE:]
        if b < q - 1:
            start = ds[b] * start + states[0, b]
    for b in range(q - 1, -1, -1):
        rounded = after.astype(BF16)
        gx_all[b] = gx[b] + f1s[b] * nn(bcs[b, :, :STATE], rounded)
        part = gp[b, :, :STATE] + nt(rows16[2, b], rounded)
        gp_out[b, :, :STATE] = part if before is None else part + before[b, :, :STATE]
        if b > 0:
            after = ds[b] * after + states[1, b]
    for r in range(q):
        gx_out[r][...] = gx_all[lax.rem(y + r, q)]


def assemble_body(q, group, spans, *refs):
    parts, result = refs[:-1], refs[-1]
    y = in_group(q)
    for r in range(q):
        base = lax.rem(y - r + q, q) * group
        for c, (first, width) in enumerate(spans):
            at = pl.multiple_of(base + first, 128)
            result[:, pl.ds(at, width)] = parts[r * len(spans) + c][...].astype(BF16)


def weight_body(n_dp, q, planes, rows, scale, *refs):
    it = iter(refs)
    tokens = [next(it) for _ in range(n_dp)]
    swapped = [next(it) for _ in range(q - 1)]
    grads = [next(it) for _ in range(n_dp)]
    outs = [next(it) for _ in range(planes)]
    held, factors, products = it
    width = planes * rows
    seq = lax.axis_index("seq")
    y, z = lax.rem(seq, q), lax.div(seq, q)
    for r in range(n_dp):
        held[y, r] = columns(tokens[r], y * width, width).astype(BF16)
        for b in range(q):
            factors[b, r] = grads[r][b].astype(BF16)
    for k in range(1, q):
        at = lax.rem(y - k + q, q)
        for r in range(n_dp):
            held[at, r] = swapped[k - 1][r].astype(BF16)
    total = tn(
        held[...].reshape(q * n_dp * SPAN, width), factors[...].reshape(q * n_dp * SPAN, 2 * STATE)
    )
    products[...] = (total * scale).reshape(planes, rows, 2 * STATE)
    for r in range(planes):
        outs[r][...] = products[lax.rem(z + r, planes)]


def behind(value, *others):
    return lax.optimization_barrier((value,) + others)[0]


def on_device(layer_input, proj_weight, inputs, step_size, log_decay, skip_gain, grad_out):
    n_seq, n_dp = lax.axis_size("seq"), lax.axis_size("dp")
    q = group_size(n_seq)
    planes = n_seq // q
    heads = HEADS // q
    group = heads * HEAD_DIM
    chunks = head_chunks(heads)
    spans = [(first * HEAD_DIM, count * HEAD_DIM) for first, count in chunks]
    tokens, x, g = layer_input[0], inputs[0], grad_out[0]
    length, features = tokens.shape
    seq = lax.axis_index("seq")

    def swap(value, r):
        pairs = [(z * q + i, z * q + (i + r) % q) for z in range(planes) for i in range(q)]
        return lax.ppermute(value, "seq", pairs)

    def across(value, r):
        return lax.ppermute(value, "dp", [(i, i ^ r) for i in range(n_dp)])

    def pack(first, width, keep):
        scratch = (pltpu.VMEM((q - 1, 2, SPAN, width), BF16), pltpu.SemaphoreType.DMA((q, 2)))
        outs = [out((2, SPAN, width))] * (q - 1) + [out((2, SPAN, group), BF16)] * keep
        body = functools.partial(pack_body, q, group, first, width, keep)
        return call(body, outs, scratch, name="pack", hbm=2)(x, g)

    packed = pack(*spans[0], False)
    xg_in = [[swap(packed[r - 1], r) for r in range(1, q)]]
    bundles = call(
        functools.partial(project_body, q), [out((SPAN + heads, 2 * STATE))] * q, name="project"
    )(*loose([tokens, proj_weight, log_decay[0], step_size[0]]))
    projected = bundles[0]
    bundles = [projected] + [swap(bundles[r], r) for r in range(1, q)]
    packed = pack(*spans[1], True)
    own = packed[q - 1]
    got = [behind(packed[r - 1], projected) for r in range(1, q)]
    xg_in.append([swap(got[r - 1], r) for r in range(1, q)])
    columns_each = features // n_dp
    rows = columns_each // n_seq
    part = planes * rows

    shapes = [out((length, columns_each))] * n_dp
    token_parts = list(
        call(functools.partial(deal_body, rows, q, planes), shapes, name="deal")(
            [behind(tokens, own)]
        )
    )
    for r in range(n_dp - 1, 0, -1):
        token_parts[r] = across(token_parts[r], r)

    held, local = [], []
    for c, (first, count) in enumerate(chunks):
        wide = (q, SPAN, count * HEAD_DIM)
        state = out((STATE, wide[2]))
        outs = [
            out((4,) + wide, BF16), out((2,) + wide), out(wide), out((q, 1, wide[2])),
            out((2, STATE, wide[2])), state, out((1, wide[2])),
            out((q, SPAN, 2 * STATE), BF16), out((q, count, SPAN)), out((q, SPAN, count)),
        ]
        scratch = (pltpu.VMEM((q, count, SPAN), F32),)
        body = functools.partial(states_body, q, planes, first, count)
        if c > 0:
            xg_in[c] = [behind(v, held[c - 1][5]) for v in xg_in[c]]
        held.append(call(body, outs, scratch, name="states")(own, *xg_in[c], *bundles))
        body = functools.partial(local_body, q, first, count)
        rows16, bcs, cums, a_cols = (held[c][k] for k in (0, 7, 8, 9))
        outs = [out(wide), out((q, SPAN, 2 * STATE))]
        local.append(call(body, outs, smem=1, name="local")(skip_gain, rows16, bcs, cums, a_cols))

    sent = [h[5] for h in held]
    arrived = [[] for _ in held]
    for t in range(planes - 1):
        top = planes - 1 - t
        pairs = [(t * q + i, (t + 1) * q + i) for i in range(q)]
        pairs += [(top * q + i, (top - 1) * q + i) for i in range(q)]
        for c in range(PARTS):
            came = lax.ppermute(sent[c], "seq", pairs)
            if t == planes - 2:
                came = behind(came, local[c])
            if c > 0 and t < planes - 2:
                came = behind(came, sent[c - 1])
            if c == 0 and t > 0:
                came = behind(came, sent[PARTS - 1])
            if c == 0 and t == 0:
                came = behind(came, held[-1][5], *token_parts[1:])
            arrived[c].append(came)
            if t < planes - 2:
                (sent[c],) = call(
                    functools.partial(relay_body, q, t), [out(came.shape)], name="relay"
                )(came, held[c][4], held[c][6])
        if t == 0:
            ready = behind(tuple(token_parts), sent[0])
            handed = call(
                functools.partial(hand_body, q, part), [out((n_dp, length, part))] * (q - 1), name="hand"
            )(*ready)
            swapped = [swap(handed[r - 1], r) for r in range(1, q)]

    before, gx_parts = [], {}
    for c, (first, width) in enumerate(spans):
        rows16, states, f1s, ds, bcs = (held[c][k] for k in (0, 1, 2, 3, 7))
        outs = [out((SPAN, width))] * q + [out((q, SPAN, 2 * STATE))]
        scratch = (pltpu.VMEM((q, SPAN, width), F32),)
        body = functools.partial(final_body, q, planes, bool(before))
        done = call(body, outs, scratch, name="final")(
            *arrived[c], rows16, states, f1s, ds, bcs, *local[c], *before
        )
        for r in range(q):
            gx_parts[r, c] = done[r]
        before = [done[q]]

    gp = before[0]
    for r in range(1, q):
        gp = gp + behind(swap(before[0], r), swapped[r - 1])
    grads = {0: gp}
    bit = n_dp // 2
    while bit:
        for r in list(grads):
            grads[r ^ bit] = across(grads[r], bit)
        bit //= 2
    scale = 1.0 / (length * n_seq)
    outs = [out((rows, 2 * STATE))] * planes
    args = token_parts + swapped + [grads[r] for r in range(n_dp)]
    scratch = (
        pltpu.VMEM((q, n_dp, SPAN, part), BF16),
        pltpu.VMEM((q, n_dp, SPAN, 2 * STATE), BF16),
        pltpu.VMEM((planes, rows, 2 * STATE), F32),
    )
    body = functools.partial(weight_body, n_dp, q, planes, rows, scale)
    pieces = call(body, outs, scratch, name="weight")(*args)
    grad_weight = pieces[0]
    for r in range(1, planes):
        pairs = [(z * q + i, (z + r) % planes * q + i) for z in range(planes) for i in range(q)]
        grad_weight = grad_weight + lax.ppermute(pieces[r], "seq", pairs)

    parts = [gx_parts[0, c] for c in range(PARTS)]
    for r in range(1, q):
        parts += [swap(gx_parts[r, c], r) for c in range(PARTS)]
    body = functools.partial(assemble_body, q, group, spans)
    (grad_x,) = call(body, [[out((length, q * group), BF16)]], name="assemble")(*parts)
    return grad_x[None], grad_weight


def solution(mesh):
    return jax.shard_map(
        on_device,
        mesh=mesh,
        in_specs=(
            P("dp", "seq", None),
            P(),
            P("dp", "seq", None),
            P("dp", None, "seq"),
            P("dp", None, "seq"),
            P(),
            P("dp", "seq", None),
        ),
        out_specs=(P("dp", "seq", None), P(("dp", "seq"), None)),
        check_vma=False,
    )
```
